128 devices in a mesh: ctx: 8 (over x_lo, y), img: 16 (over x_hi, z, core).
Axes of the slice: x: 4 (x_hi: 2, x_lo: 2; x = x_hi * 2 + x_lo), y: 4, z: 4, core: 2. Of those that a mesh axis runs over, the one named last changes fastest.
Arguments:
- patches: bfloat16 [8, 6144, 1280], P('ctx', 'img')
- window_ids: int32 [8, 6144], P('ctx', 'img'), may hold values from 0 to 49151, as said below
- counts: int32 [8], P('ctx'), may hold values from 3072 to 6144, as said below
- gain_one: bfloat16 [1280], replicated, may hold values from 0.099609375 to 1.8984375
- w_qkv1: bfloat16 [3, 1280, 1280], replicated
- w_out1: bfloat16 [1280, 1280], replicated, may hold values from -0.625 to 0.625
- gain_two: bfloat16 [1280], replicated, may hold values from 0.099609375 to 1.8984375
- w_qkv2: bfloat16 [3, 1280, 1280], P(None, None, 'img')
- w_out2: bfloat16 [1280, 1280], replicated, may hold values from -2.5 to 2.5
- gain_out: bfloat16 [1280], replicated, may hold values from 0.099609375 to 1.8984375
- slots: int32 [12288], P(('ctx', 'img')), may hold values from 0 to 12287, as said below
Outputs:
- context_rows: bfloat16 [12288, 5120], P(('ctx', 'img'))
The draws below stay inside these ranges and needn't reach their ends.
Inputs may be any that keep to these rules, and one draw needn't show every extreme that they name: `window_ids`: patches with equal ids form one window: consecutive patches inside one device's block of 384 patches of one image, at most 64 of them, and some window has exactly 64; different windows have different ids. Patches of image i at positions counts[i] and later are padding. Some image is full. slots holds every row number once. The merged rows of one device (aligned blocks of 96 entries) go to exactly 48 devices' blocks of context rows, 2 to each of them.
All inputs are finite; a program needn't handle non-finite values.
Results may differ from the reference program's by a relative error of at most 0.019.
Values may be sent and summed in bfloat16 or wider, within the bound.
No kernel may reach another device: no remote copies, remote signals or barrier semaphores. Data moves between devices by JAX's collectives and lax.ppermute only.
A program may use at most 192 MiB of HBM per device.

```python
import math
import jax
import jax.numpy as jnp
from jax import lax

HEADS = 16
HEAD_DIM = 80
PATCH_DEV = 384
WINDOW = 64
D = 1280
MW = 5120
IMAGES = 8
IMG_PATCHES = 6144
MERGED_DEV = 96
ROWS_ALL = 12288
CAP = 2


def projection_set(key):
    query_part = jax.random.normal(jax.random.fold_in(key, 1), (D, D), jnp.float32) * D ** (-0.5)
    own_part = jax.random.normal(jax.random.fold_in(key, 2), (D, D), jnp.float32) * D ** (-0.5)
    value_part = jax.random.normal(jax.random.fold_in(key, 3), (D, D), jnp.float32) * D ** (-0.5)
    key_part = own_part
    return jnp.stack([query_part, key_part, value_part]).astype(jnp.bfloat16)


def draw_w_qkv1(key, part):
    key = jax.random.fold_in(key, 21)
    return projection_set(key)


def draw_w_qkv2(key, part):
    key = jax.random.fold_in(key, 22)
    return projection_set(key)


def draw_patches(key, part):
    key = jax.random.fold_in(key, 5)
    values = jax.random.normal(key, (IMAGES, IMG_PATCHES, D), jnp.float32)
    return values.astype(jnp.bfloat16)


def draw_window_ids(key, part):
    key = jax.random.fold_in(key, 11)
    block_count = IMAGES * IMG_PATCHES // PATCH_DEV
    lengths = jax.random.randint(key, (block_count, PATCH_DEV), 1, WINDOW + 1, jnp.int32)
    lengths = lengths.at[:, 0].set(WINDOW)
    ends = jnp.cumsum(lengths, axis=1)
    positions = jnp.arange(PATCH_DEV, dtype=jnp.int32)
    window_index = jnp.sum((ends[:, None, :] <= positions[None, :, None]).astype(jnp.int32), axis=2)
    block_base = jnp.arange(block_count, dtype=jnp.int32)[:, None] * PATCH_DEV
    return (block_base + window_index).reshape(IMAGES, IMG_PATCHES)


def draw_counts(key, part):
    key = jax.random.fold_in(key, 13)
    values = jax.random.randint(jax.random.fold_in(key, 1), (IMAGES,), IMG_PATCHES // 2, IMG_PATCHES + 1, jnp.int32)
    chosen = jax.random.randint(jax.random.fold_in(key, 2), (), 0, IMAGES, jnp.int32)
    return values.at[chosen].set(IMG_PATCHES)


def draw_slots(key, part):
    key = jax.random.fold_in(key, 41)
    device_count = ROWS_ALL // MERGED_DEV
    piece_count = MERGED_DEV // CAP
    ordering = jax.random.permutation(jax.random.fold_in(key, 1), device_count)
    inverse = jnp.argsort(ordering)
    shifts = jax.random.permutation(jax.random.fold_in(key, 2), device_count)[:piece_count]
    target = inverse[(ordering[:, None] + shifts[None, :]) % device_count]
    source_perm = jax.vmap(lambda sub: jax.random.permutation(sub, MERGED_DEV))(jax.random.split(jax.random.fold_in(key, 3), device_count))
    target_perm = jax.vmap(lambda sub: jax.random.permutation(sub, MERGED_DEV))(jax.random.split(jax.random.fold_in(key, 4), device_count))
    within = jnp.arange(piece_count, dtype=jnp.int32)[:, None] * CAP + jnp.arange(CAP, dtype=jnp.int32)[None, :]
    values = target[:, :, None] * MERGED_DEV + target_perm[target[:, :, None], within[None, :, :]]
    senders = jnp.arange(device_count, dtype=jnp.int32)[:, None, None] * MERGED_DEV
    places = senders + source_perm[:, within]
    slots_out = jnp.zeros((ROWS_ALL,), jnp.int32)
    return slots_out.at[places.reshape(-1)].set(values.reshape(-1).astype(jnp.int32))


def centred(own_key, shape, width, most, kind=jnp.bfloat16):
    drawn = jax.random.normal(own_key, shape, jnp.float32) * width
    return jnp.minimum(jnp.maximum(drawn, -most), most).astype(kind)


def setup_inputs(seed: int = 0) -> dict:
    keys = jax.random.split(jax.random.key(seed), 12)
    return {
        "patches": draw_patches(jax.random.fold_in(keys[11], 71), 0),
        "window_ids": draw_window_ids(jax.random.fold_in(keys[11], 71), 0),
        "counts": draw_counts(jax.random.fold_in(keys[11], 71), 0),
        "gain_one": jnp.clip(1.0 + 0.18 * jax.random.normal(keys[3], (D,), jnp.float32), 0.099609375, 1.8984375).astype(jnp.bfloat16),
        "w_qkv1": draw_w_qkv1(jax.random.fold_in(keys[11], 71), 0),
        "w_out1": centred(keys[5], (D, D), (max(D // 16, 1)) ** -0.5, 0.625),
        "gain_two": jnp.clip(1.0 + 0.18 * jax.random.normal(keys[6], (D,), jnp.float32), 0.099609375, 1.8984375).astype(jnp.bfloat16),
        "w_qkv2": draw_w_qkv2(jax.random.fold_in(keys[11], 71), 0),
        "w_out2": centred(keys[8], (D, D), (max(D // 256, 1)) ** -0.5, 2.5),
        "gain_out": jnp.clip(1.0 + 0.18 * jax.random.normal(keys[9], (D,), jnp.float32), 0.099609375, 1.8984375).astype(jnp.bfloat16),
        "slots": draw_slots(jax.random.fold_in(keys[11], 71), 0),
    }


EPSILON = 1e-06
MASKED_SCORE = -1e+30

def normed(values, gain):
    values = values.astype(jnp.float32)
    return values * lax.rsqrt(lax.optimization_barrier(jnp.mean(values * values, axis=-1, keepdims=True)) + EPSILON) * gain.astype(jnp.float32)

def project(hidden, weights):
    return jnp.einsum('nd,tde->tne', hidden.astype(jnp.float32), weights.astype(jnp.float32)).astype(jnp.bfloat16)

def attention(queries, key_rows, value_rows, allowed_fn):
    total = queries.shape[0]
    block_rows = math.gcd(total, 512)
    block_count = total // block_rows
    query_blocks = queries.reshape(block_count, block_rows, HEADS, HEAD_DIM).astype(jnp.float32)
    key_heads = key_rows.reshape(total, HEADS, HEAD_DIM).astype(jnp.float32)
    value_heads = value_rows.reshape(total, HEADS, HEAD_DIM).astype(jnp.float32)
    offsets = jnp.arange(block_count, dtype=jnp.int32) * block_rows

    def one_block(inputs):
        query_block, offset = inputs
        allowed = allowed_fn(offset, block_rows)
        scores = jnp.einsum('qhd,khd->hqk', query_block, key_heads) * HEAD_DIM ** (-0.5)
        scores = jnp.where(allowed[None], scores, MASKED_SCORE)
        maxima = lax.optimization_barrier(jnp.max(scores, axis=-1, keepdims=True))
        weights = jnp.where(allowed[None], jnp.exp(scores - maxima), 0.0)
        totals = lax.optimization_barrier(jnp.sum(weights, axis=-1))
        rounded = lax.optimization_barrier(weights.astype(jnp.bfloat16)).astype(jnp.float32)
        summed = jnp.einsum('hqk,khd->qhd', rounded, value_heads)
        return (summed / totals.T[:, :, None]).astype(jnp.bfloat16)
    result = lax.map(one_block, (query_blocks, offsets))
    return result.reshape(total, HEADS * HEAD_DIM)

def encode(image, image_ids, key_count, gain_one, w_qkv1, w_out1, gain_two, w_qkv2, w_out2, gain_out):
    total = image.shape[0]
    first = image.astype(jnp.float32)
    hidden = normed(first, gain_one).astype(jnp.bfloat16)
    projected = project(hidden, w_qkv1)

    def same_window(offset, block_rows):
        query_ids = lax.dynamic_slice_in_dim(image_ids, offset, block_rows)
        return query_ids[:, None] == image_ids[None, :]
    attended = attention(projected[0], projected[1], projected[2], same_window)
    second = (first + jnp.dot(attended, w_out1, preferred_element_type=jnp.float32)).astype(jnp.bfloat16)
    hidden = normed(second, gain_two).astype(jnp.bfloat16)
    projected = project(hidden, w_qkv2)

    def valid_keys(offset, block_rows):
        valid = jnp.arange(total, dtype=jnp.int32) < key_count
        return jnp.broadcast_to(valid[None, :], (block_rows, total))
    attended = attention(projected[0], projected[1], projected[2], valid_keys)
    third = second.astype(jnp.float32) + jnp.dot(attended, w_out2, preferred_element_type=jnp.float32)
    return normed(third, gain_out).astype(jnp.bfloat16).reshape(total // 4, 4 * D)

def reference(patches, window_ids, counts, gain_one, w_qkv1, w_out1, gain_two, w_qkv2, w_out2, gain_out, slots):

    def one_image(inputs):
        image, image_ids, key_count = inputs
        return encode(image, image_ids, key_count, gain_one, w_qkv1, w_out1, gain_two, w_qkv2, w_out2, gain_out)
    merged = lax.map(one_image, (patches, window_ids, counts)).reshape(ROWS_ALL, MW)
    context_rows = jnp.zeros((ROWS_ALL, MW), jnp.bfloat16)
    return context_rows.at[slots.astype(jnp.int32)].set(merged)
```

```python
import functools
import math

import jax
import jax.numpy as jnp
from jax import lax
from jax.experimental import pallas as pl
from jax.experimental.pallas import tpu as pltpu
from jax.sharding import PartitionSpec as P

HEAD_DIM = 80
D = 1280
EPSILON = 1e-06
MASKED_SCORE = -1e30
F32 = jnp.float32
BF16 = jnp.bfloat16
Q_SCALE = HEAD_DIM ** (-0.5) * math.log2(math.e)
SAFE_BOUND = 64.0
SAFE_VALUE = 2.0**40
VMEM_LIMIT = 56 * 1024 * 1024
NT = (((1,), (1,)), ((), ()))
TN = (((0,), (0,)), ((), ()))


def normed(values, gain):
    values = values.astype(F32)
    return (
        values
        * lax.rsqrt(jnp.mean(values * values, axis=-1, keepdims=True) + EPSILON)
        * gain.astype(F32)
    )


def split_heads(row_block):
    return row_block.reshape(row_block.shape[0], -1, HEAD_DIM)


def attend_block(query_heads, key_heads, value_heads, allowed):
    scores = jnp.einsum(
        "qhd,khd->hqk", query_heads, key_heads, preferred_element_type=F32
    ) * HEAD_DIM ** (-0.5)
    scores = jnp.where(allowed[None], scores, MASKED_SCORE)
    maxima = jnp.max(scores, axis=-1)
    weights = jnp.where(allowed[None], jnp.exp(scores - maxima[:, :, None]), 0.0)
    totals = jnp.sum(weights, axis=-1)
    summed = jnp.einsum(
        "hqk,khd->qhd", weights.astype(BF16), value_heads, preferred_element_type=F32
    )
    return (maxima, totals, summed)


def finish(totals, summed):
    return (summed / totals.T[:, :, None]).astype(BF16).reshape(summed.shape[0], -1)


def whole(count):
    return [pl.BlockSpec(memory_space=pltpu.VMEM)] * count


def device_perm(move):
    pairs = []
    for i in range(128):
        c, g = divmod(i, 16)
        x_lo, y = divmod(c, 4)
        x_hi, r = divmod(g, 8)
        z, core = divmod(r, 2)
        x2, y2, z2, core2 = move(x_hi * 2 + x_lo, y, z, core)
        x2, y2, z2 = x2 % 4, y2 % 4, z2 % 4
        pairs.append((i, ((x2 % 2) * 4 + y2) * 16 + ((x2 // 2) * 4 + z2) * 2 + core2))
    return pairs


OTHER_X = {0: 3, 3: 0, 1: 2, 2: 1}
Z_UP = device_perm(lambda x, y, z, core: (x, y, z + 1, core))
Z_DOWN = device_perm(lambda x, y, z, core: (x, y, z - 1, core))
X_OTHER = device_perm(lambda x, y, z, core: (OTHER_X[x], y, z, core))
CORE_SWAP = device_perm(lambda x, y, z, core: (x, y, z, 1 - core))
BOTH = ("ctx", "img")
SHARD_OFFSETS = ((0, 0), (0, -1), (0, 1), (1, 0), (1, -1), (1, 1), (0, -2), (1, -2))


def gather_parity(shard):
    below = lax.ppermute(shard, BOTH, Z_UP)
    above = lax.ppermute(shard, BOTH, Z_DOWN)
    other = lax.ppermute(shard, BOTH, X_OTHER)
    other_below = lax.ppermute(other, BOTH, Z_UP)
    other_above = lax.ppermute(other, BOTH, Z_DOWN)
    far = lax.ppermute(below, BOTH, Z_UP)
    other_far = lax.ppermute(far, BOTH, X_OTHER)
    return [shard, below, above, other, other_below, other_above, far, other_far]


def project_kernel(order_ref, h_even_ref, h_odd_ref, *refs):
    out_ref = refs[8]
    rows = h_even_ref.shape[0]
    part = lax.broadcasted_iota(jnp.int32, (3 * HEAD_DIM, 1), 0)
    scale = jnp.where(part < HEAD_DIM, Q_SCALE, 1.0).astype(F32)
    for n in range(8):
        weights = refs[n][...]
        target = order_ref[n]
        for half, h_ref in enumerate((h_even_ref, h_odd_ref)):
            product = lax.dot_general(weights, h_ref[...], NT, preferred_element_type=F32)
            out_ref[target, :, half * rows : (half + 1) * rows] = (product * scale).astype(BF16)


def project(order, h_even, h_odd, shards):
    rows = h_even.shape[0]
    return pl.pallas_call(
        project_kernel,
        out_shape=jax.ShapeDtypeStruct((8, 3 * HEAD_DIM, 2 * rows), BF16),
        in_specs=[pl.BlockSpec(memory_space=pltpu.SMEM)] + whole(10),
        out_specs=pl.BlockSpec(memory_space=pltpu.VMEM),
        compiler_params=pltpu.CompilerParams(vmem_limit_bytes=VMEM_LIMIT),
    )(order, h_even, h_odd, *shards)


def attention_kernel(count_ref, q_ref, all_ref, out_ref, k_ref, v_ref, bound_ref, *, block):
    chips, features, rows = all_ref.shape
    total = chips * rows
    depth = HEAD_DIM

    @pl.when(pl.program_id(0) == 0)
    def _():
        count = count_ref[0]
        key_zero = all_ref[0, depth : 2 * depth, 0:1].astype(F32)
        q_most = jnp.zeros((1, rows), F32)
        k_most = jnp.zeros((1, rows), F32)
        v_most = jnp.zeros((HEAD_DIM, rows), F32)
        for chip in range(chips):
            position = chip * rows + lax.broadcasted_iota(jnp.int32, (1, rows), 1)
            valid = position < count
            keys = jnp.where(valid, all_ref[chip, depth : 2 * depth, :].astype(F32), key_zero)
            values = jnp.where(valid, all_ref[chip, 2 * depth :, :].astype(F32), 0.0)
            queries = all_ref[chip, 0:depth, :].astype(F32)
            q_most = jnp.maximum(q_most, jnp.sum(queries * queries, axis=0, keepdims=True))
            k_most = jnp.maximum(k_most, jnp.sum(keys * keys, axis=0, keepdims=True))
            v_most = jnp.maximum(v_most, jnp.abs(values))
            keys = jnp.concatenate([keys, jnp.zeros((128 - depth, rows), F32)], axis=0)
            k_ref[chip * rows : (chip + 1) * rows, :] = keys.astype(BF16).T
            v_ref[0:depth, chip * rows : (chip + 1) * rows] = values.astype(BF16)
            v_ref[depth:, chip * rows : (chip + 1) * rows] = jnp.where(
                (lax.broadcasted_iota(jnp.int32, (16, rows), 0) == 0) & valid, 1.0, 0.0
            ).astype(BF16)
        bound_ref[0] = jnp.max(q_most) * jnp.max(k_most)
        bound_ref[1] = jnp.max(v_most)

    queries = q_ref[0, 0:depth, :]
    queries = jnp.concatenate([queries, jnp.zeros((128 - depth, rows), BF16)], axis=0)
    small = (bound_ref[0] < SAFE_BOUND * SAFE_BOUND) & (bound_ref[1] < SAFE_VALUE)

    def store(acc):
        result = acc[0:depth] / acc[depth : depth + 1]
        half = rows // 2
        out_ref[0] = result[:, 0:half].astype(BF16)
        out_ref[1] = result[:, half:].astype(BF16)

    @pl.when(small)
    def _():
        acc = None
        for start in range(0, total, block):
            scores = jnp.dot(k_ref[start : start + block, :], queries, preferred_element_type=F32)
            weights = jnp.exp2(scores).astype(BF16)
            part = jnp.dot(v_ref[:, start : start + block], weights, preferred_element_type=F32)
            acc = part if acc is None else acc + part
        store(acc)

    @pl.when(jnp.logical_not(small))
    def _():
        def step(index, carried):
            most, acc = carried
            start = pl.multiple_of(index * block, block)
            scores = jnp.dot(
                k_ref[pl.ds(start, block), :], queries, preferred_element_type=F32
            )
            new_most = jnp.maximum(most, jnp.max(scores, axis=0, keepdims=True))
            weights = jnp.exp2(scores - new_most).astype(BF16)
            part = jnp.dot(
                v_ref[:, pl.ds(start, block)], weights, preferred_element_type=F32
            )
            return new_most, acc * jnp.exp2(most - new_most) + part

        start_state = (
            jnp.full((1, rows), MASKED_SCORE, F32),
            jnp.zeros((depth + 16, rows), F32),
        )
        store(lax.fori_loop(0, total // block, step, start_state)[1])


def attend_full(count, received):
    chips, features, rows = received.shape
    total = chips * rows
    return pl.pallas_call(
        functools.partial(attention_kernel, block=512),
        out_shape=jax.ShapeDtypeStruct((2 * chips, HEAD_DIM, rows // 2), BF16),
        grid=(chips,),
        in_specs=[
            pl.BlockSpec(memory_space=pltpu.SMEM),
            pl.BlockSpec((1, features, rows), lambda i: (i, 0, 0)),
            pl.BlockSpec(memory_space=pltpu.VMEM),
        ],
        out_specs=pl.BlockSpec((2, HEAD_DIM, rows // 2), lambda i: (i, 0, 0)),
        scratch_shapes=[
            pltpu.VMEM((total, 128), BF16),
            pltpu.VMEM((HEAD_DIM + 16, total), BF16),
            pltpu.SMEM((2,), F32),
        ],
        compiler_params=pltpu.CompilerParams(vmem_limit_bytes=VMEM_LIMIT),
    )(count, received, received)


def merge_kernel(bucket_ref, a_ref, x_ref, w_ref, gain_ref, out_ref):
    attended = a_ref[...]
    third = x_ref[...].astype(F32) + lax.dot_general(
        attended, w_ref[...], TN, preferred_element_type=F32
    )
    merged = normed(third, gain_ref[...]).astype(BF16)
    places, patches = out_ref.shape[0], merged.shape[0]
    chosen = lax.broadcasted_iota(jnp.int32, (places, patches), 0) == bucket_ref[...]
    out_ref[...] = jnp.dot(
        chosen.astype(BF16), merged, preferred_element_type=F32
    ).astype(BF16)


def merge(bucket, attended, second, w_out, gain, places):
    return pl.pallas_call(
        merge_kernel,
        out_shape=jax.ShapeDtypeStruct((places, D), BF16),
        in_specs=whole(5),
        out_specs=pl.BlockSpec(memory_space=pltpu.VMEM),
        compiler_params=pltpu.CompilerParams(vmem_limit_bytes=VMEM_LIMIT),
    )(bucket, attended, second, w_out, gain)


def place_kernel(target_ref, got_ref, out_ref):
    rows = out_ref.shape[0]
    got = got_ref[...]
    row = 4 * lax.broadcasted_iota(jnp.int32, (rows, got.shape[0]), 0)
    for j in range(4):
        chosen = (row + j) == target_ref[...]
        out_ref[:, j * D : (j + 1) * D] = jnp.dot(
            chosen.astype(BF16), got, preferred_element_type=F32
        ).astype(BF16)


def place(target, got, rows):
    return pl.pallas_call(
        place_kernel,
        out_shape=jax.ShapeDtypeStruct((rows, 4 * D), BF16),
        in_specs=whole(2),
        out_specs=pl.BlockSpec(memory_space=pltpu.VMEM),
        compiler_params=pltpu.CompilerParams(vmem_limit_bytes=VMEM_LIMIT),
    )(target, got)


def on_device(
    patches, window_ids, counts, gain_one, w_qkv1, w_out1, gain_two, w_qkv2, w_out2, gain_out, slots
):
    me = lax.axis_index("img")
    my_x, my_z, my_core = me // 8, (me // 2) % 4, me % 2
    shard = jnp.swapaxes(w_qkv2, 1, 2).reshape(3 * HEAD_DIM, D)
    shards = gather_parity(shard)
    order = jnp.stack([((my_x + dx) % 2) * 4 + (my_z + dz) % 4 for dx, dz in SHARD_OFFSETS])

    merged_rows = slots.shape[0]
    device_count = 128
    capacity = 2
    owner = slots // merged_rows
    local_slot = slots % merged_rows
    row_order = jnp.arange(merged_rows, dtype=jnp.int32)
    earlier = (owner[:, None] == owner[None, :]) & (row_order[None, :] < row_order[:, None])
    bucket = owner * capacity + jnp.sum(earlier.astype(jnp.int32), axis=1)
    quarter = jnp.arange(4, dtype=jnp.int32)
    bucket_rows = (4 * bucket[:, None] + quarter[None, :]).reshape(1, 4 * merged_rows)
    hits = bucket[:, None] == jnp.arange(device_count * capacity, dtype=jnp.int32)[None, :]
    send_slots = jnp.sum(jnp.where(hits, local_slot[:, None] + 1, 0), axis=0) - 1
    got_slots = lax.all_to_all(
        send_slots.reshape(device_count, capacity), BOTH, split_axis=0, concat_axis=0, tiled=True
    )
    target_rows = (4 * got_slots.reshape(-1)[:, None] + quarter[None, :]).reshape(1, -1)

    first = patches[0].astype(F32)
    hidden = normed(first, gain_one).astype(BF16)
    projected = jnp.einsum("pd,tde->tpe", hidden, w_qkv1, preferred_element_type=F32).astype(BF16)
    local_ids = window_ids[0]
    allowed = local_ids[:, None] == local_ids[None, :]
    maxima, totals, summed = attend_block(
        split_heads(projected[0]), split_heads(projected[1]), split_heads(projected[2]), allowed
    )
    attended = finish(totals, summed)
    second = (first + jnp.dot(attended, w_out1, preferred_element_type=F32)).astype(BF16)
    hidden = normed(second, gain_two).astype(BF16)

    partner = lax.ppermute(hidden, BOTH, CORE_SWAP)
    even = my_core == 0
    projected = project(
        order, jnp.where(even, hidden, partner), jnp.where(even, partner, hidden), shards
    )
    groups = [[2 * chip + core for chip in range(8)] for core in range(2)]
    received = lax.all_to_all(
        projected, "img", split_axis=0, concat_axis=0, tiled=True, axis_index_groups=groups
    )
    attended = attend_full(counts, received)
    attended = lax.all_to_all(attended, "img", split_axis=0, concat_axis=0, tiled=True)
    send = merge(
        bucket_rows,
        attended.reshape(D, -1),
        second,
        w_out2,
        gain_out.reshape(1, D),
        device_count * capacity * 4,
    )
    got = lax.all_to_all(
        send.reshape(device_count, capacity * 4, D), BOTH, split_axis=0, concat_axis=0, tiled=True
    )
    return place(target_rows, got.reshape(-1, D), merged_rows)


def solution(mesh):
    return jax.shard_map(
        on_device,
        mesh=mesh,
        in_specs=(
            P("ctx", "img", None),
            P("ctx", "img"),
            P("ctx"),
            P(),
            P(),
            P(),
            P(),
            P(None, None, "img"),
            P(),
            P(),
            P(("ctx", "img")),
        ),
        out_specs=P(("ctx", "img"), None),
        check_vma=False,
    )
```

```python
import functools
import math

import jax
import jax.numpy as jnp
from jax import lax
from jax.experimental import pallas as pl
from jax.experimental.pallas import tpu as pltpu
from jax.sharding import PartitionSpec as P

HEAD_DIM = 80
D = 1280
EPSILON = 1e-06
MASKED_SCORE = -1e30
F32 = jnp.float32
BF16 = jnp.bfloat16
Q_SCALE = HEAD_DIM ** (-0.5) * math.log2(math.e)
SAFE_BOUND = 64.0
SAFE_VALUE = 2.0**40
VMEM_LIMIT = 56 * 1024 * 1024
NT = (((1,), (1,)), ((), ()))
TN = (((0,), (0,)), ((), ()))


def normed(values, gain):
    values = values.astype(F32)
    return (
        values
        * lax.rsqrt(jnp.mean(values * values, axis=-1, keepdims=True) + EPSILON)
        * gain.astype(F32)
    )


def whole(count):
    return [pl.BlockSpec(memory_space=pltpu.VMEM)] * count


def layer_one_kernel(
    ids_row_ref, ids_column_ref, x_ref, gain_one_ref, gain_two_ref, w_qkv_ref, w_out_hbm,
    second_ref, hidden_ref, h_ref, q_ref, k_ref, a_ref, w_out_ref, sem,
):
    step = pl.program_id(0)
    copy = pltpu.make_async_copy(w_out_hbm, w_out_ref, sem)

    @pl.when(step == 0)
    def _():
        copy.start()
        h_ref[...] = normed(x_ref[0], gain_one_ref[...]).astype(BF16)

    def project_one():
        return jnp.dot(h_ref[...], w_qkv_ref[0], preferred_element_type=F32).astype(BF16)

    @pl.when(step == 0)
    def _():
        q_ref[...] = project_one()

    @pl.when(step == 1)
    def _():
        k_ref[...] = project_one()

    @pl.when(step == 2)
    def _():
        values_all = project_one()
        allowed = ids_column_ref[...] == ids_row_ref[...]
        rows = allowed.shape[0]
        tiles = {}
        for head in range(D // HEAD_DIM):
            begin, end = head * HEAD_DIM, (head + 1) * HEAD_DIM
            low, high = begin // 128 * 128, (end + 127) // 128 * 128
            lane = low + lax.broadcasted_iota(jnp.int32, (1, high - low), 1)
            mine = (lane >= begin) & (lane < end)
            keys = jnp.where(mine, k_ref[:, low:high], 0.0).astype(BF16)
            values = values_all[:, low:high]
            scores = lax.dot_general(
                q_ref[:, low:high], keys, NT, preferred_element_type=F32
            ) * HEAD_DIM ** (-0.5)
            scores = jnp.where(allowed, scores, MASKED_SCORE)
            most = jnp.max(scores, axis=1, keepdims=True)
            weights = jnp.exp(scores - most)
            total = jnp.sum(weights, axis=1, keepdims=True)
            result = jnp.dot(weights.astype(BF16), values, preferred_element_type=F32) / total
            for tile in range(low, high, 128):
                piece = result[:, tile - low : tile - low + 128]
                if tile in tiles:
                    piece = jnp.where(mine[:, tile - low : tile - low + 128], piece, tiles[tile])
                tiles[tile] = piece
                if tile + 128 <= end:
                    a_ref[:, tile : tile + 128] = tiles.pop(tile).astype(BF16)
        copy.wait()
        second = x_ref[0].astype(F32) + jnp.dot(
            a_ref[...], w_out_ref[...], preferred_element_type=F32
        )
        second = second.astype(BF16)
        second_ref[...] = second
        hidden_ref[...] = normed(second, gain_two_ref[...]).astype(BF16)


def layer_one(ids, patches, gain_one, gain_two, w_qkv, w_out):
    rows = patches.shape[1]
    fixed = lambda *shape: pl.BlockSpec(shape, lambda i: (0,) * len(shape))
    return pl.pallas_call(
        layer_one_kernel,
        out_shape=[jax.ShapeDtypeStruct((rows, D), BF16)] * 2,
        grid=(3,),
        in_specs=[
            fixed(1, rows),
            fixed(rows, 1),
            fixed(1, rows, D),
            fixed(1, D),
            fixed(1, D),
            pl.BlockSpec((1, D, D), lambda i: (i, 0, 0)),
            pl.BlockSpec(memory_space=pl.ANY),
        ],
        out_specs=[fixed(rows, D)] * 2,
        scratch_shapes=[pltpu.VMEM((rows, D), BF16)] * 4
        + [pltpu.VMEM((D, D), BF16), pltpu.SemaphoreType.DMA],
        compiler_params=pltpu.CompilerParams(vmem_limit_bytes=VMEM_LIMIT),
        cost_estimate=pl.CostEstimate(
            flops=6 * 10**9, bytes_accessed=16 * 10**6, transcendentals=3 * 10**6
        ),
    )(
        ids, ids.reshape(rows, 1), patches, gain_one.reshape(1, D), gain_two.reshape(1, D),
        w_qkv, w_out,
    )


def device_perm(move):
    pairs = []
    for i in range(128):
        c, g = divmod(i, 16)
        x_lo, y = divmod(c, 4)
        x_hi, r = divmod(g, 8)
        z, core = divmod(r, 2)
        x2, y2, z2, core2 = move(x_hi * 2 + x_lo, y, z, core)
        x2, y2, z2 = x2 % 4, y2 % 4, z2 % 4
        pairs.append((i, ((x2 % 2) * 4 + y2) * 16 + ((x2 // 2) * 4 + z2) * 2 + core2))
    return pairs


OTHER_X = {0: 3, 3: 0, 1: 2, 2: 1}
Z_UP = device_perm(lambda x, y, z, core: (x, y, z + 1, core))
Z_DOWN = device_perm(lambda x, y, z, core: (x, y, z - 1, core))
X_OTHER = device_perm(lambda x, y, z, core: (OTHER_X[x], y, z, core))
CORE_SWAP = device_perm(lambda x, y, z, core: (x, y, z, 1 - core))
BOTH = ("ctx", "img")
NEAR_OFFSETS = ((0, 0), (0, -1), (0, 1), (1, 0))
FAR_OFFSETS = ((1, -1), (1, 1), (0, 2), (1, 2))


def near_shards(shard):
    below = lax.ppermute(shard, BOTH, Z_UP)
    above = lax.ppermute(shard, BOTH, Z_DOWN)
    other = lax.ppermute(shard, BOTH, X_OTHER)
    return [shard, below, above, other]


def far_shards(near):
    shard, below, above, other = near
    half = 128
    far_top = lax.ppermute(below[:half], BOTH, Z_UP)
    far_bottom = lax.ppermute(above[half:], BOTH, Z_DOWN)
    other_below = lax.ppermute(other, BOTH, Z_UP)
    other_above = lax.ppermute(other, BOTH, Z_DOWN)
    other_far_top = lax.ppermute(far_top, BOTH, X_OTHER)
    other_far_bottom = lax.ppermute(far_bottom, BOTH, X_OTHER)
    return [other_below, other_above, far_top, far_bottom, other_far_top, other_far_bottom]


def project_kernel(order_ref, h_own_ref, h_partner_ref, *refs, parts, aliased):
    count = sum(parts)
    weights_refs = refs[:count]
    out_hbm, done_ref, sem = refs[count + aliased :]
    rows = h_own_ref.shape[0]
    part = lax.broadcasted_iota(jnp.int32, (3 * HEAD_DIM, 1), 0)
    scale = jnp.where(part < HEAD_DIM, Q_SCALE, 1.0).astype(F32)
    core = order_ref[len(parts)]
    copies = []
    first = 0
    for n, pieces in enumerate(parts):
        begin = 0
        for weights_ref in weights_refs[first : first + pieces]:
            end = begin + weights_ref.shape[0]
            for side, h_ref in ((core, h_own_ref), (1 - core, h_partner_ref)):
                product = lax.dot_general(
                    weights_ref[...], h_ref[...], NT, preferred_element_type=F32
                )
                at = pl.multiple_of(side * rows, 128)
                done_ref[n, begin:end, pl.ds(at, rows)] = (product * scale[begin:end]).astype(BF16)
            begin = end
        first += pieces
        copy = pltpu.make_async_copy(done_ref.at[n], out_hbm.at[order_ref[n]], sem.at[n])
        copy.start()
        copies.append(copy)
    for copy in copies:
        copy.wait()


def project(order, h_own, h_partner, shards, parts, into=None):
    rows = h_own.shape[0]
    aliased = 0 if into is None else 1
    return pl.pallas_call(
        functools.partial(project_kernel, parts=parts, aliased=aliased),
        out_shape=jax.ShapeDtypeStruct((8, 3 * HEAD_DIM, 2 * rows), BF16),
        in_specs=[pl.BlockSpec(memory_space=pltpu.SMEM)]
        + whole(2 + len(shards))
        + [pl.BlockSpec(memory_space=pl.ANY)] * aliased,
        out_specs=pl.BlockSpec(memory_space=pl.ANY),
        scratch_shapes=[
            pltpu.VMEM((len(parts), 3 * HEAD_DIM, 2 * rows), BF16),
            pltpu.SemaphoreType.DMA((len(parts),)),
        ],
        input_output_aliases={3 + len(shards): 0} if aliased else {},
        compiler_params=pltpu.CompilerParams(vmem_limit_bytes=VMEM_LIMIT),
        cost_estimate=pl.CostEstimate(
            flops=2 * 10**9, bytes_accessed=6 * 10**6, transcendentals=0
        ),
    )(order, h_own, h_partner, *shards, *([into] if aliased else []))


def attention_kernel(count_ref, q_ref, all_ref, out_ref, k_ref, v_ref, bound_ref, *, block):
    chips, features, rows = all_ref.shape
    total = chips * rows
    depth = HEAD_DIM

    @pl.when(pl.program_id(0) == 0)
    def _():
        count = count_ref[0]
        key_zero = all_ref[0, depth : 2 * depth, 0:1].astype(F32)
        q_most = jnp.zeros((1, rows), F32)
        k_most = jnp.zeros((1, rows), F32)
        v_most = jnp.zeros((HEAD_DIM, rows), F32)
        for chip in range(chips):
            position = chip * rows + lax.broadcasted_iota(jnp.int32, (1, rows), 1)
            valid = position < count
            keys = jnp.where(valid, all_ref[chip, depth : 2 * depth, :].astype(F32), key_zero)
            values = jnp.where(valid, all_ref[chip, 2 * depth :, :].astype(F32), 0.0)
            queries = all_ref[chip, 0:depth, :].astype(F32)
            q_most = jnp.maximum(q_most, jnp.sum(queries * queries, axis=0, keepdims=True))
            k_most = jnp.maximum(k_most, jnp.sum(keys * keys, axis=0, keepdims=True))
            v_most = jnp.maximum(v_most, jnp.abs(values))
            keys = jnp.concatenate([keys, jnp.zeros((128 - depth, rows), F32)], axis=0)
            k_ref[chip * rows : (chip + 1) * rows, :] = keys.astype(BF16).T
            v_ref[0:depth, chip * rows : (chip + 1) * rows] = values.astype(BF16)
            v_ref[depth:, chip * rows : (chip + 1) * rows] = jnp.where(
                (lax.broadcasted_iota(jnp.int32, (16, rows), 0) == 0) & valid, 1.0, 0.0
            ).astype(BF16)
        bound_ref[0] = jnp.max(q_most) * jnp.max(k_most)
        bound_ref[1] = jnp.max(v_most)

    queries = q_ref[0, 0:depth, :]
    queries = jnp.concatenate([queries, jnp.zeros((128 - depth, rows), BF16)], axis=0)
    small = (bound_ref[0] < SAFE_BOUND * SAFE_BOUND) & (bound_ref[1] < SAFE_VALUE)

    def store(acc):
        result = acc[0:depth] / acc[depth : depth + 1]
        half = rows // 2
        out_ref[0] = result[:, 0:half].astype(BF16)
        out_ref[1] = result[:, half:].astype(BF16)

    @pl.when(small)
    def _():
        acc = None
        for start in range(0, total, block):
            scores = jnp.dot(k_ref[start : start + block, :], queries, preferred_element_type=F32)
            weights = jnp.exp2(scores).astype(BF16)
            part = jnp.dot(v_ref[:, start : start + block], weights, preferred_element_type=F32)
            acc = part if acc is None else acc + part
        store(acc)

    @pl.when(jnp.logical_not(small))
    def _():
        def step(index, carried):
            most, acc = carried
            start = pl.multiple_of(index * block, block)
            scores = jnp.dot(
                k_ref[pl.ds(start, block), :], queries, preferred_element_type=F32
            )
            new_most = jnp.maximum(most, jnp.max(scores, axis=0, keepdims=True))
            weights = jnp.exp2(scores - new_most).astype(BF16)
            part = jnp.dot(
                v_ref[:, pl.ds(start, block)], weights, preferred_element_type=F32
            )
            return new_most, acc * jnp.exp2(most - new_most) + part

        start_state = (
            jnp.full((1, rows), MASKED_SCORE, F32),
            jnp.zeros((depth + 16, rows), F32),
        )
        store(lax.fori_loop(0, total // block, step, start_state)[1])


def attend_full(count, received):
    chips, features, rows = received.shape
    total = chips * rows
    return pl.pallas_call(
        functools.partial(attention_kernel, block=1024),
        out_shape=jax.ShapeDtypeStruct((2 * chips, HEAD_DIM, rows // 2), BF16),
        grid=(chips,),
        in_specs=[
            pl.BlockSpec(memory_space=pltpu.SMEM),
            pl.BlockSpec((1, features, rows), lambda i: (i, 0, 0)),
            pl.BlockSpec(memory_space=pltpu.VMEM),
        ],
        out_specs=pl.BlockSpec((2, HEAD_DIM, rows // 2), lambda i: (i, 0, 0)),
        scratch_shapes=[
            pltpu.VMEM((total, 128), BF16),
            pltpu.VMEM((HEAD_DIM + 16, total), BF16),
            pltpu.SMEM((2,), F32),
        ],
        compiler_params=pltpu.CompilerParams(vmem_limit_bytes=VMEM_LIMIT),
    )(count, received, received)


def merge_kernel(bucket_ref, a_ref, x_ref, w_ref, gain_ref, out_ref):
    attended = a_ref[...]
    third = x_ref[...].astype(F32) + lax.dot_general(
        attended, w_ref[...], TN, preferred_element_type=F32
    )
    merged = normed(third, gain_ref[...]).astype(BF16)
    places, patches = out_ref.shape[0], merged.shape[0]
    chosen = lax.broadcasted_iota(jnp.int32, (places, patches), 0) == bucket_ref[...]
    out_ref[...] = jnp.dot(
        chosen.astype(BF16), merged, preferred_element_type=F32
    ).astype(BF16)


def merge(bucket, attended, second, w_out, gain, places):
    return pl.pallas_call(
        merge_kernel,
        out_shape=jax.ShapeDtypeStruct((places, D), BF16),
        in_specs=whole(5),
        out_specs=pl.BlockSpec(memory_space=pltpu.VMEM),
        compiler_params=pltpu.CompilerParams(vmem_limit_bytes=VMEM_LIMIT),
    )(bucket, attended, second, w_out, gain)


def place_kernel(target_ref, got_ref, out_ref):
    rows = out_ref.shape[0]
    got = got_ref[...]
    row = 4 * lax.broadcasted_iota(jnp.int32, (rows, got.shape[0]), 0)
    for j in range(4):
        chosen = (row + j) == target_ref[...]
        out_ref[:, j * D : (j + 1) * D] = jnp.dot(
            chosen.astype(BF16), got, preferred_element_type=F32
        ).astype(BF16)


def place(target, got, rows):
    return pl.pallas_call(
        place_kernel,
        out_shape=jax.ShapeDtypeStruct((rows, 4 * D), BF16),
        in_specs=whole(2),
        out_specs=pl.BlockSpec(memory_space=pltpu.VMEM),
        compiler_params=pltpu.CompilerParams(vmem_limit_bytes=VMEM_LIMIT),
    )(target, got)


def on_device(
    patches, window_ids, counts, gain_one, w_qkv1, w_out1, gain_two, w_qkv2, w_out2, gain_out, slots
):
    me = lax.axis_index("img")
    my_x, my_z, my_core = me // 8, (me // 2) % 4, me % 2
    shard = jnp.swapaxes(w_qkv2, 1, 2).reshape(3 * HEAD_DIM, D)
    near = near_shards(shard)
    far = far_shards(near)

    def order_of(offsets):
        targets = [((my_x + dx) % 2) * 4 + (my_z + dz) % 4 for dx, dz in offsets]
        return jnp.stack(targets + [my_core])

    merged_rows = slots.shape[0]
    device_count = 128
    capacity = 2
    owner = slots // merged_rows
    local_slot = slots % merged_rows
    row_order = jnp.arange(merged_rows, dtype=jnp.int32)
    earlier = (owner[:, None] == owner[None, :]) & (row_order[None, :] < row_order[:, None])
    bucket = owner * capacity + jnp.sum(earlier.astype(jnp.int32), axis=1)
    quarter = jnp.arange(4, dtype=jnp.int32)
    bucket_rows = (4 * bucket[:, None] + quarter[None, :]).reshape(1, 4 * merged_rows)
    hits = bucket[:, None] == jnp.arange(device_count * capacity, dtype=jnp.int32)[None, :]
    send_slots = jnp.sum(jnp.where(hits, local_slot[:, None] + 1, 0), axis=0) - 1
    got_slots = lax.all_to_all(
        send_slots.reshape(device_count, capacity), BOTH, split_axis=0, concat_axis=0, tiled=True
    )
    target_rows = (4 * got_slots.reshape(-1)[:, None] + quarter[None, :]).reshape(1, -1)

    second, hidden = layer_one(window_ids, patches, gain_one, gain_two, w_qkv1, w_out1)

    partner = lax.ppermute(hidden, BOTH, CORE_SWAP)
    projected = project(order_of(NEAR_OFFSETS), hidden, partner, near, (1, 1, 1, 1))
    far, target_rows, bucket_rows = lax.optimization_barrier((far, target_rows, bucket_rows))
    projected = project(
        order_of(FAR_OFFSETS), hidden, partner, far, (1, 1, 2, 2), into=projected
    )
    groups = [[2 * chip + core for chip in range(8)] for core in range(2)]
    received = lax.all_to_all(
        projected, "img", split_axis=0, concat_axis=0, tiled=True, axis_index_groups=groups
    )
    attended = attend_full(counts, received)
    attended = lax.all_to_all(attended, "img", split_axis=0, concat_axis=0, tiled=True)
    send = merge(
        bucket_rows,
        attended.reshape(D, -1),
        second,
        w_out2,
        gain_out.reshape(1, D),
        device_count * capacity * 4,
    )
    got = lax.all_to_all(
        send.reshape(device_count, capacity * 4, D), BOTH, split_axis=0, concat_axis=0, tiled=True
    )
    return place(target_rows, got.reshape(-1, D), merged_rows)


def solution(mesh):
    return jax.shard_map(
        on_device,
        mesh=mesh,
        in_specs=(
            P("ctx", "img", None),
            P("ctx", "img"),
            P("ctx"),
            P(),
            P(),
            P(),
            P(),
            P(None, None, "img"),
            P(),
            P(),
            P(("ctx", "img")),
        ),
        out_specs=P(("ctx", "img"), None),
        check_vma=False,
    )
```

```python
import functools
import math

import jax
import jax.numpy as jnp
from jax import lax
from jax.experimental import pallas as pl
from jax.experimental.pallas import tpu as pltpu
from jax.sharding import PartitionSpec as P

HEAD_DIM = 80
D = 1280
EPSILON = 1e-06
MASKED_SCORE = -1e30
F32 = jnp.float32
BF16 = jnp.bfloat16
Q_SCALE = HEAD_DIM ** (-0.5) * math.log2(math.e)
SAFE_BOUND = 64.0
SAFE_VALUE = 2.0**40
VMEM_LIMIT = 56 * 1024 * 1024
NT = (((1,), (1,)), ((), ()))
TN = (((0,), (0,)), ((), ()))


def normed(values, gain):
    values = values.astype(F32)
    return (
        values
        * lax.rsqrt(jnp.mean(values * values, axis=-1, keepdims=True) + EPSILON)
        * gain.astype(F32).reshape(1, -1)
    )


def whole(count):
    return [pl.BlockSpec(memory_space=pltpu.VMEM)] * count


def layer_one_kernel(
    ids_ref, x_ref, gain_one_ref, gain_two_ref, w_qkv_ref, w_out_hbm,
    second_ref, hidden_ref, h_ref, q_ref, k_ref, a_ref, w_out_ref, sem,
):
    step = pl.program_id(0)
    copy = pltpu.make_async_copy(w_out_hbm, w_out_ref, sem)

    @pl.when(step == 0)
    def _():
        copy.start()
        h_ref[...] = normed(x_ref[0], gain_one_ref[...]).astype(BF16)

    def project_one():
        return jnp.dot(h_ref[...], w_qkv_ref[0], preferred_element_type=F32).astype(BF16)

    @pl.when(step == 0)
    def _():
        q_ref[...] = project_one()

    @pl.when(step == 1)
    def _():
        k_ref[...] = project_one()

    @pl.when(step == 2)
    def _():
        values_all = project_one()
        rows = ids_ref.shape[1]
        ids = jnp.broadcast_to(ids_ref[...], (8, rows))
        allowed = ids.T[:, 0:1] == ids[0:1]
        tiles = {}
        for head in range(D // HEAD_DIM):
            begin, end = head * HEAD_DIM, (head + 1) * HEAD_DIM
            low, high = begin // 128 * 128, (end + 127) // 128 * 128
            lane = low + lax.broadcasted_iota(jnp.int32, (1, high - low), 1)
            mine = (lane >= begin) & (lane < end)
            keys = jnp.where(mine, k_ref[:, low:high], 0.0).astype(BF16)
            values = values_all[:, low:high]
            scores = lax.dot_general(
                q_ref[:, low:high], keys, NT, preferred_element_type=F32
            ) * HEAD_DIM ** (-0.5)
            scores = jnp.where(allowed, scores, MASKED_SCORE)
            most = jnp.max(scores, axis=1, keepdims=True)
            weights = jnp.exp(scores - most)
            total = jnp.sum(weights, axis=1, keepdims=True)
            result = jnp.dot(weights.astype(BF16), values, preferred_element_type=F32) / total
            for tile in range(low, high, 128):
                piece = result[:, tile - low : tile - low + 128]
                if tile in tiles:
                    piece = jnp.where(mine[:, tile - low : tile - low + 128], piece, tiles[tile])
                tiles[tile] = piece
                if tile + 128 <= end:
                    a_ref[:, tile : tile + 128] = tiles.pop(tile).astype(BF16)
        copy.wait()
        second = x_ref[0].astype(F32) + jnp.dot(
            a_ref[...], w_out_ref[...], preferred_element_type=F32
        )
        second = second.astype(BF16)
        second_ref[...] = second
        hidden_ref[...] = normed(second, gain_two_ref[...]).astype(BF16)


def layer_one(ids, patches, gain_one, gain_two, w_qkv, w_out):
    rows = patches.shape[1]
    fixed = lambda *shape: pl.BlockSpec(shape, lambda i: (0,) * len(shape))
    return pl.pallas_call(
        layer_one_kernel,
        out_shape=[jax.ShapeDtypeStruct((rows, D), BF16)] * 2,
        grid=(3,),
        in_specs=[
            fixed(1, rows),
            fixed(1, rows, D),
            fixed(D),
            fixed(D),
            pl.BlockSpec((1, D, D), lambda i: (i, 0, 0)),
            pl.BlockSpec(memory_space=pl.ANY),
        ],
        out_specs=[fixed(rows, D)] * 2,
        scratch_shapes=[pltpu.VMEM((rows, D), BF16)] * 4
        + [pltpu.VMEM((D, D), BF16), pltpu.SemaphoreType.DMA],
        compiler_params=pltpu.CompilerParams(vmem_limit_bytes=VMEM_LIMIT),
        cost_estimate=pl.CostEstimate(
            flops=6 * 10**9, bytes_accessed=16 * 10**6, transcendentals=3 * 10**6
        ),
    )(
        ids, patches, gain_one, gain_two, w_qkv, w_out
    )


def device_perm(move):
    pairs = []
    for i in range(128):
        c, g = divmod(i, 16)
        x_lo, y = divmod(c, 4)
        x_hi, r = divmod(g, 8)
        z, core = divmod(r, 2)
        x2, y2, z2, core2 = move(x_hi * 2 + x_lo, y, z, core)
        x2, y2, z2 = x2 % 4, y2 % 4, z2 % 4
        pairs.append((i, ((x2 % 2) * 4 + y2) * 16 + ((x2 // 2) * 4 + z2) * 2 + core2))
    return pairs


OTHER_X = {0: 3, 3: 0, 1: 2, 2: 1}
Z_UP = device_perm(lambda x, y, z, core: (x, y, z + 1, core))
Z_DOWN = device_perm(lambda x, y, z, core: (x, y, z - 1, core))
X_OTHER = device_perm(lambda x, y, z, core: (OTHER_X[x], y, z, core))
CORE_SWAP = device_perm(lambda x, y, z, core: (x, y, z, 1 - core))
BOTH = ("ctx", "img")
NEAR_OFFSETS = ((0, 0), (0, -1), (0, 1), (1, 0))
FAR_OFFSETS = ((1, -1), (1, 1), (0, 2), (1, 2))


def near_shards(shard):
    below = lax.ppermute(shard, BOTH, Z_UP)
    above = lax.ppermute(shard, BOTH, Z_DOWN)
    other = lax.ppermute(shard, BOTH, X_OTHER)
    return [shard, below, above, other]


def far_shards(near):
    shard, below, above, other = near
    half = 128
    far_top = lax.ppermute(below[:half], BOTH, Z_UP)
    far_bottom = lax.ppermute(above[half:], BOTH, Z_DOWN)
    other_below = lax.ppermute(other, BOTH, Z_UP)
    other_above = lax.ppermute(other, BOTH, Z_DOWN)
    other_far_top = lax.ppermute(far_top, BOTH, X_OTHER)
    other_far_bottom = lax.ppermute(far_bottom, BOTH, X_OTHER)
    return [other_below, other_above, far_top, far_bottom, other_far_top, other_far_bottom]


def project_kernel(order_ref, h_own_ref, h_partner_ref, *refs, parts, aliased):
    count = sum(parts)
    weights_refs = refs[:count]
    out_hbm, w_ref, h_ref, done_ref, sem = refs[count + aliased :]
    rows = h_own_ref.shape[0]
    wide = 3 * HEAD_DIM
    core = order_ref[len(parts)]
    for side, ref in ((core, h_own_ref), (1 - core, h_partner_ref)):
        h_ref[pl.ds(pl.multiple_of(side * rows, 16), rows), :] = ref[...]
    at = 0
    for weights_ref in weights_refs:
        w_ref[at : at + weights_ref.shape[0], :] = weights_ref[...]
        at += weights_ref.shape[0]
    part = lax.broadcasted_iota(jnp.int32, (len(parts) * wide, 1), 0) % wide
    scale = jnp.where(part < HEAD_DIM, Q_SCALE, 1.0).astype(F32)
    product = lax.dot_general(w_ref[...], h_ref[...], NT, preferred_element_type=F32)
    product = (product * scale).astype(BF16)
    copies = []
    for n in range(len(parts)):
        done_ref[n] = product[n * wide : (n + 1) * wide]
        copy = pltpu.make_async_copy(done_ref.at[n], out_hbm.at[order_ref[n]], sem.at[n])
        copy.start()
        copies.append(copy)
    for copy in copies:
        copy.wait()


def project(order, h_own, h_partner, shards, parts, into=None):
    rows = h_own.shape[0]
    wide = 3 * HEAD_DIM
    aliased = 0 if into is None else 1
    return pl.pallas_call(
        functools.partial(project_kernel, parts=parts, aliased=aliased),
        out_shape=jax.ShapeDtypeStruct((8, wide, 2 * rows), BF16),
        in_specs=[pl.BlockSpec(memory_space=pltpu.SMEM)]
        + whole(2 + len(shards))
        + [pl.BlockSpec(memory_space=pl.ANY)] * aliased,
        out_specs=pl.BlockSpec(memory_space=pl.ANY),
        scratch_shapes=[
            pltpu.VMEM((len(parts) * wide, D), BF16),
            pltpu.VMEM((2 * rows, D), BF16),
            pltpu.VMEM((len(parts), wide, 2 * rows), BF16),
            pltpu.SemaphoreType.DMA((len(parts),)),
        ],
        input_output_aliases={3 + len(shards): 0} if aliased else {},
        compiler_params=pltpu.CompilerParams(vmem_limit_bytes=VMEM_LIMIT),
        cost_estimate=pl.CostEstimate(
            flops=2 * 10**9, bytes_accessed=6 * 10**6, transcendentals=0
        ),
    )(order, h_own, h_partner, *shards, *([into] if aliased else []))


def attention_kernel(count_ref, q_ref, all_ref, out_ref, k_ref, v_ref, bound_ref, *, block):
    chips, features, rows = all_ref.shape
    total = chips * rows
    depth = HEAD_DIM

    @pl.when(pl.program_id(0) == 0)
    def _():
        count = count_ref[0]
        key_zero = all_ref[0, depth : 2 * depth, 0:1].astype(F32)
        q_most = jnp.zeros((1, rows), F32)
        k_most = jnp.zeros((1, rows), F32)
        v_most = jnp.zeros((HEAD_DIM, rows), F32)
        for chip in range(chips):
            position = chip * rows + lax.broadcasted_iota(jnp.int32, (1, rows), 1)
            valid = position < count
            keys = jnp.where(valid, all_ref[chip, depth : 2 * depth, :].astype(F32), key_zero)
            values = jnp.where(valid, all_ref[chip, 2 * depth :, :].astype(F32), 0.0)
            queries = all_ref[chip, 0:depth, :].astype(F32)
            q_most = jnp.maximum(q_most, jnp.sum(queries * queries, axis=0, keepdims=True))
            k_most = jnp.maximum(k_most, jnp.sum(keys * keys, axis=0, keepdims=True))
            v_most = jnp.maximum(v_most, jnp.abs(values))
            keys = jnp.concatenate([keys, jnp.zeros((128 - depth, rows), F32)], axis=0)
            k_ref[chip * rows : (chip + 1) * rows, :] = keys.astype(BF16).T
            v_ref[0:depth, chip * rows : (chip + 1) * rows] = values.astype(BF16)
            v_ref[depth:, chip * rows : (chip + 1) * rows] = jnp.where(
                (lax.broadcasted_iota(jnp.int32, (16, rows), 0) == 0) & valid, 1.0, 0.0
            ).astype(BF16)
        bound_ref[0] = jnp.max(q_most) * jnp.max(k_most)
        bound_ref[1] = jnp.max(v_most)

    queries = q_ref[0, 0:depth, :]
    queries = jnp.concatenate([queries, jnp.zeros((128 - depth, rows), BF16)], axis=0)
    small = (bound_ref[0] < SAFE_BOUND * SAFE_BOUND) & (bound_ref[1] < SAFE_VALUE)

    def store(acc):
        result = acc[0:depth] / acc[depth : depth + 1]
        half = rows // 2
        out_ref[0] = result[:, 0:half].astype(BF16)
        out_ref[1] = result[:, half:].astype(BF16)

    @pl.when(small)
    def _():
        acc = None
        for start in range(0, total, block):
            scores = jnp.dot(k_ref[start : start + block, :], queries, preferred_element_type=F32)
            weights = jnp.exp2(scores).astype(BF16)
            part = jnp.dot(v_ref[:, start : start + block], weights, preferred_element_type=F32)
            acc = part if acc is None else acc + part
        store(acc)

    @pl.when(jnp.logical_not(small))
    def _():
        def step(index, carried):
            most, acc = carried
            start = pl.multiple_of(index * block, block)
            scores = jnp.dot(
                k_ref[pl.ds(start, block), :], queries, preferred_element_type=F32
            )
            new_most = jnp.maximum(most, jnp.max(scores, axis=0, keepdims=True))
            weights = jnp.exp2(scores - new_most).astype(BF16)
            part = jnp.dot(
                v_ref[:, pl.ds(start, block)], weights, preferred_element_type=F32
            )
            return new_most, acc * jnp.exp2(most - new_most) + part

        start_state = (
            jnp.full((1, rows), MASKED_SCORE, F32),
            jnp.zeros((depth + 16, rows), F32),
        )
        store(lax.fori_loop(0, total // block, step, start_state)[1])


def attend_full(count, received):
    chips, features, rows = received.shape
    total = chips * rows
    return pl.pallas_call(
        functools.partial(attention_kernel, block=1024),
        out_shape=jax.ShapeDtypeStruct((2 * chips, HEAD_DIM, rows // 2), BF16),
        grid=(chips,),
        in_specs=[
            pl.BlockSpec(memory_space=pltpu.SMEM),
            pl.BlockSpec((1, features, rows), lambda i: (i, 0, 0)),
            pl.BlockSpec(memory_space=pltpu.VMEM),
        ],
        out_specs=pl.BlockSpec((2, HEAD_DIM, rows // 2), lambda i: (i, 0, 0)),
        scratch_shapes=[
            pltpu.VMEM((total, 128), BF16),
            pltpu.VMEM((HEAD_DIM + 16, total), BF16),
            pltpu.SMEM((2,), F32),
        ],
        compiler_params=pltpu.CompilerParams(vmem_limit_bytes=VMEM_LIMIT),
    )(count, received, received)


def merge_kernel(bucket_ref, a_ref, x_ref, w_ref, gain_ref, out_ref):
    attended = a_ref[...]
    third = x_ref[...].astype(F32) + lax.dot_general(
        attended, w_ref[...], TN, preferred_element_type=F32
    )
    merged = normed(third, gain_ref[...]).astype(BF16)
    places, patches = out_ref.shape[0], merged.shape[0]
    chosen = lax.broadcasted_iota(jnp.int32, (places, patches), 0) == bucket_ref[...]
    out_ref[...] = jnp.dot(
        chosen.astype(BF16), merged, preferred_element_type=F32
    ).astype(BF16)


def merge(bucket, attended, second, w_out, gain, places):
    return pl.pallas_call(
        merge_kernel,
        out_shape=jax.ShapeDtypeStruct((places, D), BF16),
        in_specs=whole(5),
        out_specs=pl.BlockSpec(memory_space=pltpu.VMEM),
        compiler_params=pltpu.CompilerParams(vmem_limit_bytes=VMEM_LIMIT),
    )(bucket, attended, second, w_out, gain)


def place_kernel(target_ref, got_ref, out_ref):
    rows = out_ref.shape[0]
    wide = got_ref.shape[1]
    index = lax.broadcasted_iota(jnp.int32, (4 * rows, 1), 0)
    wanted = 4 * (index % rows) + index // rows
    chosen = (wanted == target_ref[...]).astype(BF16)
    found = jnp.dot(chosen, got_ref[...], preferred_element_type=F32).astype(BF16)
    for n in range(4):
        out_ref[:, n * wide : (n + 1) * wide] = found[n * rows : (n + 1) * rows]


def place(target, got, rows):
    return pl.pallas_call(
        place_kernel,
        out_shape=jax.ShapeDtypeStruct((rows, 4 * D), BF16),
        in_specs=whole(2),
        out_specs=pl.BlockSpec(memory_space=pltpu.VMEM),
        compiler_params=pltpu.CompilerParams(vmem_limit_bytes=VMEM_LIMIT),
    )(target, got)


def routes_kernel(me_ref, all_ref, own_ref, bucket_ref, target_ref):
    devices, rows = all_ref.shape
    places = target_ref.shape[1]
    me = me_ref[0]
    owner = jnp.broadcast_to(own_ref[...] // rows, (8, rows))
    sender = owner.T[:, 0:1]
    earlier = lax.broadcasted_iota(jnp.int32, (rows, rows), 0) < lax.broadcasted_iota(
        jnp.int32, (rows, rows), 1
    )
    rank = jnp.sum(((sender == owner[0:1]) & earlier).astype(jnp.int32), axis=0, keepdims=True)
    bucket = jnp.broadcast_to(4 * (2 * owner[0:1] + rank), (8, rows)).T[:, 0:1]
    lane = lax.broadcasted_iota(jnp.int32, (rows, 4 * rows), 1)
    mine = lane // 4 == lax.broadcasted_iota(jnp.int32, (rows, 4 * rows), 0)
    bucket_ref[...] = jnp.sum(jnp.where(mine, bucket + lane % 4, 0), axis=0, keepdims=True)
    hit = all_ref[...] // rows == me
    place = all_ref[...] - me * rows
    column = lax.broadcasted_iota(jnp.int32, (devices, rows), 1)
    first = jnp.min(jnp.where(hit, column, rows), axis=1, keepdims=True)
    slot_first = jnp.sum(jnp.where(hit & (column == first), place + 1, 0), axis=1, keepdims=True)
    slot_second = jnp.sum(jnp.where(hit & (column > first), place + 1, 0), axis=1, keepdims=True)
    lane = lax.broadcasted_iota(jnp.int32, (devices, places), 1)
    source = lax.broadcasted_iota(jnp.int32, (devices, places), 0)
    slot = jnp.where(lane // 4 % 2 == 0, slot_first, slot_second) - 1
    value = jnp.where(lane // 8 == source, 4 * slot + lane % 4, 0)
    target_ref[...] = jnp.sum(value, axis=0, keepdims=True)


def routes(me, every, own, places):
    rows = own.shape[1]
    return pl.pallas_call(
        routes_kernel,
        out_shape=[
            jax.ShapeDtypeStruct((1, 4 * rows), jnp.int32),
            jax.ShapeDtypeStruct((1, places), jnp.int32),
        ],
        in_specs=[pl.BlockSpec(memory_space=pltpu.SMEM)] + whole(2),
        out_specs=whole(2),
        compiler_params=pltpu.CompilerParams(vmem_limit_bytes=VMEM_LIMIT),
        cost_estimate=pl.CostEstimate(flops=10**6, bytes_accessed=10**6, transcendentals=0),
    )(me, every, own)


def on_device(
    patches, window_ids, counts, gain_one, w_qkv1, w_out1, gain_two, w_qkv2, w_out2, gain_out, slots
):
    me = lax.axis_index("img")
    my_x, my_z, my_core = me // 8, (me // 2) % 4, me % 2
    shard = jnp.swapaxes(w_qkv2, 1, 2).reshape(3 * HEAD_DIM, D)
    near = near_shards(shard)
    far = far_shards(near)

    def order_of(offsets):
        targets = [((my_x + dx) % 2) * 4 + (my_z + dz) % 4 for dx, dz in offsets]
        return jnp.stack(targets + [my_core])

    every_slots = lax.all_gather(slots.reshape(1, -1), BOTH, axis=0, tiled=True)

    second, hidden = layer_one(window_ids, patches, gain_one, gain_two, w_qkv1, w_out1)

    partner = lax.ppermute(hidden, BOTH, CORE_SWAP)
    projected = project(order_of(NEAR_OFFSETS), hidden, partner, near, (1, 1, 1, 1))
    projected = project(
        order_of(FAR_OFFSETS), hidden, partner, far, (1, 1, 2, 2), into=projected
    )
    groups = [[2 * chip + core for chip in range(8)] for core in range(2)]
    received = lax.all_to_all(
        projected, "img", split_axis=0, concat_axis=0, tiled=True, axis_index_groups=groups
    )
    every_slots, projected = lax.optimization_barrier((every_slots, projected))
    places = 128 * 2 * 4
    device = lax.axis_index("ctx") * 16 + me
    bucket_rows, target_rows = routes(
        device.reshape(1), every_slots, slots.reshape(1, -1), places
    )
    attended = attend_full(counts, received)
    attended = lax.all_to_all(attended, "img", split_axis=0, concat_axis=0, tiled=True)
    send = merge(bucket_rows, attended.reshape(D, -1), second, w_out2, gain_out, places)
    got = lax.all_to_all(
        send.reshape(128, 8, D), BOTH, split_axis=0, concat_axis=0, tiled=True
    )
    return place(target_rows, got.reshape(places, D), slots.shape[0])


def solution(mesh):
    return jax.shard_map(
        on_device,
        mesh=mesh,
        in_specs=(
            P("ctx", "img", None),
            P("ctx", "img"),
            P("ctx"),
            P(),
            P(),
            P(),
            P(),
            P(None, None, "img"),
            P(),
            P(),
            P(("ctx", "img")),
        ),
        out_specs=P(("ctx", "img"), None),
        check_vma=False,
    )
```

```python
import functools
import math

import jax
import jax.numpy as jnp
from jax import lax
from jax.experimental import pallas as pl
from jax.experimental.pallas import tpu as pltpu
from jax.sharding import PartitionSpec as P

HEAD_DIM = 80
D = 1280
EPSILON = 1e-06
MASKED_SCORE = -1e30
F32 = jnp.float32
BF16 = jnp.bfloat16
Q_SCALE = HEAD_DIM ** (-0.5) * math.log2(math.e)
TAG = 128
SAFE_BOUND = 64.0
SAFE_VALUE = 2.0**40
VMEM_LIMIT = 56 * 1024 * 1024
NT = (((1,), (1,)), ((), ()))
TN = (((0,), (0,)), ((), ()))


def normed(values, gain):
    values = values.astype(F32)
    return (
        values
        * lax.rsqrt(jnp.mean(values * values, axis=-1, keepdims=True) + EPSILON)
        * gain.astype(F32).reshape(1, -1)
    )


def whole(count):
    return [pl.BlockSpec(memory_space=pltpu.VMEM)] * count


def layer_one_kernel(
    ids_ref, x_ref, gain_one_ref, gain_two_ref, w_qkv_ref, w_out_hbm,
    second_ref, hidden_ref, h_ref, q_ref, k_ref, a_ref, w_out_ref, sem,
):
    step = pl.program_id(0)
    copy = pltpu.make_async_copy(w_out_hbm, w_out_ref, sem)

    @pl.when(step == 0)
    def _():
        copy.start()
        h_ref[...] = normed(x_ref[0], gain_one_ref[...]).astype(BF16)

    def project_one():
        return jnp.dot(h_ref[...], w_qkv_ref[0], preferred_element_type=F32).astype(BF16)

    @pl.when(step == 0)
    def _():
        q_ref[...] = project_one()

    @pl.when(step == 1)
    def _():
        k_ref[...] = project_one()

    @pl.when(step == 2)
    def _():
        values_all = project_one()
        rows = ids_ref.shape[1]
        ids = jnp.broadcast_to(ids_ref[...], (8, rows))
        allowed = ids.T[:, 0:1] == ids[0:1]
        tiles = {}
        for head in range(D // HEAD_DIM):
            begin, end = head * HEAD_DIM, (head + 1) * HEAD_DIM
            low, high = begin // 128 * 128, (end + 127) // 128 * 128
            lane = low + lax.broadcasted_iota(jnp.int32, (1, high - low), 1)
            mine = (lane >= begin) & (lane < end)
            keys = jnp.where(mine, k_ref[:, low:high], 0.0).astype(BF16)
            values = values_all[:, low:high]
            scores = lax.dot_general(
                q_ref[:, low:high], keys, NT, preferred_element_type=F32
            ) * HEAD_DIM ** (-0.5)
            scores = jnp.where(allowed, scores, MASKED_SCORE)
            most = jnp.max(scores, axis=1, keepdims=True)
            weights = jnp.exp(scores - most)
            total = jnp.sum(weights, axis=1, keepdims=True)
            result = jnp.dot(weights.astype(BF16), values, preferred_element_type=F32) / total
            for tile in range(low, high, 128):
                piece = result[:, tile - low : tile - low + 128]
                if tile in tiles:
                    piece = jnp.where(mine[:, tile - low : tile - low + 128], piece, tiles[tile])
                tiles[tile] = piece
                if tile + 128 <= end:
                    a_ref[:, tile : tile + 128] = tiles.pop(tile).astype(BF16)
        copy.wait()
        second = x_ref[0].astype(F32) + jnp.dot(
            a_ref[...], w_out_ref[...], preferred_element_type=F32
        )
        second = second.astype(BF16)
        second_ref[...] = second
        hidden_ref[...] = normed(second, gain_two_ref[...]).astype(BF16)


def layer_one(ids, patches, gain_one, gain_two, w_qkv, w_out):
    rows = patches.shape[1]
    fixed = lambda *shape: pl.BlockSpec(shape, lambda i: (0,) * len(shape))
    return pl.pallas_call(
        layer_one_kernel,
        out_shape=[jax.ShapeDtypeStruct((rows, D), BF16)] * 2,
        grid=(3,),
        in_specs=[
            fixed(1, rows),
            fixed(1, rows, D),
            fixed(D),
            fixed(D),
            pl.BlockSpec((1, D, D), lambda i: (i, 0, 0)),
            pl.BlockSpec(memory_space=pl.ANY),
        ],
        out_specs=[fixed(rows, D)] * 2,
        scratch_shapes=[pltpu.VMEM((rows, D), BF16)] * 4
        + [pltpu.VMEM((D, D), BF16), pltpu.SemaphoreType.DMA],
        compiler_params=pltpu.CompilerParams(vmem_limit_bytes=VMEM_LIMIT),
        cost_estimate=pl.CostEstimate(
            flops=6 * 10**9, bytes_accessed=16 * 10**6, transcendentals=3 * 10**6
        ),
    )(
        ids, patches, gain_one, gain_two, w_qkv, w_out
    )


def device_perm(move):
    pairs = []
    for i in range(128):
        c, g = divmod(i, 16)
        x_lo, y = divmod(c, 4)
        x_hi, r = divmod(g, 8)
        z, core = divmod(r, 2)
        x2, y2, z2, core2 = move(x_hi * 2 + x_lo, y, z, core)
        x2, y2, z2 = x2 % 4, y2 % 4, z2 % 4
        pairs.append((i, ((x2 % 2) * 4 + y2) * 16 + ((x2 // 2) * 4 + z2) * 2 + core2))
    return pairs


OTHER_X = {0: 3, 3: 0, 1: 2, 2: 1}
Z_UP = device_perm(lambda x, y, z, core: (x, y, z + 1, core))
Z_DOWN = device_perm(lambda x, y, z, core: (x, y, z - 1, core))
X_OTHER = device_perm(lambda x, y, z, core: (OTHER_X[x], y, z, core))
CORE_SWAP = device_perm(lambda x, y, z, core: (x, y, z, 1 - core))
BOTH = ("ctx", "img")
NEAR_OFFSETS = ((0, 0), (0, -1), (0, 1), (1, 0))
FAR_OFFSETS = ((1, -1), (1, 1), (0, 2), (1, 2))


def near_shards(shard):
    below = lax.ppermute(shard, BOTH, Z_UP)
    above = lax.ppermute(shard, BOTH, Z_DOWN)
    other = lax.ppermute(shard, BOTH, X_OTHER)
    return [shard, below, above, other]


def far_shards(near):
    shard, below, above, other = near
    half = 128
    far_top = lax.ppermute(below[:half], BOTH, Z_UP)
    far_bottom = lax.ppermute(above[half:], BOTH, Z_DOWN)
    far_top, far_bottom, other = lax.optimization_barrier((far_top, far_bottom, other))
    other_far_top = lax.ppermute(far_top, BOTH, X_OTHER)
    other_far_bottom = lax.ppermute(far_bottom, BOTH, X_OTHER)
    other_below = lax.ppermute(other, BOTH, Z_UP)
    other_above = lax.ppermute(other, BOTH, Z_DOWN)
    return [other_below, other_above, far_top, far_bottom, other_far_top, other_far_bottom]


def project_kernel(h_own_ref, h_partner_ref, *refs, parts, offsets, aliased):
    count = sum(parts)
    me = lax.axis_index("img")
    my_x, my_z, core = me // 8, me // 2 % 4, me % 2
    weights_refs = refs[:count]
    out_hbm, w_ref, h_ref, done_ref, sem = refs[count + aliased :]
    rows = h_own_ref.shape[0]
    wide = 3 * HEAD_DIM
    for side, ref in ((core, h_own_ref), (1 - core, h_partner_ref)):
        h_ref[pl.ds(pl.multiple_of(side * rows, 16), rows), :] = ref[...]
    at = 0
    for weights_ref in weights_refs:
        w_ref[at : at + weights_ref.shape[0], :] = weights_ref[...]
        at += weights_ref.shape[0]
    part = lax.broadcasted_iota(jnp.int32, (len(parts) * wide, 1), 0) % wide
    scale = jnp.where(part < HEAD_DIM, Q_SCALE, 1.0).astype(F32)
    product = lax.dot_general(w_ref[...], h_ref[...], NT, preferred_element_type=F32)
    product = (product * scale).astype(BF16)
    copies = []
    for n in range(len(parts)):
        done_ref[n] = product[n * wide : (n + 1) * wide]
        target = (my_x + offsets[n][0]) % 2 * 4 + (my_z + offsets[n][1] + 4) % 4
        copy = pltpu.make_async_copy(done_ref.at[n], out_hbm.at[target], sem.at[n])
        copy.start()
        copies.append(copy)
    for copy in copies:
        copy.wait()


def project(offsets, h_own, h_partner, shards, parts, into=None):
    rows = h_own.shape[0]
    wide = 3 * HEAD_DIM
    aliased = 0 if into is None else 1
    return pl.pallas_call(
        functools.partial(
            project_kernel, parts=parts, offsets=offsets, aliased=aliased
        ),
        out_shape=jax.ShapeDtypeStruct((8, wide, 2 * rows), BF16),
        in_specs=whole(2 + len(shards))
        + [pl.BlockSpec(memory_space=pl.ANY)] * aliased,
        out_specs=pl.BlockSpec(memory_space=pl.ANY),
        scratch_shapes=[
            pltpu.VMEM((len(parts) * wide, D), BF16),
            pltpu.VMEM((2 * rows, D), BF16),
            pltpu.VMEM((len(parts), wide, 2 * rows), BF16),
            pltpu.SemaphoreType.DMA((len(parts),)),
        ],
        input_output_aliases={2 + len(shards): 0} if aliased else {},
        compiler_params=pltpu.CompilerParams(vmem_limit_bytes=VMEM_LIMIT),
        cost_estimate=pl.CostEstimate(
            flops=2 * 10**9, bytes_accessed=6 * 10**6, transcendentals=0
        ),
    )(h_own, h_partner, *shards, *([into] if aliased else []))


def attention_kernel(count_ref, q_ref, all_ref, out_ref, k_ref, v_ref, bound_ref, *, block):
    chips, features, rows = all_ref.shape
    total = chips * rows
    depth = HEAD_DIM

    @pl.when(pl.program_id(0) == 0)
    def _():
        count = count_ref[0]
        key_zero = all_ref[0, depth : 2 * depth, 0:1].astype(F32)
        q_most = jnp.zeros((1, rows), F32)
        k_most = jnp.zeros((1, rows), F32)
        v_most = jnp.zeros((HEAD_DIM, rows), F32)
        for chip in range(chips):
            position = chip * rows + lax.broadcasted_iota(jnp.int32, (1, rows), 1)
            valid = position < count
            keys = jnp.where(valid, all_ref[chip, depth : 2 * depth, :].astype(F32), key_zero)
            values = jnp.where(valid, all_ref[chip, 2 * depth :, :].astype(F32), 0.0)
            queries = all_ref[chip, 0:depth, :].astype(F32)
            q_most = jnp.maximum(q_most, jnp.sum(queries * queries, axis=0, keepdims=True))
            k_most = jnp.maximum(k_most, jnp.sum(keys * keys, axis=0, keepdims=True))
            v_most = jnp.maximum(v_most, jnp.abs(values))
            keys = jnp.concatenate([keys, jnp.zeros((128 - depth, rows), F32)], axis=0)
            k_ref[chip * rows : (chip + 1) * rows, :] = keys.astype(BF16).T
            v_ref[0:depth, chip * rows : (chip + 1) * rows] = values.astype(BF16)
            v_ref[depth:, chip * rows : (chip + 1) * rows] = jnp.where(
                (lax.broadcasted_iota(jnp.int32, (16, rows), 0) == 0) & valid, 1.0, 0.0
            ).astype(BF16)
        bound_ref[0] = jnp.max(q_most) * jnp.max(k_most)
        bound_ref[1] = jnp.max(v_most)

    taken = q_ref.shape[0]
    queries = jnp.concatenate([q_ref[n, 0:depth, :] for n in range(taken)], axis=1)
    queries = jnp.concatenate([queries, jnp.zeros((128 - depth, taken * rows), BF16)], axis=0)
    small = (bound_ref[0] < SAFE_BOUND * SAFE_BOUND) & (bound_ref[1] < SAFE_VALUE)

    def store(acc):
        result = acc[0:depth] / acc[depth : depth + 1]
        half = rows // 2
        for n in range(2 * taken):
            out_ref[n] = result[:, n * half : (n + 1) * half].astype(BF16)

    @pl.when(small)
    def _():
        acc = None
        for start in range(0, total, block):
            scores = jnp.dot(k_ref[start : start + block, :], queries, preferred_element_type=F32)
            weights = jnp.exp2(scores).astype(BF16)
            part = jnp.dot(v_ref[:, start : start + block], weights, preferred_element_type=F32)
            acc = part if acc is None else acc + part
        store(acc)

    @pl.when(jnp.logical_not(small))
    def _():
        def step(index, carried):
            most, acc = carried
            start = pl.multiple_of(index * block, block)
            scores = jnp.dot(
                k_ref[pl.ds(start, block), :], queries, preferred_element_type=F32
            )
            new_most = jnp.maximum(most, jnp.max(scores, axis=0, keepdims=True))
            weights = jnp.exp2(scores - new_most).astype(BF16)
            part = jnp.dot(
                v_ref[:, pl.ds(start, block)], weights, preferred_element_type=F32
            )
            return new_most, acc * jnp.exp2(most - new_most) + part

        start_state = (
            jnp.full((1, taken * rows), MASKED_SCORE, F32),
            jnp.zeros((depth + 16, taken * rows), F32),
        )
        store(lax.fori_loop(0, total // block, step, start_state)[1])


def attend_full(count, received):
    chips, features, rows = received.shape
    total = chips * rows
    taken = 2
    return pl.pallas_call(
        functools.partial(attention_kernel, block=512),
        out_shape=jax.ShapeDtypeStruct((2 * chips, HEAD_DIM, rows // 2), BF16),
        grid=(chips // taken,),
        in_specs=[
            pl.BlockSpec(memory_space=pltpu.SMEM),
            pl.BlockSpec((taken, features, rows), lambda i: (i, 0, 0)),
            pl.BlockSpec(memory_space=pltpu.VMEM),
        ],
        out_specs=pl.BlockSpec((2 * taken, HEAD_DIM, rows // 2), lambda i: (i, 0, 0)),
        scratch_shapes=[
            pltpu.VMEM((total, 128), BF16),
            pltpu.VMEM((HEAD_DIM + 16, total), BF16),
            pltpu.SMEM((2,), F32),
        ],
        compiler_params=pltpu.CompilerParams(vmem_limit_bytes=VMEM_LIMIT),
    )(count, received, received)


def merge_kernel(bucket_ref, tag_ref, a_ref, x_ref, w_ref, gain_ref, out_ref):
    attended = a_ref[...]
    third = x_ref[...].astype(F32) + lax.dot_general(
        attended, w_ref[...], TN, preferred_element_type=F32
    )
    merged = normed(third, gain_ref[...]).astype(BF16)
    merged = jnp.concatenate([merged, tag_ref[...]], axis=1)
    places, patches = out_ref.shape[0], merged.shape[0]
    chosen = lax.broadcasted_iota(jnp.int32, (places, patches), 0) == bucket_ref[...]
    out_ref[...] = jnp.dot(
        chosen.astype(BF16), merged, preferred_element_type=F32
    ).astype(BF16)


def merge(bucket, tag, attended, second, w_out, gain, places):
    return pl.pallas_call(
        merge_kernel,
        out_shape=jax.ShapeDtypeStruct((places, D + TAG), BF16),
        in_specs=whole(6),
        out_specs=pl.BlockSpec(memory_space=pltpu.VMEM),
        compiler_params=pltpu.CompilerParams(vmem_limit_bytes=VMEM_LIMIT),
    )(bucket, tag, attended, second, w_out, gain)


def place_kernel(got_ref, out_ref):
    rows = out_ref.shape[0]
    places = got_ref.shape[0]
    tag = got_ref[:, D:].astype(F32).T[0:1].astype(jnp.int32)
    target = 4 * tag + lax.broadcasted_iota(jnp.int32, (1, places), 1) % 4
    index = lax.broadcasted_iota(jnp.int32, (4 * rows, 1), 0)
    wanted = 4 * (index % rows + 1) + index // rows
    chosen = (wanted == target).astype(BF16)
    found = jnp.dot(chosen, got_ref[:, :D], preferred_element_type=F32).astype(BF16)
    for n in range(4):
        out_ref[:, n * D : (n + 1) * D] = found[n * rows : (n + 1) * rows]


def place(got, rows):
    return pl.pallas_call(
        place_kernel,
        out_shape=jax.ShapeDtypeStruct((rows, 4 * D), BF16),
        in_specs=whole(1),
        out_specs=pl.BlockSpec(memory_space=pltpu.VMEM),
        compiler_params=pltpu.CompilerParams(vmem_limit_bytes=VMEM_LIMIT),
    )(got)


def routes_kernel(slots_ref, bucket_ref, tag_ref):
    rows = slots_ref.shape[1]
    slots = jnp.broadcast_to(slots_ref[...], (8, rows))
    owner = slots // rows
    sender = owner.T[:, 0:1]
    earlier = lax.broadcasted_iota(jnp.int32, (rows, rows), 0) < lax.broadcasted_iota(
        jnp.int32, (rows, rows), 1
    )
    rank = jnp.sum(((sender == owner[0:1]) & earlier).astype(jnp.int32), axis=0, keepdims=True)
    bucket = jnp.broadcast_to(4 * (2 * owner[0:1] + rank), (8, rows)).T[:, 0:1]
    lane = lax.broadcasted_iota(jnp.int32, (rows, 4 * rows), 1)
    mine = lane // 4 == lax.broadcasted_iota(jnp.int32, (rows, 4 * rows), 0)
    bucket_ref[...] = jnp.sum(jnp.where(mine, bucket + lane % 4, 0), axis=0, keepdims=True)
    place = (slots - owner * rows + 1).T[:, 0:1].astype(F32)
    patch = lax.broadcasted_iota(jnp.int32, (4 * rows, rows), 0) // 4
    spread = (patch == lax.broadcasted_iota(jnp.int32, (4 * rows, rows), 1)).astype(BF16)
    tag_ref[...] = jnp.dot(
        spread,
        jnp.broadcast_to(place, (rows, TAG)).astype(BF16),
        preferred_element_type=F32,
    ).astype(BF16)


def routes(slots):
    rows = slots.shape[0]
    return pl.pallas_call(
        routes_kernel,
        out_shape=[
            jax.ShapeDtypeStruct((1, 4 * rows), jnp.int32),
            jax.ShapeDtypeStruct((4 * rows, TAG), BF16),
        ],
        in_specs=whole(1),
        out_specs=whole(2),
        compiler_params=pltpu.CompilerParams(vmem_limit_bytes=VMEM_LIMIT),
        cost_estimate=pl.CostEstimate(flops=10**6, bytes_accessed=10**6, transcendentals=0),
    )(slots.reshape(1, rows))


def on_device(
    patches, window_ids, counts, gain_one, w_qkv1, w_out1, gain_two, w_qkv2, w_out2, gain_out, slots
):
    shard = jnp.swapaxes(w_qkv2, 1, 2).reshape(3 * HEAD_DIM, D)
    near = near_shards(shard)
    far = far_shards(near)

    second, hidden = layer_one(window_ids, patches, gain_one, gain_two, w_qkv1, w_out1)

    partner = lax.ppermute(hidden, BOTH, CORE_SWAP)
    projected = project(NEAR_OFFSETS, hidden, partner, near, (1, 1, 1, 1))
    projected = project(
        FAR_OFFSETS, hidden, partner, far, (1, 1, 2, 2), into=projected
    )
    groups = [[2 * chip + core for chip in range(8)] for core in range(2)]
    received = lax.all_to_all(
        projected, "img", split_axis=0, concat_axis=0, tiled=True, axis_index_groups=groups
    )
    slots, projected = lax.optimization_barrier((slots, projected))
    bucket_rows, tag = routes(slots)
    attended = attend_full(counts, received)
    attended = lax.all_to_all(attended, "img", split_axis=0, concat_axis=0, tiled=True)
    places = 128 * 2 * 4
    send = merge(bucket_rows, tag, attended.reshape(D, -1), second, w_out2, gain_out, places)
    got = lax.all_to_all(
        send.reshape(128, 8, D + TAG), BOTH, split_axis=0, concat_axis=0, tiled=True
    )
    return place(got.reshape(places, D + TAG), slots.shape[0])


def solution(mesh):
    return jax.shard_map(
        on_device,
        mesh=mesh,
        in_specs=(
            P("ctx", "img", None),
            P("ctx", "img"),
            P("ctx"),
            P(),
            P(),
            P(),
            P(),
            P(None, None, "img"),
            P(),
            P(),
            P(("ctx", "img")),
        ),
        out_specs=P(("ctx", "img"), None),
        check_vma=False,
    )
```

```python
import functools
import math

import jax
import jax.numpy as jnp
from jax import lax
from jax.experimental import pallas as pl
from jax.experimental.pallas import tpu as pltpu
from jax.sharding import PartitionSpec as P

HEAD_DIM = 80
D = 1280
EPSILON = 1e-06
MASKED_SCORE = -1e30
F32 = jnp.float32
BF16 = jnp.bfloat16
Q_SCALE = HEAD_DIM ** (-0.5) * math.log2(math.e)
WINDOW = 64
QUERY_BLOCK = 384
TAG = 128
SAFE_BOUND = 64.0
SAFE_VALUE = 2.0**40
VMEM_LIMIT = 56 * 1024 * 1024
NT = (((1,), (1,)), ((), ()))
TN = (((0,), (0,)), ((), ()))


def normed(values, gain):
    values = values.astype(F32)
    return (
        values
        * lax.rsqrt(jnp.mean(values * values, axis=-1, keepdims=True) + EPSILON)
        * gain.astype(F32).reshape(1, -1)
    )


def whole(count):
    return [pl.BlockSpec(memory_space=pltpu.VMEM)] * count


def layer_one_kernel(
    ids_ref, x_ref, gain_one_ref, gain_two_ref, w_qkv_ref, w_out_hbm,
    second_ref, hidden_ref, h_ref, q_ref, k_ref, a_ref, w_out_ref, sem,
):
    step = pl.program_id(0)
    copy = pltpu.make_async_copy(w_out_hbm, w_out_ref, sem)

    @pl.when(step == 0)
    def _():
        h_ref[...] = normed(x_ref[0], gain_one_ref[...]).astype(BF16)

    def project_one(scale=None):
        product = jnp.dot(h_ref[...], w_qkv_ref[0], preferred_element_type=F32)
        return (product if scale is None else product * scale).astype(BF16)

    @pl.when(step == 0)
    def _():
        q_ref[...] = project_one(Q_SCALE)

    @pl.when(step == 1)
    def _():
        copy.start()
        k_ref[...] = project_one()

    @pl.when(step == 2)
    def _():
        values_all = project_one()
        rows = ids_ref.shape[1]
        ids = jnp.broadcast_to(ids_ref[...], (8, rows))
        ids_column = ids.T[:, 0:1]
        spans = []
        for start in range(0, rows, QUERY_BLOCK):
            begin = max(start - WINDOW, 0)
            end = min(start + QUERY_BLOCK + WINDOW, rows)
            allowed = ids_column[start : start + QUERY_BLOCK] == ids[0:1, begin:end]
            spans.append((start, begin, end, allowed))
        tiles = {}
        allowed = spans[0][3]

        def window(head):
            first, last = head * HEAD_DIM, (head + 1) * HEAD_DIM
            low, high = first // 128 * 128, (last + 127) // 128 * 128
            lane = low + lax.broadcasted_iota(jnp.int32, (1, high - low), 1)
            return low, high, last, (lane >= first) & (lane < last)

        def score(head):
            low, high, last, mine = window(head)
            keys = jnp.where(mine, k_ref[:, low:high], 0.0).astype(BF16)
            return lax.dot_general(q_ref[:, low:high], keys, NT, preferred_element_type=F32)

        heads = D // HEAD_DIM
        ahead = score(0)
        for head in range(heads):
            scores = jnp.where(allowed, ahead, MASKED_SCORE)
            if head + 1 < heads:
                ahead = score(head + 1)
            low, high, last, mine = window(head)
            most = jnp.max(scores, axis=1, keepdims=True)
            weights = jnp.exp2(scores - most)
            total = jnp.sum(weights, axis=1, keepdims=True)
            result = jnp.dot(
                weights.astype(BF16), values_all[:, low:high], preferred_element_type=F32
            ) * (1.0 / total)
            for tile in range(low, high, 128):
                piece = result[:, tile - low : tile - low + 128]
                if tile in tiles:
                    piece = jnp.where(mine[:, tile - low : tile - low + 128], piece, tiles[tile])
                tiles[tile] = piece
                if tile + 128 <= last:
                    a_ref[:, tile : tile + 128] = tiles.pop(tile).astype(BF16)
        copy.wait()
        second = x_ref[0].astype(F32) + jnp.dot(
            a_ref[...], w_out_ref[...], preferred_element_type=F32
        )
        second = second.astype(BF16)
        second_ref[...] = second
        hidden_ref[...] = normed(second, gain_two_ref[...]).astype(BF16)


def layer_one(ids, patches, gain_one, gain_two, w_qkv, w_out):
    rows = patches.shape[1]
    fixed = lambda *shape: pl.BlockSpec(shape, lambda i: (0,) * len(shape))
    return pl.pallas_call(
        layer_one_kernel,
        out_shape=[jax.ShapeDtypeStruct((rows, D), BF16)] * 2,
        grid=(3,),
        in_specs=[
            fixed(1, rows),
            fixed(1, rows, D),
            fixed(D),
            fixed(D),
            pl.BlockSpec((1, D, D), lambda i: (i, 0, 0)),
            pl.BlockSpec(memory_space=pl.ANY),
        ],
        out_specs=[fixed(rows, D)] * 2,
        scratch_shapes=[pltpu.VMEM((rows, D), BF16)] * 4
        + [pltpu.VMEM((D, D), BF16), pltpu.SemaphoreType.DMA],
        compiler_params=pltpu.CompilerParams(vmem_limit_bytes=VMEM_LIMIT),
        cost_estimate=pl.CostEstimate(
            flops=6 * 10**9, bytes_accessed=16 * 10**6, transcendentals=3 * 10**6
        ),
    )(
        ids, patches, gain_one, gain_two, w_qkv, w_out
    )


def device_perm(move):
    pairs = []
    for i in range(128):
        c, g = divmod(i, 16)
        x_lo, y = divmod(c, 4)
        x_hi, r = divmod(g, 8)
        z, core = divmod(r, 2)
        x2, y2, z2, core2 = move(x_hi * 2 + x_lo, y, z, core)
        x2, y2, z2 = x2 % 4, y2 % 4, z2 % 4
        pairs.append((i, ((x2 % 2) * 4 + y2) * 16 + ((x2 // 2) * 4 + z2) * 2 + core2))
    return pairs


OTHER_X = {0: 3, 3: 0, 1: 2, 2: 1}
Z_UP = device_perm(lambda x, y, z, core: (x, y, z + 1, core))
Z_DOWN = device_perm(lambda x, y, z, core: (x, y, z - 1, core))
X_OTHER = device_perm(lambda x, y, z, core: (OTHER_X[x], y, z, core))
CORE_SWAP = device_perm(lambda x, y, z, core: (x, y, z, 1 - core))
BOTH = ("ctx", "img")
NEAR_OFFSETS = ((0, 0), (0, -1), (0, 1), (1, 0), (0, 2))
FAR_OFFSETS = ((1, -1), (1, 1), (1, 2))


def near_shards(shard):
    below = lax.ppermute(shard, BOTH, Z_UP)
    above = lax.ppermute(shard, BOTH, Z_DOWN)
    other = lax.ppermute(shard, BOTH, X_OTHER)
    return [shard, below, above, other]


def far_shards(near):
    shard, below, above, other = near
    half = 128
    far_top = lax.ppermute(below[:half], BOTH, Z_UP)
    far_bottom = lax.ppermute(above[half:], BOTH, Z_DOWN)
    far_top, far_bottom, other = lax.optimization_barrier((far_top, far_bottom, other))
    other_far_top = lax.ppermute(far_top, BOTH, X_OTHER)
    other_far_bottom = lax.ppermute(far_bottom, BOTH, X_OTHER)
    other_below = lax.ppermute(other, BOTH, Z_UP)
    other_above = lax.ppermute(other, BOTH, Z_DOWN)
    return [far_top, far_bottom], [other_below, other_above, other_far_top, other_far_bottom]


def project_kernel(h_own_ref, h_partner_ref, *refs, parts, offsets, aliased):
    count = sum(parts)
    me = lax.axis_index("img")
    my_x, my_z, core = me // 8, me // 2 % 4, me % 2
    weights_refs = refs[:count]
    out_hbm, w_ref, h_ref, done_ref, sem = refs[count + aliased :]
    rows = h_own_ref.shape[0]
    wide = 3 * HEAD_DIM
    for side, ref in ((core, h_own_ref), (1 - core, h_partner_ref)):
        h_ref[pl.ds(pl.multiple_of(side * rows, 16), rows), :] = ref[...]
    at = 0
    for weights_ref in weights_refs:
        w_ref[at : at + weights_ref.shape[0], :] = weights_ref[...]
        at += weights_ref.shape[0]
    part = lax.broadcasted_iota(jnp.int32, (len(parts) * wide, 1), 0) % wide
    scale = jnp.where(part < HEAD_DIM, Q_SCALE, 1.0).astype(F32)
    product = lax.dot_general(w_ref[...], h_ref[...], NT, preferred_element_type=F32)
    product = (product * scale).astype(BF16)
    copies = []
    for n in range(len(parts)):
        done_ref[n] = product[n * wide : (n + 1) * wide]
        target = (my_x + offsets[n][0]) % 2 * 4 + (my_z + offsets[n][1] + 4) % 4
        copy = pltpu.make_async_copy(done_ref.at[n], out_hbm.at[target], sem.at[n])
        copy.start()
        copies.append(copy)
    for copy in copies:
        copy.wait()


def project(offsets, h_own, h_partner, shards, parts, into=None):
    rows = h_own.shape[0]
    wide = 3 * HEAD_DIM
    aliased = 0 if into is None else 1
    return pl.pallas_call(
        functools.partial(
            project_kernel, parts=parts, offsets=offsets, aliased=aliased
        ),
        out_shape=jax.ShapeDtypeStruct((8, wide, 2 * rows), BF16),
        in_specs=whole(2 + len(shards))
        + [pl.BlockSpec(memory_space=pl.ANY)] * aliased,
        out_specs=pl.BlockSpec(memory_space=pl.ANY),
        scratch_shapes=[
            pltpu.VMEM((len(parts) * wide, D), BF16),
            pltpu.VMEM((2 * rows, D), BF16),
            pltpu.VMEM((len(parts), wide, 2 * rows), BF16),
            pltpu.SemaphoreType.DMA((len(parts),)),
        ],
        input_output_aliases={2 + len(shards): 0} if aliased else {},
        compiler_params=pltpu.CompilerParams(vmem_limit_bytes=VMEM_LIMIT),
        cost_estimate=pl.CostEstimate(
            flops=2 * 10**9, bytes_accessed=6 * 10**6, transcendentals=0
        ),
    )(h_own, h_partner, *shards, *([into] if aliased else []))


def attention_kernel(count_ref, q_ref, all_ref, out_ref, k_ref, v_ref, bound_ref, *, block):
    chips, features, rows = all_ref.shape
    total = chips * rows
    depth = HEAD_DIM

    @pl.when(pl.program_id(0) == 0)
    def _():
        count = count_ref[0]
        key_zero = all_ref[0, depth : 2 * depth, 0:1].astype(F32)
        q_most = jnp.zeros((1, rows), F32)
        k_most = jnp.zeros((1, rows), F32)
        v_most = jnp.zeros((HEAD_DIM, rows), F32)
        for chip in range(chips):
            position = chip * rows + lax.broadcasted_iota(jnp.int32, (1, rows), 1)
            valid = position < count
            keys = jnp.where(valid, all_ref[chip, depth : 2 * depth, :].astype(F32), key_zero)
            values = jnp.where(valid, all_ref[chip, 2 * depth :, :].astype(F32), 0.0)
            queries = all_ref[chip, 0:depth, :].astype(F32)
            q_most = jnp.maximum(q_most, jnp.sum(queries * queries, axis=0, keepdims=True))
            k_most = jnp.maximum(k_most, jnp.sum(keys * keys, axis=0, keepdims=True))
            v_most = jnp.maximum(v_most, jnp.abs(values))
            keys = jnp.concatenate([keys, jnp.zeros((128 - depth, rows), F32)], axis=0)
            k_ref[chip * rows : (chip + 1) * rows, :] = keys.astype(BF16).T
            v_ref[0:depth, chip * rows : (chip + 1) * rows] = values.astype(BF16)
            v_ref[depth:, chip * rows : (chip + 1) * rows] = jnp.where(
                (lax.broadcasted_iota(jnp.int32, (16, rows), 0) == 0) & valid, 1.0, 0.0
            ).astype(BF16)
        bound_ref[0] = jnp.max(q_most) * jnp.max(k_most)
        bound_ref[1] = jnp.max(v_most)

    taken = q_ref.shape[0]
    queries = jnp.concatenate([q_ref[n, 0:depth, :] for n in range(taken)], axis=1)
    queries = jnp.concatenate([queries, jnp.zeros((128 - depth, taken * rows), BF16)], axis=0)
    small = (bound_ref[0] < SAFE_BOUND * SAFE_BOUND) & (bound_ref[1] < SAFE_VALUE)

    def store(acc):
        result = acc[0:depth] / acc[depth : depth + 1]
        half = rows // 2
        for n in range(2 * taken):
            out_ref[n] = result[:, n * half : (n + 1) * half].astype(BF16)

    @pl.when(small)
    def _():
        acc = None
        for start in range(0, total, block):
            scores = jnp.dot(k_ref[start : start + block, :], queries, preferred_element_type=F32)
            weights = jnp.exp2(scores).astype(BF16)
            part = jnp.dot(v_ref[:, start : start + block], weights, preferred_element_type=F32)
            acc = part if acc is None else acc + part
        store(acc)

    @pl.when(jnp.logical_not(small))
    def _():
        def step(index, carried):
            most, acc = carried
            start = pl.multiple_of(index * block, block)
            scores = jnp.dot(
                k_ref[pl.ds(start, block), :], queries, preferred_element_type=F32
            )
            new_most = jnp.maximum(most, jnp.max(scores, axis=0, keepdims=True))
            weights = jnp.exp2(scores - new_most).astype(BF16)
            part = jnp.dot(
                v_ref[:, pl.ds(start, block)], weights, preferred_element_type=F32
            )
            return new_most, acc * jnp.exp2(most - new_most) + part

        start_state = (
            jnp.full((1, taken * rows), MASKED_SCORE, F32),
            jnp.zeros((depth + 16, taken * rows), F32),
        )
        store(lax.fori_loop(0, total // block, step, start_state)[1])


def attend_full(count, received):
    chips, features, rows = received.shape
    total = chips * rows
    taken = 2
    return pl.pallas_call(
        functools.partial(attention_kernel, block=512),
        out_shape=jax.ShapeDtypeStruct((2 * chips, HEAD_DIM, rows // 2), BF16),
        grid=(chips // taken,),
        in_specs=[
            pl.BlockSpec(memory_space=pltpu.SMEM),
            pl.BlockSpec((taken, features, rows), lambda i: (i, 0, 0)),
            pl.BlockSpec(memory_space=pltpu.VMEM),
        ],
        out_specs=pl.BlockSpec((2 * taken, HEAD_DIM, rows // 2), lambda i: (i, 0, 0)),
        scratch_shapes=[
            pltpu.VMEM((total, 128), BF16),
            pltpu.VMEM((HEAD_DIM + 16, total), BF16),
            pltpu.SMEM((2,), F32),
        ],
        compiler_params=pltpu.CompilerParams(vmem_limit_bytes=VMEM_LIMIT),
    )(count, received, received)


def merge_kernel(bucket_ref, tag_ref, a_ref, x_ref, w_ref, gain_ref, out_ref):
    attended = a_ref[...]
    third = x_ref[...].astype(F32) + lax.dot_general(
        attended, w_ref[...], TN, preferred_element_type=F32
    )
    merged = normed(third, gain_ref[...]).astype(BF16)
    merged = jnp.concatenate([merged, tag_ref[...]], axis=1)
    places, patches = out_ref.shape[0], merged.shape[0]
    chosen = lax.broadcasted_iota(jnp.int32, (places, patches), 0) == bucket_ref[...]
    out_ref[...] = jnp.dot(
        chosen.astype(BF16), merged, preferred_element_type=F32
    ).astype(BF16)


def merge(bucket, tag, attended, second, w_out, gain, places):
    return pl.pallas_call(
        merge_kernel,
        out_shape=jax.ShapeDtypeStruct((places, D + TAG), BF16),
        in_specs=whole(6),
        out_specs=pl.BlockSpec(memory_space=pltpu.VMEM),
        compiler_params=pltpu.CompilerParams(vmem_limit_bytes=VMEM_LIMIT),
    )(bucket, tag, attended, second, w_out, gain)


def place_kernel(got_ref, out_ref):
    rows = out_ref.shape[0]
    places = got_ref.shape[0]
    tag = got_ref[:, D:].astype(F32).T[0:1].astype(jnp.int32)
    target = 4 * tag + lax.broadcasted_iota(jnp.int32, (1, places), 1) % 4
    index = lax.broadcasted_iota(jnp.int32, (4 * rows, 1), 0)
    wanted = 4 * (index % rows + 1) + index // rows
    chosen = (wanted == target).astype(BF16)
    found = jnp.dot(chosen, got_ref[:, :D], preferred_element_type=F32).astype(BF16)
    for n in range(4):
        out_ref[:, n * D : (n + 1) * D] = found[n * rows : (n + 1) * rows]


def place(got, rows):
    return pl.pallas_call(
        place_kernel,
        out_shape=jax.ShapeDtypeStruct((rows, 4 * D), BF16),
        in_specs=whole(1),
        out_specs=pl.BlockSpec(memory_space=pltpu.VMEM),
        compiler_params=pltpu.CompilerParams(vmem_limit_bytes=VMEM_LIMIT),
    )(got)


def routes_kernel(slots_ref, bucket_ref, tag_ref):
    rows = slots_ref.shape[1]
    slots = jnp.broadcast_to(slots_ref[...], (8, rows))
    owner = slots // rows
    sender = owner.T[:, 0:1]
    earlier = lax.broadcasted_iota(jnp.int32, (rows, rows), 0) < lax.broadcasted_iota(
        jnp.int32, (rows, rows), 1
    )
    rank = jnp.sum(((sender == owner[0:1]) & earlier).astype(jnp.int32), axis=0, keepdims=True)
    bucket = jnp.broadcast_to(4 * (2 * owner[0:1] + rank), (8, rows)).T[:, 0:1]
    lane = lax.broadcasted_iota(jnp.int32, (rows, 4 * rows), 1)
    mine = lane // 4 == lax.broadcasted_iota(jnp.int32, (rows, 4 * rows), 0)
    bucket_ref[...] = jnp.sum(jnp.where(mine, bucket + lane % 4, 0), axis=0, keepdims=True)
    place = (slots - owner * rows + 1).T[:, 0:1].astype(F32)
    patch = lax.broadcasted_iota(jnp.int32, (4 * rows, rows), 0) // 4
    spread = (patch == lax.broadcasted_iota(jnp.int32, (4 * rows, rows), 1)).astype(BF16)
    tag_ref[...] = jnp.dot(
        spread,
        jnp.broadcast_to(place, (rows, TAG)).astype(BF16),
        preferred_element_type=F32,
    ).astype(BF16)


def routes(slots):
    rows = slots.shape[0]
    return pl.pallas_call(
        routes_kernel,
        out_shape=[
            jax.ShapeDtypeStruct((1, 4 * rows), jnp.int32),
            jax.ShapeDtypeStruct((4 * rows, TAG), BF16),
        ],
        in_specs=whole(1),
        out_specs=whole(2),
        compiler_params=pltpu.CompilerParams(vmem_limit_bytes=VMEM_LIMIT),
        cost_estimate=pl.CostEstimate(flops=10**6, bytes_accessed=10**6, transcendentals=0),
    )(slots.reshape(1, rows))


def on_device(
    patches, window_ids, counts, gain_one, w_qkv1, w_out1, gain_two, w_qkv2, w_out2, gain_out, slots
):
    shard = jnp.swapaxes(w_qkv2, 1, 2).reshape(3 * HEAD_DIM, D)
    near = near_shards(shard)
    far, last = far_shards(near)

    second, hidden = layer_one(window_ids, patches, gain_one, gain_two, w_qkv1, w_out1)

    partner = lax.ppermute(hidden, BOTH, CORE_SWAP)
    projected = project(NEAR_OFFSETS, hidden, partner, near + far, (1, 1, 1, 1, 2))
    projected = project(FAR_OFFSETS, hidden, partner, last, (1, 1, 2), into=projected)
    groups = [[2 * chip + core for chip in range(8)] for core in range(2)]
    received = lax.all_to_all(
        projected, "img", split_axis=0, concat_axis=0, tiled=True, axis_index_groups=groups
    )
    slots, projected = lax.optimization_barrier((slots, projected))
    bucket_rows, tag = routes(slots)
    attended = attend_full(counts, received)
    attended = lax.all_to_all(attended, "img", split_axis=0, concat_axis=0, tiled=True)
    places = 128 * 2 * 4
    send = merge(bucket_rows, tag, attended.reshape(D, -1), second, w_out2, gain_out, places)
    got = lax.all_to_all(
        send.reshape(128, 8, D + TAG), BOTH, split_axis=0, concat_axis=0, tiled=True
    )
    return place(got.reshape(places, D + TAG), slots.shape[0])


def solution(mesh):
    return jax.shard_map(
        on_device,
        mesh=mesh,
        in_specs=(
            P("ctx", "img", None),
            P("ctx", "img"),
            P("ctx"),
            P(),
            P(),
            P(),
            P(),
            P(None, None, "img"),
            P(),
            P(),
            P(("ctx", "img")),
        ),
        out_specs=P(("ctx", "img"), None),
        check_vma=False,
    )
```

```python
import functools
import math

import jax
import jax.numpy as jnp
from jax import lax
from jax.experimental import pallas as pl
from jax.experimental.pallas import tpu as pltpu
from jax.sharding import PartitionSpec as P

HEAD_DIM = 80
D = 1280
EPSILON = 1e-06
MASKED_SCORE = -1e30
F32 = jnp.float32
BF16 = jnp.bfloat16
Q_SCALE = HEAD_DIM ** (-0.5) * math.log2(math.e)
WINDOW = 64
QUERY_BLOCK = 384
TAG = 128
SAFE_BOUND = 64.0
SAFE_VALUE = 2.0**40
VMEM_LIMIT = 56 * 1024 * 1024
VMEM_ALL = 63 * 1024 * 1024
NT = (((1,), (1,)), ((), ()))
TN = (((0,), (0,)), ((), ()))


def normed(values, gain):
    values = values.astype(F32)
    return (
        values
        * lax.rsqrt(jnp.mean(values * values, axis=-1, keepdims=True) + EPSILON)
        * gain.astype(F32).reshape(1, -1)
    )


def whole(count):
    return [pl.BlockSpec(memory_space=pltpu.VMEM)] * count


def layer_one_kernel(
    ids_ref, x_ref, gain_one_ref, gain_two_ref, w_qkv_ref, w_out_hbm,
    second_ref, hidden_ref, h_ref, q_ref, k_ref, a_ref, w_out_ref, sem,
):
    step = pl.program_id(0)
    copy = pltpu.make_async_copy(w_out_hbm, w_out_ref, sem)

    @pl.when(step == 0)
    def _():
        h_ref[...] = normed(x_ref[0], gain_one_ref[...]).astype(BF16)

    def project_one(scale=None):
        product = jnp.dot(h_ref[...], w_qkv_ref[0], preferred_element_type=F32)
        return (product if scale is None else product * scale).astype(BF16)

    @pl.when(step == 0)
    def _():
        q_ref[...] = project_one(Q_SCALE)

    @pl.when(step == 1)
    def _():
        copy.start()
        k_ref[...] = project_one()

    @pl.when(step == 2)
    def _():
        values_all = project_one()
        rows = ids_ref.shape[1]
        ids = jnp.broadcast_to(ids_ref[...], (8, rows))
        ids_column = ids.T[:, 0:1]
        spans = []
        for start in range(0, rows, QUERY_BLOCK):
            begin = max(start - WINDOW, 0)
            end = min(start + QUERY_BLOCK + WINDOW, rows)
            allowed = ids_column[start : start + QUERY_BLOCK] == ids[0:1, begin:end]
            spans.append((start, begin, end, allowed))
        tiles = {}
        allowed = spans[0][3]

        def window(head):
            first, last = head * HEAD_DIM, (head + 1) * HEAD_DIM
            low, high = first // 128 * 128, (last + 127) // 128 * 128
            lane = low + lax.broadcasted_iota(jnp.int32, (1, high - low), 1)
            return low, high, last, (lane >= first) & (lane < last)

        def score(head):
            low, high, last, mine = window(head)
            keys = jnp.where(mine, k_ref[:, low:high], 0.0).astype(BF16)
            return lax.dot_general(q_ref[:, low:high], keys, NT, preferred_element_type=F32)

        heads = D // HEAD_DIM
        ahead = score(0)
        for head in range(heads):
            scores = jnp.where(allowed, ahead, MASKED_SCORE)
            if head + 1 < heads:
                ahead = score(head + 1)
            low, high, last, mine = window(head)
            most = jnp.max(scores, axis=1, keepdims=True)
            weights = jnp.exp2(scores - most)
            total = jnp.sum(weights, axis=1, keepdims=True)
            result = jnp.dot(
                weights.astype(BF16), values_all[:, low:high], preferred_element_type=F32
            ) * (1.0 / total)
            for tile in range(low, high, 128):
                piece = result[:, tile - low : tile - low + 128]
                if tile in tiles:
                    piece = jnp.where(mine[:, tile - low : tile - low + 128], piece, tiles[tile])
                tiles[tile] = piece
                if tile + 128 <= last:
                    a_ref[:, tile : tile + 128] = tiles.pop(tile).astype(BF16)
        copy.wait()
        second = x_ref[0].astype(F32) + jnp.dot(
            a_ref[...], w_out_ref[...], preferred_element_type=F32
        )
        second = second.astype(BF16)
        second_ref[...] = second
        hidden_ref[...] = normed(second, gain_two_ref[...]).astype(BF16)


def layer_one(ids, patches, gain_one, gain_two, w_qkv, w_out):
    rows = patches.shape[1]
    fixed = lambda *shape: pl.BlockSpec(shape, lambda i: (0,) * len(shape))
    return pl.pallas_call(
        layer_one_kernel,
        out_shape=[jax.ShapeDtypeStruct((rows, D), BF16)] * 2,
        grid=(3,),
        in_specs=[
            fixed(1, rows),
            fixed(1, rows, D),
            fixed(D),
            fixed(D),
            pl.BlockSpec((1, D, D), lambda i: (i, 0, 0)),
            pl.BlockSpec(memory_space=pl.ANY),
        ],
        out_specs=[fixed(rows, D)] * 2,
        scratch_shapes=[pltpu.VMEM((rows, D), BF16)] * 4
        + [pltpu.VMEM((D, D), BF16), pltpu.SemaphoreType.DMA],
        compiler_params=pltpu.CompilerParams(vmem_limit_bytes=VMEM_LIMIT),
        cost_estimate=pl.CostEstimate(
            flops=6 * 10**9, bytes_accessed=16 * 10**6, transcendentals=3 * 10**6
        ),
    )(
        ids, patches, gain_one, gain_two, w_qkv, w_out
    )


def device_perm(move):
    pairs = []
    for i in range(128):
        c, g = divmod(i, 16)
        x_lo, y = divmod(c, 4)
        x_hi, r = divmod(g, 8)
        z, core = divmod(r, 2)
        x2, y2, z2, core2 = move(x_hi * 2 + x_lo, y, z, core)
        x2, y2, z2 = x2 % 4, y2 % 4, z2 % 4
        pairs.append((i, ((x2 % 2) * 4 + y2) * 16 + ((x2 // 2) * 4 + z2) * 2 + core2))
    return pairs


OTHER_X = {0: 3, 3: 0, 1: 2, 2: 1}
Z_UP = device_perm(lambda x, y, z, core: (x, y, z + 1, core))
Z_DOWN = device_perm(lambda x, y, z, core: (x, y, z - 1, core))
X_OTHER = device_perm(lambda x, y, z, core: (OTHER_X[x], y, z, core))
CORE_SWAP = device_perm(lambda x, y, z, core: (x, y, z, 1 - core))
BOTH = ("ctx", "img")
NEAR_OFFSETS = ((0, 0), (0, -1), (0, 1), (1, 0), (0, 2))
FAR_OFFSETS = ((1, -1), (1, 1), (1, 2))


def near_shards(shard):
    below = lax.ppermute(shard, BOTH, Z_UP)
    above = lax.ppermute(shard, BOTH, Z_DOWN)
    other = lax.ppermute(shard, BOTH, X_OTHER)
    return [shard, below, above, other]


def far_shards(near):
    shard, below, above, other = near
    half = 128
    far_top = lax.ppermute(below[:half], BOTH, Z_UP)
    far_bottom = lax.ppermute(above[half:], BOTH, Z_DOWN)
    far_top, far_bottom, other = lax.optimization_barrier((far_top, far_bottom, other))
    other_far_top = lax.ppermute(far_top, BOTH, X_OTHER)
    other_far_bottom = lax.ppermute(far_bottom, BOTH, X_OTHER)
    other_below = lax.ppermute(other, BOTH, Z_UP)
    other_above = lax.ppermute(other, BOTH, Z_DOWN)
    return [far_top, far_bottom], [other_below, other_above, other_far_top, other_far_bottom]


def project_kernel(h_own_ref, h_partner_ref, *refs, parts, offsets, aliased):
    count = sum(parts)
    me = lax.axis_index("img")
    my_x, my_z, core = me // 8, me // 2 % 4, me % 2
    weights_refs = refs[:count]
    out_hbm, w_ref, h_ref, done_ref, sem, in_sem = refs[count + aliased :]
    rows = h_own_ref.shape[0]
    wide = 3 * HEAD_DIM
    loads = []
    at = 0
    for n, weights_ref in enumerate(weights_refs):
        end = at + weights_ref.shape[0]
        load = pltpu.make_async_copy(weights_ref, w_ref.at[at:end], in_sem.at[n])
        load.start()
        loads.append(load)
        at = end
    for side, ref in ((core, h_own_ref), (1 - core, h_partner_ref)):
        h_ref[pl.ds(pl.multiple_of(side * rows, 16), rows), :] = ref[...]
    part = lax.broadcasted_iota(jnp.int32, (len(parts) * wide, 1), 0) % wide
    scale = jnp.where(part < HEAD_DIM, Q_SCALE, 1.0).astype(F32)
    for load in loads:
        load.wait()
    product = lax.dot_general(w_ref[...], h_ref[...], NT, preferred_element_type=F32)
    product = (product * scale).astype(BF16)
    copies = []
    for n in range(len(parts)):
        done_ref[n] = product[n * wide : (n + 1) * wide]
        target = (my_x + offsets[n][0]) % 2 * 4 + (my_z + offsets[n][1] + 4) % 4
        copy = pltpu.make_async_copy(done_ref.at[n], out_hbm.at[target], sem.at[n])
        copy.start()
        copies.append(copy)
    for copy in copies:
        copy.wait()


def project(offsets, h_own, h_partner, shards, parts, into=None):
    rows = h_own.shape[0]
    wide = 3 * HEAD_DIM
    aliased = 0 if into is None else 1
    return pl.pallas_call(
        functools.partial(
            project_kernel, parts=parts, offsets=offsets, aliased=aliased
        ),
        out_shape=jax.ShapeDtypeStruct((8, wide, 2 * rows), BF16),
        in_specs=whole(2) + [pl.BlockSpec(memory_space=pl.ANY)] * (len(shards) + aliased),
        out_specs=pl.BlockSpec(memory_space=pl.ANY),
        scratch_shapes=[
            pltpu.VMEM((len(parts) * wide, D), BF16),
            pltpu.VMEM((2 * rows, D), BF16),
            pltpu.VMEM((len(parts), wide, 2 * rows), BF16),
            pltpu.SemaphoreType.DMA((len(parts),)),
            pltpu.SemaphoreType.DMA((len(shards),)),
        ],
        input_output_aliases={2 + len(shards): 0} if aliased else {},
        compiler_params=pltpu.CompilerParams(vmem_limit_bytes=VMEM_ALL),
        cost_estimate=pl.CostEstimate(
            flops=2 * 10**9, bytes_accessed=6 * 10**6, transcendentals=0
        ),
    )(h_own, h_partner, *shards, *([into] if aliased else []))


def attention_kernel(
    count_ref, all_hbm, out_ref, all_ref, k_ref, v_ref, bound_ref, sem, *, block, taken
):
    chips, features, rows = all_ref.shape
    total = chips * rows
    depth = HEAD_DIM

    @pl.when(pl.program_id(0) == 0)
    def _():
        copies = [
            pltpu.make_async_copy(all_hbm.at[chip], all_ref.at[chip], sem.at[chip])
            for chip in range(chips)
        ]
        for copy in copies:
            copy.start()
        count = count_ref[0]
        copies[0].wait()
        key_zero = all_ref[0, depth : 2 * depth, 0:1].astype(F32)
        q_most = jnp.zeros((1, rows), F32)
        k_most = jnp.zeros((1, rows), F32)
        v_most = jnp.zeros((HEAD_DIM, rows), F32)
        for chip in range(chips):
            if chip:
                copies[chip].wait()
            position = chip * rows + lax.broadcasted_iota(jnp.int32, (1, rows), 1)
            valid = position < count
            keys = jnp.where(valid, all_ref[chip, depth : 2 * depth, :].astype(F32), key_zero)
            values = jnp.where(valid, all_ref[chip, 2 * depth :, :].astype(F32), 0.0)
            queries = all_ref[chip, 0:depth, :].astype(F32)
            q_most = jnp.maximum(q_most, jnp.sum(queries * queries, axis=0, keepdims=True))
            k_most = jnp.maximum(k_most, jnp.sum(keys * keys, axis=0, keepdims=True))
            v_most = jnp.maximum(v_most, jnp.abs(values))
            keys = jnp.concatenate([keys, jnp.zeros((128 - depth, rows), F32)], axis=0)
            k_ref[chip * rows : (chip + 1) * rows, :] = keys.astype(BF16).T
            v_ref[0:depth, chip * rows : (chip + 1) * rows] = values.astype(BF16)
            v_ref[depth:, chip * rows : (chip + 1) * rows] = jnp.where(
                (lax.broadcasted_iota(jnp.int32, (16, rows), 0) == 0) & valid, 1.0, 0.0
            ).astype(BF16)
        bound_ref[0] = jnp.max(q_most) * jnp.max(k_most)
        bound_ref[1] = jnp.max(v_most)

    first = taken * pl.program_id(0)
    queries = jnp.concatenate([all_ref[first + n, 0:depth, :] for n in range(taken)], axis=1)
    queries = jnp.concatenate([queries, jnp.zeros((128 - depth, taken * rows), BF16)], axis=0)
    small = (bound_ref[0] < SAFE_BOUND * SAFE_BOUND) & (bound_ref[1] < SAFE_VALUE)

    def store(acc):
        result = acc[0:depth] / acc[depth : depth + 1]
        half = rows // 2
        for n in range(2 * taken):
            out_ref[n] = result[:, n * half : (n + 1) * half].astype(BF16)

    @pl.when(small)
    def _():
        acc = None
        for start in range(0, total, block):
            scores = jnp.dot(k_ref[start : start + block, :], queries, preferred_element_type=F32)
            weights = jnp.exp2(scores).astype(BF16)
            part = jnp.dot(v_ref[:, start : start + block], weights, preferred_element_type=F32)
            acc = part if acc is None else acc + part
        store(acc)

    @pl.when(jnp.logical_not(small))
    def _():
        def step(index, carried):
            most, acc = carried
            start = pl.multiple_of(index * block, block)
            scores = jnp.dot(
                k_ref[pl.ds(start, block), :], queries, preferred_element_type=F32
            )
            new_most = jnp.maximum(most, jnp.max(scores, axis=0, keepdims=True))
            weights = jnp.exp2(scores - new_most).astype(BF16)
            part = jnp.dot(
                v_ref[:, pl.ds(start, block)], weights, preferred_element_type=F32
            )
            return new_most, acc * jnp.exp2(most - new_most) + part

        start_state = (
            jnp.full((1, taken * rows), MASKED_SCORE, F32),
            jnp.zeros((depth + 16, taken * rows), F32),
        )
        store(lax.fori_loop(0, total // block, step, start_state)[1])


def attend_full(count, received):
    chips, features, rows = received.shape
    total = chips * rows
    taken = 2
    return pl.pallas_call(
        functools.partial(attention_kernel, block=512, taken=taken),
        out_shape=jax.ShapeDtypeStruct((2 * chips, HEAD_DIM, rows // 2), BF16),
        grid=(chips // taken,),
        in_specs=[
            pl.BlockSpec(memory_space=pltpu.SMEM),
            pl.BlockSpec(memory_space=pl.ANY),
        ],
        out_specs=pl.BlockSpec((2 * taken, HEAD_DIM, rows // 2), lambda i: (i, 0, 0)),
        scratch_shapes=[
            pltpu.VMEM(received.shape, BF16),
            pltpu.VMEM((total, 128), BF16),
            pltpu.VMEM((HEAD_DIM + 16, total), BF16),
            pltpu.SMEM((2,), F32),
            pltpu.SemaphoreType.DMA((chips,)),
        ],
        compiler_params=pltpu.CompilerParams(vmem_limit_bytes=VMEM_ALL),
    )(count, received)


def merge_kernel(bucket_ref, tag_ref, a_ref, x_ref, w_ref, gain_ref, out_ref):
    attended = a_ref[...]
    third = x_ref[...].astype(F32) + lax.dot_general(
        attended, w_ref[...], TN, preferred_element_type=F32
    )
    merged = normed(third, gain_ref[...]).astype(BF16)
    merged = jnp.concatenate([merged, tag_ref[...]], axis=1)
    places, patches = out_ref.shape[0], merged.shape[0]
    chosen = lax.broadcasted_iota(jnp.int32, (places, patches), 0) == bucket_ref[...]
    out_ref[...] = jnp.dot(
        chosen.astype(BF16), merged, preferred_element_type=F32
    ).astype(BF16)


def merge(bucket, tag, attended, second, w_out, gain, places):
    return pl.pallas_call(
        merge_kernel,
        out_shape=jax.ShapeDtypeStruct((places, D + TAG), BF16),
        in_specs=whole(6),
        out_specs=pl.BlockSpec(memory_space=pltpu.VMEM),
        compiler_params=pltpu.CompilerParams(vmem_limit_bytes=VMEM_LIMIT),
    )(bucket, tag, attended, second, w_out, gain)


def place_kernel(got_ref, out_ref):
    rows = out_ref.shape[0]
    places = got_ref.shape[0]
    tag = got_ref[:, D:].astype(F32).T[0:1].astype(jnp.int32)
    target = 4 * tag + lax.broadcasted_iota(jnp.int32, (1, places), 1) % 4
    index = lax.broadcasted_iota(jnp.int32, (4 * rows, 1), 0)
    wanted = 4 * (index % rows + 1) + index // rows
    chosen = (wanted == target).astype(BF16)
    found = jnp.dot(chosen, got_ref[:, :D], preferred_element_type=F32).astype(BF16)
    for n in range(4):
        out_ref[:, n * D : (n + 1) * D] = found[n * rows : (n + 1) * rows]


def place(got, rows):
    return pl.pallas_call(
        place_kernel,
        out_shape=jax.ShapeDtypeStruct((rows, 4 * D), BF16),
        in_specs=whole(1),
        out_specs=pl.BlockSpec(memory_space=pltpu.VMEM),
        compiler_params=pltpu.CompilerParams(vmem_limit_bytes=VMEM_LIMIT),
    )(got)


def routes_kernel(slots_ref, bucket_ref, tag_ref):
    rows = slots_ref.shape[1]
    slots = jnp.broadcast_to(slots_ref[...], (8, rows))
    owner = slots // rows
    sender = owner.T[:, 0:1]
    earlier = lax.broadcasted_iota(jnp.int32, (rows, rows), 0) < lax.broadcasted_iota(
        jnp.int32, (rows, rows), 1
    )
    rank = jnp.sum(((sender == owner[0:1]) & earlier).astype(jnp.int32), axis=0, keepdims=True)
    bucket = jnp.broadcast_to(4 * (2 * owner[0:1] + rank), (8, rows)).T[:, 0:1]
    lane = lax.broadcasted_iota(jnp.int32, (rows, 4 * rows), 1)
    mine = lane // 4 == lax.broadcasted_iota(jnp.int32, (rows, 4 * rows), 0)
    bucket_ref[...] = jnp.sum(jnp.where(mine, bucket + lane % 4, 0), axis=0, keepdims=True)
    place = (slots - owner * rows + 1).T[:, 0:1].astype(F32)
    patch = lax.broadcasted_iota(jnp.int32, (4 * rows, rows), 0) // 4
    spread = (patch == lax.broadcasted_iota(jnp.int32, (4 * rows, rows), 1)).astype(BF16)
    tag_ref[...] = jnp.dot(
        spread,
        jnp.broadcast_to(place, (rows, TAG)).astype(BF16),
        preferred_element_type=F32,
    ).astype(BF16)


def routes(slots):
    rows = slots.shape[0]
    return pl.pallas_call(
        routes_kernel,
        out_shape=[
            jax.ShapeDtypeStruct((1, 4 * rows), jnp.int32),
            jax.ShapeDtypeStruct((4 * rows, TAG), BF16),
        ],
        in_specs=whole(1),
        out_specs=whole(2),
        compiler_params=pltpu.CompilerParams(vmem_limit_bytes=VMEM_LIMIT),
        cost_estimate=pl.CostEstimate(flops=10**6, bytes_accessed=10**6, transcendentals=0),
    )(slots.reshape(1, rows))


def on_device(
    patches, window_ids, counts, gain_one, w_qkv1, w_out1, gain_two, w_qkv2, w_out2, gain_out, slots
):
    shard = jnp.swapaxes(w_qkv2, 1, 2).reshape(3 * HEAD_DIM, D)
    near = near_shards(shard)
    far, last = far_shards(near)

    second, hidden = layer_one(window_ids, patches, gain_one, gain_two, w_qkv1, w_out1)

    partner = lax.ppermute(hidden, BOTH, CORE_SWAP)
    projected = project(NEAR_OFFSETS, hidden, partner, near + far, (1, 1, 1, 1, 2))
    projected = project(FAR_OFFSETS, hidden, partner, last, (1, 1, 2), into=projected)
    groups = [[2 * chip + core for chip in range(8)] for core in range(2)]
    received = lax.all_to_all(
        projected, "img", split_axis=0, concat_axis=0, tiled=True, axis_index_groups=groups
    )
    slots, projected = lax.optimization_barrier((slots, projected))
    bucket_rows, tag = routes(slots)
    attended = attend_full(counts, received)
    attended = lax.all_to_all(attended, "img", split_axis=0, concat_axis=0, tiled=True)
    places = 128 * 2 * 4
    send = merge(bucket_rows, tag, attended.reshape(D, -1), second, w_out2, gain_out, places)
    got = lax.all_to_all(
        send.reshape(128, 8, D + TAG), BOTH, split_axis=0, concat_axis=0, tiled=True
    )
    return place(got.reshape(places, D + TAG), slots.shape[0])


def solution(mesh):
    return jax.shard_map(
        on_device,
        mesh=mesh,
        in_specs=(
            P("ctx", "img", None),
            P("ctx", "img"),
            P("ctx"),
            P(),
            P(),
            P(),
            P(),
            P(None, None, "img"),
            P(),
            P(),
            P(("ctx", "img")),
        ),
        out_specs=P(("ctx", "img"), None),
        check_vma=False,
    )
```

```python
import functools
import math

import jax
import jax.numpy as jnp
from jax import lax
from jax.experimental import pallas as pl
from jax.experimental.pallas import tpu as pltpu
from jax.sharding import PartitionSpec as P

HEAD_DIM = 80
D = 1280
EPSILON = 1e-06
MASKED_SCORE = -1e30
F32 = jnp.float32
BF16 = jnp.bfloat16
Q_SCALE = HEAD_DIM ** (-0.5) * math.log2(math.e)
WINDOW = 64
QUERY_BLOCK = 384
TAG = 128
SAFE_BOUND = 64.0
SAFE_VALUE = 2.0**40
VMEM_LIMIT = 56 * 1024 * 1024
VMEM_ALL = 63 * 1024 * 1024
NT = (((1,), (1,)), ((), ()))
TN = (((0,), (0,)), ((), ()))


def normed(values, gain):
    values = values.astype(F32)
    return (
        values
        * lax.rsqrt(jnp.mean(values * values, axis=-1, keepdims=True) + EPSILON)
        * gain.astype(F32).reshape(1, -1)
    )


def whole(count):
    return [pl.BlockSpec(memory_space=pltpu.VMEM)] * count


def layer_one_kernel(
    ids_ref, x_ref, gain_one_ref, gain_two_ref, w_qkv_ref, w_out_hbm,
    second_ref, hidden_ref, h_ref, q_ref, k_ref, a_ref, w_out_ref, sem,
):
    step = pl.program_id(0)
    copy = pltpu.make_async_copy(w_out_hbm, w_out_ref, sem)

    @pl.when(step == 0)
    def _():
        h_ref[...] = normed(x_ref[0], gain_one_ref[...]).astype(BF16)

    def project_one(scale=None):
        product = jnp.dot(h_ref[...], w_qkv_ref[0], preferred_element_type=F32)
        return (product if scale is None else product * scale).astype(BF16)

    @pl.when(step == 0)
    def _():
        q_ref[...] = project_one(Q_SCALE)

    @pl.when(step == 1)
    def _():
        copy.start()
        k_ref[...] = project_one()

    @pl.when(step == 2)
    def _():
        values_all = project_one()
        rows = ids_ref.shape[1]
        ids = jnp.broadcast_to(ids_ref[...], (8, rows))
        ids_column = ids.T[:, 0:1]
        spans = []
        for start in range(0, rows, QUERY_BLOCK):
            begin = max(start - WINDOW, 0)
            end = min(start + QUERY_BLOCK + WINDOW, rows)
            allowed = ids_column[start : start + QUERY_BLOCK] == ids[0:1, begin:end]
            spans.append((start, begin, end, allowed))
        tiles = {}
        allowed = spans[0][3]

        def window(head):
            first, last = head * HEAD_DIM, (head + 1) * HEAD_DIM
            low, high = first // 128 * 128, (last + 127) // 128 * 128
            lane = low + lax.broadcasted_iota(jnp.int32, (1, high - low), 1)
            return low, high, last, (lane >= first) & (lane < last)

        def score(head):
            low, high, last, mine = window(head)
            keys = jnp.where(mine, k_ref[:, low:high], 0.0).astype(BF16)
            return lax.dot_general(q_ref[:, low:high], keys, NT, preferred_element_type=F32)

        heads = D // HEAD_DIM
        ahead = score(0)
        for head in range(heads):
            scores = jnp.where(allowed, ahead, MASKED_SCORE)
            if head + 1 < heads:
                ahead = score(head + 1)
            low, high, last, mine = window(head)
            most = jnp.max(scores, axis=1, keepdims=True)
            weights = jnp.exp2(scores - most)
            total = jnp.sum(weights, axis=1, keepdims=True)
            result = jnp.dot(
                weights.astype(BF16), values_all[:, low:high], preferred_element_type=F32
            ) * (1.0 / total)
            for tile in range(low, high, 128):
                piece = result[:, tile - low : tile - low + 128]
                if tile in tiles:
                    piece = jnp.where(mine[:, tile - low : tile - low + 128], piece, tiles[tile])
                tiles[tile] = piece
                if tile + 128 <= last:
                    a_ref[:, tile : tile + 128] = tiles.pop(tile).astype(BF16)
        copy.wait()
        second = x_ref[0].astype(F32) + jnp.dot(
            a_ref[...], w_out_ref[...], preferred_element_type=F32
        )
        second = second.astype(BF16)
        second_ref[...] = second
        hidden_ref[...] = normed(second, gain_two_ref[...]).astype(BF16)


def layer_one(ids, patches, gain_one, gain_two, w_qkv, w_out):
    rows = patches.shape[1]
    fixed = lambda *shape: pl.BlockSpec(shape, lambda i: (0,) * len(shape))
    return pl.pallas_call(
        layer_one_kernel,
        out_shape=[jax.ShapeDtypeStruct((rows, D), BF16)] * 2,
        grid=(3,),
        in_specs=[
            fixed(1, rows),
            fixed(1, rows, D),
            fixed(D),
            fixed(D),
            pl.BlockSpec((1, D, D), lambda i: (i, 0, 0)),
            pl.BlockSpec(memory_space=pl.ANY),
        ],
        out_specs=[fixed(rows, D)] * 2,
        scratch_shapes=[pltpu.VMEM((rows, D), BF16)] * 4
        + [pltpu.VMEM((D, D), BF16), pltpu.SemaphoreType.DMA],
        compiler_params=pltpu.CompilerParams(vmem_limit_bytes=VMEM_LIMIT),
        cost_estimate=pl.CostEstimate(
            flops=6 * 10**9, bytes_accessed=16 * 10**6, transcendentals=3 * 10**6
        ),
    )(
        ids, patches, gain_one, gain_two, w_qkv, w_out
    )


def device_perm(move):
    pairs = []
    for i in range(128):
        c, g = divmod(i, 16)
        x_lo, y = divmod(c, 4)
        x_hi, r = divmod(g, 8)
        z, core = divmod(r, 2)
        x2, y2, z2, core2 = move(x_hi * 2 + x_lo, y, z, core)
        x2, y2, z2 = x2 % 4, y2 % 4, z2 % 4
        pairs.append((i, ((x2 % 2) * 4 + y2) * 16 + ((x2 // 2) * 4 + z2) * 2 + core2))
    return pairs


OTHER_X = {0: 3, 3: 0, 1: 2, 2: 1}
Z_UP = device_perm(lambda x, y, z, core: (x, y, z + 1, core))
Z_DOWN = device_perm(lambda x, y, z, core: (x, y, z - 1, core))
X_OTHER = device_perm(lambda x, y, z, core: (OTHER_X[x], y, z, core))
CORE_SWAP = device_perm(lambda x, y, z, core: (x, y, z, 1 - core))
BOTH = ("ctx", "img")
NEAR_OFFSETS = ((0, 0), (0, -1), (0, 1), (1, 0), (0, 2))
FAR_OFFSETS = ((1, -1), (1, 1), (1, 2))


def near_shards(shard):
    below = lax.ppermute(shard, BOTH, Z_UP)
    above = lax.ppermute(shard, BOTH, Z_DOWN)
    other = lax.ppermute(shard, BOTH, X_OTHER)
    return [shard, below, above, other]


def far_shards(near):
    shard, below, above, other = near
    half = 128
    far_top = lax.ppermute(below[:half], BOTH, Z_UP)
    far_bottom = lax.ppermute(above[half:], BOTH, Z_DOWN)
    far_top, far_bottom, other = lax.optimization_barrier((far_top, far_bottom, other))
    other_far_top = lax.ppermute(far_top, BOTH, X_OTHER)
    other_far_bottom = lax.ppermute(far_bottom, BOTH, X_OTHER)
    other_below = lax.ppermute(other, BOTH, Z_UP)
    other_above = lax.ppermute(other, BOTH, Z_DOWN)
    return [far_top, far_bottom], [other_below, other_above, other_far_top, other_far_bottom]


def project_kernel(h_own_ref, h_partner_ref, *refs, parts, offsets, aliased):
    count = sum(parts)
    me = lax.axis_index("img")
    my_x, my_z, core = me // 8, me // 2 % 4, me % 2
    weights_refs = refs[:count]
    out_hbm, w_ref, h_ref, done_ref, sem, in_sem = refs[count + aliased :]
    rows = h_own_ref.shape[0]
    wide = 3 * HEAD_DIM
    loads = []
    at = 0
    for n, weights_ref in enumerate(weights_refs):
        end = at + weights_ref.shape[0]
        load = pltpu.make_async_copy(weights_ref, w_ref.at[at:end], in_sem.at[n])
        load.start()
        loads.append(load)
        at = end
    for n, (side, ref) in enumerate(((core, h_own_ref), (1 - core, h_partner_ref))):
        load = pltpu.make_async_copy(
            ref, h_ref.at[pl.ds(pl.multiple_of(side * rows, 16), rows)], in_sem.at[count + n]
        )
        load.start()
        loads.append(load)
    part = lax.broadcasted_iota(jnp.int32, (len(parts) * wide, 1), 0) % wide
    scale = jnp.where(part < HEAD_DIM, Q_SCALE, 1.0).astype(F32)
    for load in loads:
        load.wait()
    product = lax.dot_general(w_ref[...], h_ref[...], NT, preferred_element_type=F32)
    product = (product * scale).astype(BF16)
    copies = []
    for n in range(len(parts)):
        done_ref[n] = product[n * wide : (n + 1) * wide]
        target = (my_x + offsets[n][0]) % 2 * 4 + (my_z + offsets[n][1] + 4) % 4
        copy = pltpu.make_async_copy(done_ref.at[n], out_hbm.at[target], sem.at[n])
        copy.start()
        copies.append(copy)
    for copy in copies:
        copy.wait()


def project(offsets, h_own, h_partner, shards, parts, into=None):
    rows = h_own.shape[0]
    wide = 3 * HEAD_DIM
    aliased = 0 if into is None else 1
    return pl.pallas_call(
        functools.partial(
            project_kernel, parts=parts, offsets=offsets, aliased=aliased
        ),
        out_shape=jax.ShapeDtypeStruct((8, wide, 2 * rows), BF16),
        in_specs=[pl.BlockSpec(memory_space=pl.ANY)] * (2 + len(shards) + aliased),
        out_specs=pl.BlockSpec(memory_space=pl.ANY),
        scratch_shapes=[
            pltpu.VMEM((len(parts) * wide, D), BF16),
            pltpu.VMEM((2 * rows, D), BF16),
            pltpu.VMEM((len(parts), wide, 2 * rows), BF16),
            pltpu.SemaphoreType.DMA((len(parts),)),
            pltpu.SemaphoreType.DMA((len(shards) + 2,)),
        ],
        input_output_aliases={2 + len(shards): 0} if aliased else {},
        compiler_params=pltpu.CompilerParams(vmem_limit_bytes=VMEM_ALL),
        cost_estimate=pl.CostEstimate(
            flops=2 * 10**9, bytes_accessed=6 * 10**6, transcendentals=0
        ),
    )(h_own, h_partner, *shards, *([into] if aliased else []))


def attention_kernel(
    count_ref, all_hbm, out_ref, all_ref, k_ref, v_ref, bound_ref, sem, *, block, taken
):
    chips, features, rows = all_ref.shape
    total = chips * rows
    depth = HEAD_DIM

    @pl.when(pl.program_id(0) == 0)
    def _():
        copies = [
            pltpu.make_async_copy(all_hbm.at[chip], all_ref.at[chip], sem.at[chip])
            for chip in range(chips)
        ]
        for copy in copies:
            copy.start()
        count = count_ref[0]
        copies[0].wait()
        key_zero = all_ref[0, depth : 2 * depth, 0:1].astype(F32)
        q_most = jnp.zeros((1, rows), F32)
        k_most = jnp.zeros((1, rows), F32)
        v_most = jnp.zeros((HEAD_DIM, rows), F32)
        for chip in range(chips):
            if chip:
                copies[chip].wait()
            position = chip * rows + lax.broadcasted_iota(jnp.int32, (1, rows), 1)
            valid = position < count
            keys = jnp.where(valid, all_ref[chip, depth : 2 * depth, :].astype(F32), key_zero)
            values = jnp.where(valid, all_ref[chip, 2 * depth :, :].astype(F32), 0.0)
            queries = all_ref[chip, 0:depth, :].astype(F32)
            q_most = jnp.maximum(q_most, jnp.sum(queries * queries, axis=0, keepdims=True))
            k_most = jnp.maximum(k_most, jnp.sum(keys * keys, axis=0, keepdims=True))
            v_most = jnp.maximum(v_most, jnp.abs(values))
            keys = jnp.concatenate([keys, jnp.zeros((128 - depth, rows), F32)], axis=0)
            k_ref[chip * rows : (chip + 1) * rows, :] = keys.astype(BF16).T
            v_ref[0:depth, chip * rows : (chip + 1) * rows] = values.astype(BF16)
            v_ref[depth:, chip * rows : (chip + 1) * rows] = jnp.where(
                (lax.broadcasted_iota(jnp.int32, (16, rows), 0) == 0) & valid, 1.0, 0.0
            ).astype(BF16)
        bound_ref[0] = jnp.max(q_most) * jnp.max(k_most)
        bound_ref[1] = jnp.max(v_most)

    first = taken * pl.program_id(0)
    queries = jnp.concatenate([all_ref[first + n, 0:depth, :] for n in range(taken)], axis=1)
    queries = jnp.concatenate([queries, jnp.zeros((128 - depth, taken * rows), BF16)], axis=0)
    small = (bound_ref[0] < SAFE_BOUND * SAFE_BOUND) & (bound_ref[1] < SAFE_VALUE)

    def store(acc):
        result = acc[0:depth] / acc[depth : depth + 1]
        half = rows // 2
        for n in range(2 * taken):
            out_ref[n] = result[:, n * half : (n + 1) * half].astype(BF16)

    @pl.when(small)
    def _():
        acc = None
        for start in range(0, total, block):
            scores = jnp.dot(k_ref[start : start + block, :], queries, preferred_element_type=F32)
            weights = jnp.exp2(scores).astype(BF16)
            part = jnp.dot(v_ref[:, start : start + block], weights, preferred_element_type=F32)
            acc = part if acc is None else acc + part
        store(acc)

    @pl.when(jnp.logical_not(small))
    def _():
        def step(index, carried):
            most, acc = carried
            start = pl.multiple_of(index * block, block)
            scores = jnp.dot(
                k_ref[pl.ds(start, block), :], queries, preferred_element_type=F32
            )
            new_most = jnp.maximum(most, jnp.max(scores, axis=0, keepdims=True))
            weights = jnp.exp2(scores - new_most).astype(BF16)
            part = jnp.dot(
                v_ref[:, pl.ds(start, block)], weights, preferred_element_type=F32
            )
            return new_most, acc * jnp.exp2(most - new_most) + part

        start_state = (
            jnp.full((1, taken * rows), MASKED_SCORE, F32),
            jnp.zeros((depth + 16, taken * rows), F32),
        )
        store(lax.fori_loop(0, total // block, step, start_state)[1])


def attend_full(count, received):
    chips, features, rows = received.shape
    total = chips * rows
    taken = 2
    return pl.pallas_call(
        functools.partial(attention_kernel, block=512, taken=taken),
        out_shape=jax.ShapeDtypeStruct((2 * chips, HEAD_DIM, rows // 2), BF16),
        grid=(chips // taken,),
        in_specs=[
            pl.BlockSpec(memory_space=pltpu.SMEM),
            pl.BlockSpec(memory_space=pl.ANY),
        ],
        out_specs=pl.BlockSpec((2 * taken, HEAD_DIM, rows // 2), lambda i: (i, 0, 0)),
        scratch_shapes=[
            pltpu.VMEM(received.shape, BF16),
            pltpu.VMEM((total, 128), BF16),
            pltpu.VMEM((HEAD_DIM + 16, total), BF16),
            pltpu.SMEM((2,), F32),
            pltpu.SemaphoreType.DMA((chips,)),
        ],
        compiler_params=pltpu.CompilerParams(vmem_limit_bytes=VMEM_ALL),
    )(count, received)


def merge_kernel(bucket_ref, tag_ref, a_ref, x_ref, w_ref, gain_ref, out_ref):
    attended = a_ref[...]
    third = x_ref[...].astype(F32) + lax.dot_general(
        attended, w_ref[...], TN, preferred_element_type=F32
    )
    merged = normed(third, gain_ref[...]).astype(BF16)
    merged = jnp.concatenate([merged, tag_ref[...]], axis=1)
    places, patches = out_ref.shape[0], merged.shape[0]
    chosen = lax.broadcasted_iota(jnp.int32, (places, patches), 0) == bucket_ref[...]
    out_ref[...] = jnp.dot(
        chosen.astype(BF16), merged, preferred_element_type=F32
    ).astype(BF16)


def merge(bucket, tag, attended, second, w_out, gain, places):
    return pl.pallas_call(
        merge_kernel,
        out_shape=jax.ShapeDtypeStruct((places, D + TAG), BF16),
        in_specs=whole(6),
        out_specs=pl.BlockSpec(memory_space=pltpu.VMEM),
        compiler_params=pltpu.CompilerParams(vmem_limit_bytes=VMEM_LIMIT),
    )(bucket, tag, attended, second, w_out, gain)


def place_kernel(got_ref, out_ref):
    rows = out_ref.shape[0]
    places = got_ref.shape[0]
    tag = got_ref[:, D:].astype(F32).T[0:1].astype(jnp.int32)
    target = 4 * tag + lax.broadcasted_iota(jnp.int32, (1, places), 1) % 4
    index = lax.broadcasted_iota(jnp.int32, (4 * rows, 1), 0)
    wanted = 4 * (index % rows + 1) + index // rows
    chosen = (wanted == target).astype(BF16)
    found = jnp.dot(chosen, got_ref[:, :D], preferred_element_type=F32).astype(BF16)
    for n in range(4):
        out_ref[:, n * D : (n + 1) * D] = found[n * rows : (n + 1) * rows]


def place(got, rows):
    return pl.pallas_call(
        place_kernel,
        out_shape=jax.ShapeDtypeStruct((rows, 4 * D), BF16),
        in_specs=whole(1),
        out_specs=pl.BlockSpec(memory_space=pltpu.VMEM),
        compiler_params=pltpu.CompilerParams(vmem_limit_bytes=VMEM_LIMIT),
    )(got)


def routes_kernel(slots_ref, bucket_ref, tag_ref):
    rows = slots_ref.shape[1]
    slots = jnp.broadcast_to(slots_ref[...], (8, rows))
    owner = slots // rows
    sender = owner.T[:, 0:1]
    earlier = lax.broadcasted_iota(jnp.int32, (rows, rows), 0) < lax.broadcasted_iota(
        jnp.int32, (rows, rows), 1
    )
    rank = jnp.sum(((sender == owner[0:1]) & earlier).astype(jnp.int32), axis=0, keepdims=True)
    bucket = jnp.broadcast_to(4 * (2 * owner[0:1] + rank), (8, rows)).T[:, 0:1]
    lane = lax.broadcasted_iota(jnp.int32, (rows, 4 * rows), 1)
    mine = lane // 4 == lax.broadcasted_iota(jnp.int32, (rows, 4 * rows), 0)
    bucket_ref[...] = jnp.sum(jnp.where(mine, bucket + lane % 4, 0), axis=0, keepdims=True)
    place = (slots - owner * rows + 1).T[:, 0:1].astype(F32)
    patch = lax.broadcasted_iota(jnp.int32, (4 * rows, rows), 0) // 4
    spread = (patch == lax.broadcasted_iota(jnp.int32, (4 * rows, rows), 1)).astype(BF16)
    tag_ref[...] = jnp.dot(
        spread,
        jnp.broadcast_to(place, (rows, TAG)).astype(BF16),
        preferred_element_type=F32,
    ).astype(BF16)


def routes(slots):
    rows = slots.shape[0]
    return pl.pallas_call(
        routes_kernel,
        out_shape=[
            jax.ShapeDtypeStruct((1, 4 * rows), jnp.int32),
            jax.ShapeDtypeStruct((4 * rows, TAG), BF16),
        ],
        in_specs=whole(1),
        out_specs=whole(2),
        compiler_params=pltpu.CompilerParams(vmem_limit_bytes=VMEM_LIMIT),
        cost_estimate=pl.CostEstimate(flops=10**6, bytes_accessed=10**6, transcendentals=0),
    )(slots.reshape(1, rows))


def on_device(
    patches, window_ids, counts, gain_one, w_qkv1, w_out1, gain_two, w_qkv2, w_out2, gain_out, slots
):
    shard = jnp.swapaxes(w_qkv2, 1, 2).reshape(3 * HEAD_DIM, D)
    near = near_shards(shard)
    far, last = far_shards(near)

    second, hidden = layer_one(window_ids, patches, gain_one, gain_two, w_qkv1, w_out1)

    partner = lax.ppermute(hidden, BOTH, CORE_SWAP)
    projected = project(NEAR_OFFSETS, hidden, partner, near + far, (1, 1, 1, 1, 2))
    projected = project(FAR_OFFSETS, hidden, partner, last, (1, 1, 2), into=projected)
    groups = [[2 * chip + core for chip in range(8)] for core in range(2)]
    received = lax.all_to_all(
        projected, "img", split_axis=0, concat_axis=0, tiled=True, axis_index_groups=groups
    )
    slots, projected = lax.optimization_barrier((slots, projected))
    bucket_rows, tag = routes(slots)
    attended = attend_full(counts, received)
    attended = lax.all_to_all(attended, "img", split_axis=0, concat_axis=0, tiled=True)
    places = 128 * 2 * 4
    send = merge(bucket_rows, tag, attended.reshape(D, -1), second, w_out2, gain_out, places)
    got = lax.all_to_all(
        send.reshape(128, 8, D + TAG), BOTH, split_axis=0, concat_axis=0, tiled=True
    )
    return place(got.reshape(places, D + TAG), slots.shape[0])


def solution(mesh):
    return jax.shard_map(
        on_device,
        mesh=mesh,
        in_specs=(
            P("ctx", "img", None),
            P("ctx", "img"),
            P("ctx"),
            P(),
            P(),
            P(),
            P(),
            P(None, None, "img"),
            P(),
            P(),
            P(("ctx", "img")),
        ),
        out_specs=P(("ctx", "img"), None),
        check_vma=False,
    )
```

```python
import functools
import math

import jax
import jax.numpy as jnp
from jax import lax
from jax.experimental import pallas as pl
from jax.experimental.pallas import tpu as pltpu
from jax.sharding import PartitionSpec as P

HEAD_DIM = 80
D = 1280
EPSILON = 1e-06
MASKED_SCORE = -1e30
F32 = jnp.float32
BF16 = jnp.bfloat16
Q_SCALE = HEAD_DIM ** (-0.5) * math.log2(math.e)
WINDOW = 64
QUERY_BLOCK = 384
TAG = 128
SAFE_BOUND = 64.0
SAFE_VALUE = 2.0**40
VMEM_LIMIT = 56 * 1024 * 1024
VMEM_ALL = 63 * 1024 * 1024
NT = (((1,), (1,)), ((), ()))
TN = (((0,), (0,)), ((), ()))


def normed(values, gain):
    values = values.astype(F32)
    return (
        values
        * lax.rsqrt(jnp.mean(values * values, axis=-1, keepdims=True) + EPSILON)
        * gain.astype(F32).reshape(1, -1)
    )


def whole(count):
    return [pl.BlockSpec(memory_space=pltpu.VMEM)] * count


def layer_one_kernel(
    ids_ref, x_ref, gain_one_ref, gain_two_ref, w_qkv_ref, w_out_hbm,
    second_ref, hidden_ref, h_ref, q_ref, k_ref, a_ref, w_out_ref, sem,
):
    step = pl.program_id(0)
    copy = pltpu.make_async_copy(w_out_hbm, w_out_ref, sem)

    @pl.when(step == 0)
    def _():
        h_ref[...] = normed(x_ref[0], gain_one_ref[...]).astype(BF16)

    def project_one(scale=None):
        product = jnp.dot(h_ref[...], w_qkv_ref[0], preferred_element_type=F32)
        return (product if scale is None else product * scale).astype(BF16)

    @pl.when(step == 0)
    def _():
        q_ref[...] = project_one(Q_SCALE)

    @pl.when(step == 1)
    def _():
        copy.start()
        k_ref[...] = project_one()

    @pl.when(step == 2)
    def _():
        values_all = project_one()
        rows = ids_ref.shape[1]
        ids = jnp.broadcast_to(ids_ref[...], (8, rows))
        ids_column = ids.T[:, 0:1]
        spans = []
        for start in range(0, rows, QUERY_BLOCK):
            begin = max(start - WINDOW, 0)
            end = min(start + QUERY_BLOCK + WINDOW, rows)
            allowed = ids_column[start : start + QUERY_BLOCK] == ids[0:1, begin:end]
            spans.append((start, begin, end, allowed))
        tiles = {}
        allowed = spans[0][3]

        def window(head):
            first, last = head * HEAD_DIM, (head + 1) * HEAD_DIM
            low, high = first // 128 * 128, (last + 127) // 128 * 128
            lane = low + lax.broadcasted_iota(jnp.int32, (1, high - low), 1)
            return low, high, last, (lane >= first) & (lane < last)

        def score(head):
            low, high, last, mine = window(head)
            keys = jnp.where(mine, k_ref[:, low:high], 0.0).astype(BF16)
            return lax.dot_general(q_ref[:, low:high], keys, NT, preferred_element_type=F32)

        heads = D // HEAD_DIM
        ahead = score(0)
        for head in range(heads):
            scores = jnp.where(allowed, ahead, MASKED_SCORE)
            if head + 1 < heads:
                ahead = score(head + 1)
            low, high, last, mine = window(head)
            most = jnp.max(scores, axis=1, keepdims=True)
            weights = jnp.exp2(scores - most)
            total = jnp.sum(weights, axis=1, keepdims=True)
            result = jnp.dot(
                weights.astype(BF16), values_all[:, low:high], preferred_element_type=F32
            ) * (1.0 / total)
            for tile in range(low, high, 128):
                piece = result[:, tile - low : tile - low + 128]
                if tile in tiles:
                    piece = jnp.where(mine[:, tile - low : tile - low + 128], piece, tiles[tile])
                tiles[tile] = piece
                if tile + 128 <= last:
                    a_ref[:, tile : tile + 128] = tiles.pop(tile).astype(BF16)
        copy.wait()
        second = x_ref[0].astype(F32) + jnp.dot(
            a_ref[...], w_out_ref[...], preferred_element_type=F32
        )
        second = second.astype(BF16)
        second_ref[...] = second
        hidden_ref[...] = normed(second, gain_two_ref[...]).astype(BF16)


def layer_one(ids, patches, gain_one, gain_two, w_qkv, w_out):
    rows = patches.shape[1]
    fixed = lambda *shape: pl.BlockSpec(shape, lambda i: (0,) * len(shape))
    return pl.pallas_call(
        layer_one_kernel,
        out_shape=[jax.ShapeDtypeStruct((rows, D), BF16)] * 2,
        grid=(3,),
        in_specs=[
            fixed(1, rows),
            fixed(1, rows, D),
            fixed(D),
            fixed(D),
            pl.BlockSpec((1, D, D), lambda i: (i, 0, 0)),
            pl.BlockSpec(memory_space=pl.ANY),
        ],
        out_specs=[fixed(rows, D)] * 2,
        scratch_shapes=[pltpu.VMEM((rows, D), BF16)] * 4
        + [pltpu.VMEM((D, D), BF16), pltpu.SemaphoreType.DMA],
        compiler_params=pltpu.CompilerParams(vmem_limit_bytes=VMEM_LIMIT),
        cost_estimate=pl.CostEstimate(
            flops=6 * 10**9, bytes_accessed=16 * 10**6, transcendentals=3 * 10**6
        ),
    )(
        ids, patches, gain_one, gain_two, w_qkv, w_out
    )


def device_perm(move):
    pairs = []
    for i in range(128):
        c, g = divmod(i, 16)
        x_lo, y = divmod(c, 4)
        x_hi, r = divmod(g, 8)
        z, core = divmod(r, 2)
        x2, y2, z2, core2 = move(x_hi * 2 + x_lo, y, z, core)
        x2, y2, z2 = x2 % 4, y2 % 4, z2 % 4
        pairs.append((i, ((x2 % 2) * 4 + y2) * 16 + ((x2 // 2) * 4 + z2) * 2 + core2))
    return pairs


OTHER_X = {0: 3, 3: 0, 1: 2, 2: 1}
Z_UP = device_perm(lambda x, y, z, core: (x, y, z + 1, core))
Z_DOWN = device_perm(lambda x, y, z, core: (x, y, z - 1, core))
X_OTHER = device_perm(lambda x, y, z, core: (OTHER_X[x], y, z, core))
CORE_SWAP = device_perm(lambda x, y, z, core: (x, y, z, 1 - core))
BOTH = ("ctx", "img")
NEAR_OFFSETS = ((0, 0), (0, -1), (0, 1), (1, 0), (0, 2))
FAR_OFFSETS = ((1, -1), (1, 1), (1, 2))


def near_shards(shard):
    below = lax.ppermute(shard, BOTH, Z_UP)
    above = lax.ppermute(shard, BOTH, Z_DOWN)
    other = lax.ppermute(shard, BOTH, X_OTHER)
    return [shard, below, above, other]


def far_shards(near):
    shard, below, above, other = near
    half = 128
    far_top = lax.ppermute(below[:half], BOTH, Z_UP)
    far_bottom = lax.ppermute(above[half:], BOTH, Z_DOWN)
    far_top, other_up = lax.optimization_barrier((far_top, other))
    far_bottom, other_down = lax.optimization_barrier((far_bottom, other))
    other_far_top = lax.ppermute(far_top, BOTH, X_OTHER)
    other_below = lax.ppermute(other_up, BOTH, Z_UP)
    other_far_bottom = lax.ppermute(far_bottom, BOTH, X_OTHER)
    other_above = lax.ppermute(other_down, BOTH, Z_DOWN)
    return [far_top, far_bottom], [other_below, other_above, other_far_top, other_far_bottom]


def project_kernel(h_own_ref, h_partner_ref, *refs, parts, offsets, aliased):
    count = sum(parts)
    me = lax.axis_index("img")
    my_x, my_z, core = me // 8, me // 2 % 4, me % 2
    weights_refs = refs[:count]
    out_hbm, w_ref, h_ref, done_ref, sem, in_sem = refs[count + aliased :]
    rows = h_own_ref.shape[0]
    wide = 3 * HEAD_DIM
    loads = []
    at = 0
    for n, weights_ref in enumerate(weights_refs):
        end = at + weights_ref.shape[0]
        load = pltpu.make_async_copy(weights_ref, w_ref.at[at:end], in_sem.at[n])
        load.start()
        loads.append(load)
        at = end
    for n, (side, ref) in enumerate(((core, h_own_ref), (1 - core, h_partner_ref))):
        load = pltpu.make_async_copy(
            ref, h_ref.at[pl.ds(pl.multiple_of(side * rows, 16), rows)], in_sem.at[count + n]
        )
        load.start()
        loads.append(load)
    part = lax.broadcasted_iota(jnp.int32, (len(parts) * wide, 1), 0) % wide
    scale = jnp.where(part < HEAD_DIM, Q_SCALE, 1.0).astype(F32)
    for load in loads:
        load.wait()
    product = lax.dot_general(w_ref[...], h_ref[...], NT, preferred_element_type=F32)
    product = (product * scale).astype(BF16)
    copies = []
    for n in range(len(parts)):
        done_ref[n] = product[n * wide : (n + 1) * wide]
        target = (my_x + offsets[n][0]) % 2 * 4 + (my_z + offsets[n][1] + 4) % 4
        copy = pltpu.make_async_copy(done_ref.at[n], out_hbm.at[target], sem.at[n])
        copy.start()
        copies.append(copy)
    for copy in copies:
        copy.wait()


def project(offsets, h_own, h_partner, shards, parts, into=None):
    rows = h_own.shape[0]
    wide = 3 * HEAD_DIM
    aliased = 0 if into is None else 1
    return pl.pallas_call(
        functools.partial(
            project_kernel, parts=parts, offsets=offsets, aliased=aliased
        ),
        out_shape=jax.ShapeDtypeStruct((8, wide, 2 * rows), BF16),
        in_specs=[pl.BlockSpec(memory_space=pl.ANY)] * (2 + len(shards) + aliased),
        out_specs=pl.BlockSpec(memory_space=pl.ANY),
        scratch_shapes=[
            pltpu.VMEM((len(parts) * wide, D), BF16),
            pltpu.VMEM((2 * rows, D), BF16),
            pltpu.VMEM((len(parts), wide, 2 * rows), BF16),
            pltpu.SemaphoreType.DMA((len(parts),)),
            pltpu.SemaphoreType.DMA((len(shards) + 2,)),
        ],
        input_output_aliases={2 + len(shards): 0} if aliased else {},
        compiler_params=pltpu.CompilerParams(vmem_limit_bytes=VMEM_ALL),
        cost_estimate=pl.CostEstimate(
            flops=2 * 10**9, bytes_accessed=6 * 10**6, transcendentals=0
        ),
    )(h_own, h_partner, *shards, *([into] if aliased else []))


def attention_kernel(
    count_ref, all_hbm, out_ref, all_ref, k_ref, v_ref, bound_ref, sem, *, block, taken
):
    chips, features, rows = all_ref.shape
    total = chips * rows
    depth = HEAD_DIM

    @pl.when(pl.program_id(0) == 0)
    def _():
        copies = [
            pltpu.make_async_copy(all_hbm.at[chip], all_ref.at[chip], sem.at[chip])
            for chip in range(chips)
        ]
        for copy in copies:
            copy.start()
        count = count_ref[0]
        copies[0].wait()
        key_zero = all_ref[0, depth : 2 * depth, 0:1].astype(F32)
        q_most = jnp.zeros((1, rows), F32)
        k_most = jnp.zeros((1, rows), F32)
        v_most = jnp.zeros((HEAD_DIM, rows), F32)
        for chip in range(chips):
            if chip:
                copies[chip].wait()
            position = chip * rows + lax.broadcasted_iota(jnp.int32, (1, rows), 1)
            valid = position < count
            keys = jnp.where(valid, all_ref[chip, depth : 2 * depth, :].astype(F32), key_zero)
            values = jnp.where(valid, all_ref[chip, 2 * depth :, :].astype(F32), 0.0)
            queries = all_ref[chip, 0:depth, :].astype(F32)
            q_most = jnp.maximum(q_most, jnp.sum(queries * queries, axis=0, keepdims=True))
            k_most = jnp.maximum(k_most, jnp.sum(keys * keys, axis=0, keepdims=True))
            v_most = jnp.maximum(v_most, jnp.abs(values))
            keys = jnp.concatenate([keys, jnp.zeros((128 - depth, rows), F32)], axis=0)
            k_ref[chip * rows : (chip + 1) * rows, :] = keys.astype(BF16).T
            v_ref[0:depth, chip * rows : (chip + 1) * rows] = values.astype(BF16)
            v_ref[depth:, chip * rows : (chip + 1) * rows] = jnp.where(
                (lax.broadcasted_iota(jnp.int32, (16, rows), 0) == 0) & valid, 1.0, 0.0
            ).astype(BF16)
        bound_ref[0] = jnp.max(q_most) * jnp.max(k_most)
        bound_ref[1] = jnp.max(v_most)

    first = taken * pl.program_id(0)
    queries = jnp.concatenate([all_ref[first + n, 0:depth, :] for n in range(taken)], axis=1)
    queries = jnp.concatenate([queries, jnp.zeros((128 - depth, taken * rows), BF16)], axis=0)
    small = (bound_ref[0] < SAFE_BOUND * SAFE_BOUND) & (bound_ref[1] < SAFE_VALUE)

    def store(acc):
        result = acc[0:depth] / acc[depth : depth + 1]
        half = rows // 2
        for n in range(2 * taken):
            out_ref[n] = result[:, n * half : (n + 1) * half].astype(BF16)

    @pl.when(small)
    def _():
        acc = None
        for start in range(0, total, block):
            scores = jnp.dot(k_ref[start : start + block, :], queries, preferred_element_type=F32)
            weights = jnp.exp2(scores).astype(BF16)
            part = jnp.dot(v_ref[:, start : start + block], weights, preferred_element_type=F32)
            acc = part if acc is None else acc + part
        store(acc)

    @pl.when(jnp.logical_not(small))
    def _():
        def step(index, carried):
            most, acc = carried
            start = pl.multiple_of(index * block, block)
            scores = jnp.dot(
                k_ref[pl.ds(start, block), :], queries, preferred_element_type=F32
            )
            new_most = jnp.maximum(most, jnp.max(scores, axis=0, keepdims=True))
            weights = jnp.exp2(scores - new_most).astype(BF16)
            part = jnp.dot(
                v_ref[:, pl.ds(start, block)], weights, preferred_element_type=F32
            )
            return new_most, acc * jnp.exp2(most - new_most) + part

        start_state = (
            jnp.full((1, taken * rows), MASKED_SCORE, F32),
            jnp.zeros((depth + 16, taken * rows), F32),
        )
        store(lax.fori_loop(0, total // block, step, start_state)[1])


def attend_full(count, received):
    chips, features, rows = received.shape
    total = chips * rows
    taken = 2
    return pl.pallas_call(
        functools.partial(attention_kernel, block=512, taken=taken),
        out_shape=jax.ShapeDtypeStruct((2 * chips, HEAD_DIM, rows // 2), BF16),
        grid=(chips // taken,),
        in_specs=[
            pl.BlockSpec(memory_space=pltpu.SMEM),
            pl.BlockSpec(memory_space=pl.ANY),
        ],
        out_specs=pl.BlockSpec((2 * taken, HEAD_DIM, rows // 2), lambda i: (i, 0, 0)),
        scratch_shapes=[
            pltpu.VMEM(received.shape, BF16),
            pltpu.VMEM((total, 128), BF16),
            pltpu.VMEM((HEAD_DIM + 16, total), BF16),
            pltpu.SMEM((2,), F32),
            pltpu.SemaphoreType.DMA((chips,)),
        ],
        compiler_params=pltpu.CompilerParams(vmem_limit_bytes=VMEM_ALL),
    )(count, received)


def merge_kernel(bucket_ref, tag_ref, a_ref, x_ref, w_ref, gain_ref, out_ref):
    attended = a_ref[...]
    third = x_ref[...].astype(F32) + lax.dot_general(
        attended, w_ref[...], TN, preferred_element_type=F32
    )
    merged = normed(third, gain_ref[...]).astype(BF16)
    merged = jnp.concatenate([merged, tag_ref[...]], axis=1)
    places, patches = out_ref.shape[0], merged.shape[0]
    chosen = lax.broadcasted_iota(jnp.int32, (places, patches), 0) == bucket_ref[...]
    out_ref[...] = jnp.dot(
        chosen.astype(BF16), merged, preferred_element_type=F32
    ).astype(BF16)


def merge(bucket, tag, attended, second, w_out, gain, places):
    return pl.pallas_call(
        merge_kernel,
        out_shape=jax.ShapeDtypeStruct((places, D + TAG), BF16),
        in_specs=whole(6),
        out_specs=pl.BlockSpec(memory_space=pltpu.VMEM),
        compiler_params=pltpu.CompilerParams(vmem_limit_bytes=VMEM_LIMIT),
    )(bucket, tag, attended, second, w_out, gain)


def place_kernel(got_ref, out_ref):
    rows = out_ref.shape[0]
    places = got_ref.shape[0]
    tag = got_ref[:, D:].astype(F32).T[0:1].astype(jnp.int32)
    target = 4 * tag + lax.broadcasted_iota(jnp.int32, (1, places), 1) % 4
    index = lax.broadcasted_iota(jnp.int32, (4 * rows, 1), 0)
    wanted = 4 * (index % rows + 1) + index // rows
    chosen = (wanted == target).astype(BF16)
    found = jnp.dot(chosen, got_ref[:, :D], preferred_element_type=F32).astype(BF16)
    for n in range(4):
        out_ref[:, n * D : (n + 1) * D] = found[n * rows : (n + 1) * rows]


def place(got, rows):
    return pl.pallas_call(
        place_kernel,
        out_shape=jax.ShapeDtypeStruct((rows, 4 * D), BF16),
        in_specs=whole(1),
        out_specs=pl.BlockSpec(memory_space=pltpu.VMEM),
        compiler_params=pltpu.CompilerParams(vmem_limit_bytes=VMEM_LIMIT),
    )(got)


def routes_kernel(slots_ref, bucket_ref, tag_ref):
    rows = slots_ref.shape[1]
    slots = jnp.broadcast_to(slots_ref[...], (8, rows))
    owner = slots // rows
    sender = owner.T[:, 0:1]
    earlier = lax.broadcasted_iota(jnp.int32, (rows, rows), 0) < lax.broadcasted_iota(
        jnp.int32, (rows, rows), 1
    )
    rank = jnp.sum(((sender == owner[0:1]) & earlier).astype(jnp.int32), axis=0, keepdims=True)
    bucket = jnp.broadcast_to(4 * (2 * owner[0:1] + rank), (8, rows)).T[:, 0:1]
    lane = lax.broadcasted_iota(jnp.int32, (rows, 4 * rows), 1)
    mine = lane // 4 == lax.broadcasted_iota(jnp.int32, (rows, 4 * rows), 0)
    bucket_ref[...] = jnp.sum(jnp.where(mine, bucket + lane % 4, 0), axis=0, keepdims=True)
    place = (slots - owner * rows + 1).T[:, 0:1].astype(F32)
    patch = lax.broadcasted_iota(jnp.int32, (4 * rows, rows), 0) // 4
    spread = (patch == lax.broadcasted_iota(jnp.int32, (4 * rows, rows), 1)).astype(BF16)
    tag_ref[...] = jnp.dot(
        spread,
        jnp.broadcast_to(place, (rows, TAG)).astype(BF16),
        preferred_element_type=F32,
    ).astype(BF16)


def routes(slots):
    rows = slots.shape[0]
    return pl.pallas_call(
        routes_kernel,
        out_shape=[
            jax.ShapeDtypeStruct((1, 4 * rows), jnp.int32),
            jax.ShapeDtypeStruct((4 * rows, TAG), BF16),
        ],
        in_specs=whole(1),
        out_specs=whole(2),
        compiler_params=pltpu.CompilerParams(vmem_limit_bytes=VMEM_LIMIT),
        cost_estimate=pl.CostEstimate(flops=10**6, bytes_accessed=10**6, transcendentals=0),
    )(slots.reshape(1, rows))


def on_device(
    patches, window_ids, counts, gain_one, w_qkv1, w_out1, gain_two, w_qkv2, w_out2, gain_out, slots
):
    shard = jnp.swapaxes(w_qkv2, 1, 2).reshape(3 * HEAD_DIM, D)
    near = near_shards(shard)
    far, last = far_shards(near)

    second, hidden = layer_one(window_ids, patches, gain_one, gain_two, w_qkv1, w_out1)

    partner = lax.ppermute(hidden, BOTH, CORE_SWAP)
    projected = project(NEAR_OFFSETS, hidden, partner, near + far, (1, 1, 1, 1, 2))
    projected = project(FAR_OFFSETS, hidden, partner, last, (1, 1, 2), into=projected)
    groups = [[2 * chip + core for chip in range(8)] for core in range(2)]
    received = lax.all_to_all(
        projected, "img", split_axis=0, concat_axis=0, tiled=True, axis_index_groups=groups
    )
    slots, projected = lax.optimization_barrier((slots, projected))
    bucket_rows, tag = routes(slots)
    attended = attend_full(counts, received)
    attended = lax.all_to_all(attended, "img", split_axis=0, concat_axis=0, tiled=True)
    places = 128 * 2 * 4
    send = merge(bucket_rows, tag, attended.reshape(D, -1), second, w_out2, gain_out, places)
    got = lax.all_to_all(
        send.reshape(128, 8, D + TAG), BOTH, split_axis=0, concat_axis=0, tiled=True
    )
    return place(got.reshape(places, D + TAG), slots.shape[0])


def solution(mesh):
    return jax.shard_map(
        on_device,
        mesh=mesh,
        in_specs=(
            P("ctx", "img", None),
            P("ctx", "img"),
            P("ctx"),
            P(),
            P(),
            P(),
            P(),
            P(None, None, "img"),
            P(),
            P(),
            P(("ctx", "img")),
        ),
        out_specs=P(("ctx", "img"), None),
        check_vma=False,
    )
```

```python
import functools
import math

import jax
import jax.numpy as jnp
from jax import lax
from jax.experimental import pallas as pl
from jax.experimental.pallas import tpu as pltpu
from jax.sharding import PartitionSpec as P

HEAD_DIM = 80
D = 1280
EPSILON = 1e-06
MASKED_SCORE = -1e30
F32 = jnp.float32
BF16 = jnp.bfloat16
Q_SCALE = HEAD_DIM ** (-0.5) * math.log2(math.e)
WINDOW = 64
QUERY_BLOCK = 384
TAG = 128
SAFE_BOUND = 64.0
SAFE_VALUE = 2.0**40
VMEM_LIMIT = 56 * 1024 * 1024
VMEM_ALL = 63 * 1024 * 1024
NT = (((1,), (1,)), ((), ()))
TN = (((0,), (0,)), ((), ()))


def normed(values, gain):
    values = values.astype(F32)
    return (
        values
        * lax.rsqrt(jnp.mean(values * values, axis=-1, keepdims=True) + EPSILON)
        * gain.astype(F32).reshape(1, -1)
    )


def whole(count):
    return [pl.BlockSpec(memory_space=pltpu.VMEM)] * count


def layer_one_kernel(
    ids_ref, x_ref, gain_one_ref, gain_two_ref, w_qkv_ref, w_out_hbm,
    second_ref, hidden_ref, h_ref, q_ref, k_ref, a_ref, w_out_ref, sem,
):
    step = pl.program_id(0)
    copy = pltpu.make_async_copy(w_out_hbm, w_out_ref, sem)

    @pl.when(step == 0)
    def _():
        h_ref[...] = normed(x_ref[0], gain_one_ref[...]).astype(BF16)

    def project_one(scale=None):
        product = jnp.dot(h_ref[...], w_qkv_ref[0], preferred_element_type=F32)
        return (product if scale is None else product * scale).astype(BF16)

    @pl.when(step == 0)
    def _():
        q_ref[...] = project_one(Q_SCALE)

    @pl.when(step == 1)
    def _():
        copy.start()
        k_ref[...] = project_one()

    @pl.when(step == 2)
    def _():
        values_all = project_one()
        rows = ids_ref.shape[1]
        ids = jnp.broadcast_to(ids_ref[...], (8, rows))
        ids_column = ids.T[:, 0:1]
        spans = []
        for start in range(0, rows, QUERY_BLOCK):
            begin = max(start - WINDOW, 0)
            end = min(start + QUERY_BLOCK + WINDOW, rows)
            allowed = ids_column[start : start + QUERY_BLOCK] == ids[0:1, begin:end]
            spans.append((start, begin, end, allowed))
        tiles = {}
        allowed = spans[0][3]

        def window(head):
            first, last = head * HEAD_DIM, (head + 1) * HEAD_DIM
            low, high = first // 128 * 128, (last + 127) // 128 * 128
            lane = low + lax.broadcasted_iota(jnp.int32, (1, high - low), 1)
            return low, high, last, (lane >= first) & (lane < last)

        def score(head):
            low, high, last, mine = window(head)
            keys = jnp.where(mine, k_ref[:, low:high], 0.0).astype(BF16)
            return lax.dot_general(q_ref[:, low:high], keys, NT, preferred_element_type=F32)

        heads = D // HEAD_DIM
        ahead = score(0)
        for head in range(heads):
            scores = jnp.where(allowed, ahead, MASKED_SCORE)
            if head + 1 < heads:
                ahead = score(head + 1)
            low, high, last, mine = window(head)
            most = jnp.max(scores, axis=1, keepdims=True)
            weights = jnp.exp2(scores - most)
            total = jnp.sum(weights, axis=1, keepdims=True)
            result = jnp.dot(
                weights.astype(BF16), values_all[:, low:high], preferred_element_type=F32
            ) * (1.0 / total)
            for tile in range(low, high, 128):
                piece = result[:, tile - low : tile - low + 128]
                if tile in tiles:
                    piece = jnp.where(mine[:, tile - low : tile - low + 128], piece, tiles[tile])
                tiles[tile] = piece
                if tile + 128 <= last:
                    a_ref[:, tile : tile + 128] = tiles.pop(tile).astype(BF16)
        copy.wait()
        second = x_ref[0].astype(F32) + jnp.dot(
            a_ref[...], w_out_ref[...], preferred_element_type=F32
        )
        second = second.astype(BF16)
        second_ref[...] = second
        hidden_ref[...] = normed(second, gain_two_ref[...]).astype(BF16)


def layer_one(ids, patches, gain_one, gain_two, w_qkv, w_out):
    rows = patches.shape[1]
    fixed = lambda *shape: pl.BlockSpec(shape, lambda i: (0,) * len(shape))
    return pl.pallas_call(
        layer_one_kernel,
        out_shape=[jax.ShapeDtypeStruct((rows, D), BF16)] * 2,
        grid=(3,),
        in_specs=[
            fixed(1, rows),
            fixed(1, rows, D),
            fixed(D),
            fixed(D),
            pl.BlockSpec((1, D, D), lambda i: (i, 0, 0)),
            pl.BlockSpec(memory_space=pl.ANY),
        ],
        out_specs=[fixed(rows, D)] * 2,
        scratch_shapes=[pltpu.VMEM((rows, D), BF16)] * 4
        + [pltpu.VMEM((D, D), BF16), pltpu.SemaphoreType.DMA],
        compiler_params=pltpu.CompilerParams(vmem_limit_bytes=VMEM_LIMIT),
        cost_estimate=pl.CostEstimate(
            flops=6 * 10**9, bytes_accessed=16 * 10**6, transcendentals=3 * 10**6
        ),
    )(
        ids, patches, gain_one, gain_two, w_qkv, w_out
    )


def device_perm(move):
    pairs = []
    for i in range(128):
        c, g = divmod(i, 16)
        x_lo, y = divmod(c, 4)
        x_hi, r = divmod(g, 8)
        z, core = divmod(r, 2)
        x2, y2, z2, core2 = move(x_hi * 2 + x_lo, y, z, core)
        x2, y2, z2 = x2 % 4, y2 % 4, z2 % 4
        pairs.append((i, ((x2 % 2) * 4 + y2) * 16 + ((x2 // 2) * 4 + z2) * 2 + core2))
    return pairs


OTHER_X = {0: 3, 3: 0, 1: 2, 2: 1}
Z_UP = device_perm(lambda x, y, z, core: (x, y, z + 1, core))
Z_DOWN = device_perm(lambda x, y, z, core: (x, y, z - 1, core))
X_OTHER = device_perm(lambda x, y, z, core: (OTHER_X[x], y, z, core))
CORE_SWAP = device_perm(lambda x, y, z, core: (x, y, z, 1 - core))
BOTH = ("ctx", "img")
NEAR_OFFSETS = ((0, 0), (0, -1), (0, 1), (1, 0), (0, 2))
FAR_OFFSETS = ((1, -1), (1, 1), (1, 2))


def near_shards(shard):
    below = lax.ppermute(shard, BOTH, Z_UP)
    above = lax.ppermute(shard, BOTH, Z_DOWN)
    other = lax.ppermute(shard, BOTH, X_OTHER)
    return [shard, below, above, other]


def far_shards(near, partner):
    shard, below, above, other = near
    half = 128
    far_top = lax.ppermute(below[:half], BOTH, Z_UP)
    far_bottom = lax.ppermute(above[half:], BOTH, Z_DOWN)
    other_far_top = lax.ppermute(far_top, BOTH, X_OTHER)
    other_far_bottom = lax.ppermute(far_bottom, BOTH, X_OTHER)
    far_top, other_up, partner = lax.optimization_barrier((far_top, other, partner))
    far_bottom, other_down, partner = lax.optimization_barrier((far_bottom, other, partner))
    other_below = lax.ppermute(other_up, BOTH, Z_UP)
    other_above = lax.ppermute(other_down, BOTH, Z_DOWN)
    last = [other_below, other_above, other_far_top, other_far_bottom]
    return [far_top, far_bottom], last, partner


def project_kernel(h_own_ref, h_partner_ref, *refs, parts, offsets, aliased):
    count = sum(parts)
    me = lax.axis_index("img")
    my_x, my_z, core = me // 8, me // 2 % 4, me % 2
    weights_refs = refs[:count]
    out_hbm, w_ref, h_ref, done_ref, sem, in_sem = refs[count + aliased :]
    rows = h_own_ref.shape[0]
    wide = 3 * HEAD_DIM
    loads = []
    at = 0
    for n, weights_ref in enumerate(weights_refs):
        end = at + weights_ref.shape[0]
        load = pltpu.make_async_copy(weights_ref, w_ref.at[at:end], in_sem.at[n])
        load.start()
        loads.append(load)
        at = end
    for n, (side, ref) in enumerate(((core, h_own_ref), (1 - core, h_partner_ref))):
        load = pltpu.make_async_copy(
            ref, h_ref.at[pl.ds(pl.multiple_of(side * rows, 16), rows)], in_sem.at[count + n]
        )
        load.start()
        loads.append(load)
    part = lax.broadcasted_iota(jnp.int32, (len(parts) * wide, 1), 0) % wide
    scale = jnp.where(part < HEAD_DIM, Q_SCALE, 1.0).astype(F32)
    for load in loads:
        load.wait()
    product = lax.dot_general(w_ref[...], h_ref[...], NT, preferred_element_type=F32)
    product = (product * scale).astype(BF16)
    copies = []
    for n in range(len(parts)):
        done_ref[n] = product[n * wide : (n + 1) * wide]
        target = (my_x + offsets[n][0]) % 2 * 4 + (my_z + offsets[n][1] + 4) % 4
        copy = pltpu.make_async_copy(done_ref.at[n], out_hbm.at[target], sem.at[n])
        copy.start()
        copies.append(copy)
    for copy in copies:
        copy.wait()


def project(offsets, h_own, h_partner, shards, parts, into=None):
    rows = h_own.shape[0]
    wide = 3 * HEAD_DIM
    aliased = 0 if into is None else 1
    return pl.pallas_call(
        functools.partial(
            project_kernel, parts=parts, offsets=offsets, aliased=aliased
        ),
        out_shape=jax.ShapeDtypeStruct((8, wide, 2 * rows), BF16),
        in_specs=[pl.BlockSpec(memory_space=pl.ANY)] * (2 + len(shards) + aliased),
        out_specs=pl.BlockSpec(memory_space=pl.ANY),
        scratch_shapes=[
            pltpu.VMEM((len(parts) * wide, D), BF16),
            pltpu.VMEM((2 * rows, D), BF16),
            pltpu.VMEM((len(parts), wide, 2 * rows), BF16),
            pltpu.SemaphoreType.DMA((len(parts),)),
            pltpu.SemaphoreType.DMA((len(shards) + 2,)),
        ],
        input_output_aliases={2 + len(shards): 0} if aliased else {},
        compiler_params=pltpu.CompilerParams(vmem_limit_bytes=VMEM_ALL),
        cost_estimate=pl.CostEstimate(
            flops=2 * 10**9, bytes_accessed=6 * 10**6, transcendentals=0
        ),
    )(h_own, h_partner, *shards, *([into] if aliased else []))


def attention_kernel(
    count_ref, all_hbm, out_ref, all_ref, k_ref, v_ref, bound_ref, sem, *, block, taken
):
    chips, features, rows = all_ref.shape
    total = chips * rows
    depth = HEAD_DIM

    @pl.when(pl.program_id(0) == 0)
    def _():
        copies = [
            pltpu.make_async_copy(all_hbm.at[chip], all_ref.at[chip], sem.at[chip])
            for chip in range(chips)
        ]
        for copy in copies:
            copy.start()
        count = count_ref[0]
        copies[0].wait()
        key_zero = all_ref[0, depth : 2 * depth, 0:1].astype(F32)
        q_most = jnp.zeros((1, rows), F32)
        k_most = jnp.zeros((1, rows), F32)
        v_most = jnp.zeros((HEAD_DIM, rows), F32)
        for chip in range(chips):
            if chip:
                copies[chip].wait()
            position = chip * rows + lax.broadcasted_iota(jnp.int32, (1, rows), 1)
            valid = position < count
            keys = jnp.where(valid, all_ref[chip, depth : 2 * depth, :].astype(F32), key_zero)
            values = jnp.where(valid, all_ref[chip, 2 * depth :, :].astype(F32), 0.0)
            queries = all_ref[chip, 0:depth, :].astype(F32)
            q_most = jnp.maximum(q_most, jnp.sum(queries * queries, axis=0, keepdims=True))
            k_most = jnp.maximum(k_most, jnp.sum(keys * keys, axis=0, keepdims=True))
            v_most = jnp.maximum(v_most, jnp.abs(values))
            keys = jnp.concatenate([keys, jnp.zeros((128 - depth, rows), F32)], axis=0)
            k_ref[chip * rows : (chip + 1) * rows, :] = keys.astype(BF16).T
            v_ref[0:depth, chip * rows : (chip + 1) * rows] = values.astype(BF16)
            v_ref[depth:, chip * rows : (chip + 1) * rows] = jnp.where(
                (lax.broadcasted_iota(jnp.int32, (16, rows), 0) == 0) & valid, 1.0, 0.0
            ).astype(BF16)
        bound_ref[0] = jnp.max(q_most) * jnp.max(k_most)
        bound_ref[1] = jnp.max(v_most)

    first = taken * pl.program_id(0)
    queries = jnp.concatenate([all_ref[first + n, 0:depth, :] for n in range(taken)], axis=1)
    queries = jnp.concatenate([queries, jnp.zeros((128 - depth, taken * rows), BF16)], axis=0)
    small = (bound_ref[0] < SAFE_BOUND * SAFE_BOUND) & (bound_ref[1] < SAFE_VALUE)

    def store(acc):
        result = acc[0:depth] / acc[depth : depth + 1]
        half = rows // 2
        for n in range(2 * taken):
            out_ref[n] = result[:, n * half : (n + 1) * half].astype(BF16)

    @pl.when(small)
    def _():
        acc = None
        for start in range(0, total, block):
            scores = jnp.dot(k_ref[start : start + block, :], queries, preferred_element_type=F32)
            weights = jnp.exp2(scores).astype(BF16)
            part = jnp.dot(v_ref[:, start : start + block], weights, preferred_element_type=F32)
            acc = part if acc is None else acc + part
        store(acc)

    @pl.when(jnp.logical_not(small))
    def _():
        def step(index, carried):
            most, acc = carried
            start = pl.multiple_of(index * block, block)
            scores = jnp.dot(
                k_ref[pl.ds(start, block), :], queries, preferred_element_type=F32
            )
            new_most = jnp.maximum(most, jnp.max(scores, axis=0, keepdims=True))
            weights = jnp.exp2(scores - new_most).astype(BF16)
            part = jnp.dot(
                v_ref[:, pl.ds(start, block)], weights, preferred_element_type=F32
            )
            return new_most, acc * jnp.exp2(most - new_most) + part

        start_state = (
            jnp.full((1, taken * rows), MASKED_SCORE, F32),
            jnp.zeros((depth + 16, taken * rows), F32),
        )
        store(lax.fori_loop(0, total // block, step, start_state)[1])


def attend_full(count, received):
    chips, features, rows = received.shape
    total = chips * rows
    taken = 2
    return pl.pallas_call(
        functools.partial(attention_kernel, block=512, taken=taken),
        out_shape=jax.ShapeDtypeStruct((2 * chips, HEAD_DIM, rows // 2), BF16),
        grid=(chips // taken,),
        in_specs=[
            pl.BlockSpec(memory_space=pltpu.SMEM),
            pl.BlockSpec(memory_space=pl.ANY),
        ],
        out_specs=pl.BlockSpec((2 * taken, HEAD_DIM, rows // 2), lambda i: (i, 0, 0)),
        scratch_shapes=[
            pltpu.VMEM(received.shape, BF16),
            pltpu.VMEM((total, 128), BF16),
            pltpu.VMEM((HEAD_DIM + 16, total), BF16),
            pltpu.SMEM((2,), F32),
            pltpu.SemaphoreType.DMA((chips,)),
        ],
        compiler_params=pltpu.CompilerParams(vmem_limit_bytes=VMEM_ALL),
    )(count, received)


def merge_kernel(bucket_ref, tag_ref, a_ref, x_ref, w_ref, gain_ref, out_ref):
    attended = a_ref[...]
    third = x_ref[...].astype(F32) + lax.dot_general(
        attended, w_ref[...], TN, preferred_element_type=F32
    )
    merged = normed(third, gain_ref[...]).astype(BF16)
    merged = jnp.concatenate([merged, tag_ref[...]], axis=1)
    places, patches = out_ref.shape[0], merged.shape[0]
    chosen = lax.broadcasted_iota(jnp.int32, (places, patches), 0) == bucket_ref[...]
    out_ref[...] = jnp.dot(
        chosen.astype(BF16), merged, preferred_element_type=F32
    ).astype(BF16)


def merge(bucket, tag, attended, second, w_out, gain, places):
    return pl.pallas_call(
        merge_kernel,
        out_shape=jax.ShapeDtypeStruct((places, D + TAG), BF16),
        in_specs=whole(6),
        out_specs=pl.BlockSpec(memory_space=pltpu.VMEM),
        compiler_params=pltpu.CompilerParams(vmem_limit_bytes=VMEM_LIMIT),
    )(bucket, tag, attended, second, w_out, gain)


def place_kernel(got_ref, out_ref):
    rows = out_ref.shape[0]
    places = got_ref.shape[0]
    tag = got_ref[:, D:].astype(F32).T[0:1].astype(jnp.int32)
    target = 4 * tag + lax.broadcasted_iota(jnp.int32, (1, places), 1) % 4
    index = lax.broadcasted_iota(jnp.int32, (4 * rows, 1), 0)
    wanted = 4 * (index % rows + 1) + index // rows
    chosen = (wanted == target).astype(BF16)
    found = jnp.dot(chosen, got_ref[:, :D], preferred_element_type=F32).astype(BF16)
    for n in range(4):
        out_ref[:, n * D : (n + 1) * D] = found[n * rows : (n + 1) * rows]


def place(got, rows):
    return pl.pallas_call(
        place_kernel,
        out_shape=jax.ShapeDtypeStruct((rows, 4 * D), BF16),
        in_specs=whole(1),
        out_specs=pl.BlockSpec(memory_space=pltpu.VMEM),
        compiler_params=pltpu.CompilerParams(vmem_limit_bytes=VMEM_LIMIT),
    )(got)


def routes_kernel(slots_ref, bucket_ref, tag_ref):
    rows = slots_ref.shape[1]
    slots = jnp.broadcast_to(slots_ref[...], (8, rows))
    owner = slots // rows
    sender = owner.T[:, 0:1]
    earlier = lax.broadcasted_iota(jnp.int32, (rows, rows), 0) < lax.broadcasted_iota(
        jnp.int32, (rows, rows), 1
    )
    rank = jnp.sum(((sender == owner[0:1]) & earlier).astype(jnp.int32), axis=0, keepdims=True)
    bucket = jnp.broadcast_to(4 * (2 * owner[0:1] + rank), (8, rows)).T[:, 0:1]
    lane = lax.broadcasted_iota(jnp.int32, (rows, 4 * rows), 1)
    mine = lane // 4 == lax.broadcasted_iota(jnp.int32, (rows, 4 * rows), 0)
    bucket_ref[...] = jnp.sum(jnp.where(mine, bucket + lane % 4, 0), axis=0, keepdims=True)
    place = (slots - owner * rows + 1).T[:, 0:1].astype(F32)
    patch = lax.broadcasted_iota(jnp.int32, (4 * rows, rows), 0) // 4
    spread = (patch == lax.broadcasted_iota(jnp.int32, (4 * rows, rows), 1)).astype(BF16)
    tag_ref[...] = jnp.dot(
        spread,
        jnp.broadcast_to(place, (rows, TAG)).astype(BF16),
        preferred_element_type=F32,
    ).astype(BF16)


def routes(slots):
    rows = slots.shape[0]
    return pl.pallas_call(
        routes_kernel,
        out_shape=[
            jax.ShapeDtypeStruct((1, 4 * rows), jnp.int32),
            jax.ShapeDtypeStruct((4 * rows, TAG), BF16),
        ],
        in_specs=whole(1),
        out_specs=whole(2),
        compiler_params=pltpu.CompilerParams(vmem_limit_bytes=VMEM_LIMIT),
        cost_estimate=pl.CostEstimate(flops=10**6, bytes_accessed=10**6, transcendentals=0),
    )(slots.reshape(1, rows))


def on_device(
    patches, window_ids, counts, gain_one, w_qkv1, w_out1, gain_two, w_qkv2, w_out2, gain_out, slots
):
    shard = jnp.swapaxes(w_qkv2, 1, 2).reshape(3 * HEAD_DIM, D)
    near = near_shards(shard)

    second, hidden = layer_one(window_ids, patches, gain_one, gain_two, w_qkv1, w_out1)

    partner = lax.ppermute(hidden, BOTH, CORE_SWAP)
    far, last, partner = far_shards(near, partner)
    projected = project(NEAR_OFFSETS, hidden, partner, near + far, (1, 1, 1, 1, 2))
    projected = project(FAR_OFFSETS, hidden, partner, last, (1, 1, 2), into=projected)
    groups = [[2 * chip + core for chip in range(8)] for core in range(2)]
    received = lax.all_to_all(
        projected, "img", split_axis=0, concat_axis=0, tiled=True, axis_index_groups=groups
    )
    slots, projected = lax.optimization_barrier((slots, projected))
    bucket_rows, tag = routes(slots)
    attended = attend_full(counts, received)
    attended = lax.all_to_all(attended, "img", split_axis=0, concat_axis=0, tiled=True)
    places = 128 * 2 * 4
    send = merge(bucket_rows, tag, attended.reshape(D, -1), second, w_out2, gain_out, places)
    got = lax.all_to_all(
        send.reshape(128, 8, D + TAG), BOTH, split_axis=0, concat_axis=0, tiled=True
    )
    return place(got.reshape(places, D + TAG), slots.shape[0])


def solution(mesh):
    return jax.shard_map(
        on_device,
        mesh=mesh,
        in_specs=(
            P("ctx", "img", None),
            P("ctx", "img"),
            P("ctx"),
            P(),
            P(),
            P(),
            P(),
            P(None, None, "img"),
            P(),
            P(),
            P(("ctx", "img")),
        ),
        out_specs=P(("ctx", "img"), None),
        check_vma=False,
    )
```

```python
import functools
import math

import jax
import jax.numpy as jnp
from jax import lax
from jax.experimental import pallas as pl
from jax.experimental.pallas import tpu as pltpu
from jax.sharding import PartitionSpec as P

HEAD_DIM = 80
D = 1280
EPSILON = 1e-06
MASKED_SCORE = -1e30
F32 = jnp.float32
BF16 = jnp.bfloat16
Q_SCALE = HEAD_DIM ** (-0.5) * math.log2(math.e)
WINDOW = 64
QUERY_BLOCK = 384
TAG = 128
SAFE_BOUND = 64.0
SAFE_VALUE = 2.0**40
VMEM_LIMIT = 56 * 1024 * 1024
VMEM_ALL = 63 * 1024 * 1024
NT = (((1,), (1,)), ((), ()))
TN = (((0,), (0,)), ((), ()))


def normed(values, gain):
    values = values.astype(F32)
    return (
        values
        * lax.rsqrt(jnp.mean(values * values, axis=-1, keepdims=True) + EPSILON)
        * gain.astype(F32).reshape(1, -1)
    )


def whole(count):
    return [pl.BlockSpec(memory_space=pltpu.VMEM)] * count


def layer_one_kernel(
    ids_ref, x_ref, gain_one_ref, gain_two_ref, w_qkv_ref, w_out_hbm,
    second_ref, hidden_ref, h_ref, q_ref, k_ref, a_ref, w_out_ref, sem,
):
    step = pl.program_id(0)
    copy = pltpu.make_async_copy(w_out_hbm, w_out_ref, sem)

    @pl.when(step == 0)
    def _():
        h_ref[...] = normed(x_ref[0], gain_one_ref[...]).astype(BF16)

    def project_one(scale=None):
        product = jnp.dot(h_ref[...], w_qkv_ref[0], preferred_element_type=F32)
        return (product if scale is None else product * scale).astype(BF16)

    @pl.when(step == 0)
    def _():
        q_ref[...] = project_one(Q_SCALE)

    @pl.when(step == 1)
    def _():
        copy.start()
        k_ref[...] = project_one()

    @pl.when(step == 2)
    def _():
        values_all = project_one()
        rows = ids_ref.shape[1]
        ids = jnp.broadcast_to(ids_ref[...], (8, rows))
        ids_column = ids.T[:, 0:1]
        spans = []
        for start in range(0, rows, QUERY_BLOCK):
            begin = max(start - WINDOW, 0)
            end = min(start + QUERY_BLOCK + WINDOW, rows)
            allowed = ids_column[start : start + QUERY_BLOCK] == ids[0:1, begin:end]
            spans.append((start, begin, end, allowed))
        tiles = {}
        allowed = spans[0][3]

        def window(head):
            first, last = head * HEAD_DIM, (head + 1) * HEAD_DIM
            low, high = first // 128 * 128, (last + 127) // 128 * 128
            lane = low + lax.broadcasted_iota(jnp.int32, (1, high - low), 1)
            return low, high, last, (lane >= first) & (lane < last)

        def score(head):
            low, high, last, mine = window(head)
            keys = jnp.where(mine, k_ref[:, low:high], 0.0).astype(BF16)
            return lax.dot_general(q_ref[:, low:high], keys, NT, preferred_element_type=F32)

        heads = D // HEAD_DIM
        ahead = score(0)
        for head in range(heads):
            scores = jnp.where(allowed, ahead, MASKED_SCORE)
            if head + 1 < heads:
                ahead = score(head + 1)
            low, high, last, mine = window(head)
            most = jnp.max(scores, axis=1, keepdims=True)
            weights = jnp.exp2(scores - most)
            total = jnp.sum(weights, axis=1, keepdims=True)
            result = jnp.dot(
                weights.astype(BF16), values_all[:, low:high], preferred_element_type=F32
            ) * (1.0 / total)
            for tile in range(low, high, 128):
                piece = result[:, tile - low : tile - low + 128]
                if tile in tiles:
                    piece = jnp.where(mine[:, tile - low : tile - low + 128], piece, tiles[tile])
                tiles[tile] = piece
                if tile + 128 <= last:
                    a_ref[:, tile : tile + 128] = tiles.pop(tile).astype(BF16)
        copy.wait()
        second = x_ref[0].astype(F32) + jnp.dot(
            a_ref[...], w_out_ref[...], preferred_element_type=F32
        )
        second = second.astype(BF16)
        second_ref[...] = second
        hidden_ref[...] = normed(second, gain_two_ref[...]).astype(BF16)


def layer_one(ids, patches, gain_one, gain_two, w_qkv, w_out):
    rows = patches.shape[1]
    fixed = lambda *shape: pl.BlockSpec(shape, lambda i: (0,) * len(shape))
    return pl.pallas_call(
        layer_one_kernel,
        out_shape=[jax.ShapeDtypeStruct((rows, D), BF16)] * 2,
        grid=(3,),
        in_specs=[
            fixed(1, rows),
            fixed(1, rows, D),
            fixed(D),
            fixed(D),
            pl.BlockSpec((1, D, D), lambda i: (i, 0, 0)),
            pl.BlockSpec(memory_space=pl.ANY),
        ],
        out_specs=[fixed(rows, D)] * 2,
        scratch_shapes=[pltpu.VMEM((rows, D), BF16)] * 4
        + [pltpu.VMEM((D, D), BF16), pltpu.SemaphoreType.DMA],
        compiler_params=pltpu.CompilerParams(vmem_limit_bytes=VMEM_LIMIT),
        cost_estimate=pl.CostEstimate(
            flops=6 * 10**9, bytes_accessed=16 * 10**6, transcendentals=3 * 10**6
        ),
    )(
        ids, patches, gain_one, gain_two, w_qkv, w_out
    )


def device_perm(move):
    pairs = []
    for i in range(128):
        c, g = divmod(i, 16)
        x_lo, y = divmod(c, 4)
        x_hi, r = divmod(g, 8)
        z, core = divmod(r, 2)
        x2, y2, z2, core2 = move(x_hi * 2 + x_lo, y, z, core)
        x2, y2, z2 = x2 % 4, y2 % 4, z2 % 4
        pairs.append((i, ((x2 % 2) * 4 + y2) * 16 + ((x2 // 2) * 4 + z2) * 2 + core2))
    return pairs


OTHER_X = {0: 3, 3: 0, 1: 2, 2: 1}
Z_UP = device_perm(lambda x, y, z, core: (x, y, z + 1, core))
Z_DOWN = device_perm(lambda x, y, z, core: (x, y, z - 1, core))
X_OTHER = device_perm(lambda x, y, z, core: (OTHER_X[x], y, z, core))
CORE_SWAP = device_perm(lambda x, y, z, core: (x, y, z, 1 - core))
BOTH = ("ctx", "img")
NEAR_OFFSETS = ((0, 0), (0, -1), (0, 1), (1, 0), (0, 2))
FAR_OFFSETS = ((1, -1), (1, 1), (1, 2))


def near_shards(shard):
    below = lax.ppermute(shard, BOTH, Z_UP)
    above = lax.ppermute(shard, BOTH, Z_DOWN)
    other = lax.ppermute(shard, BOTH, X_OTHER)
    return [shard, below, above, other]


def far_shards(near):
    shard, below, above, other = near
    half = 144
    far_top = lax.ppermute(below[:half], BOTH, Z_UP)
    far_bottom = lax.ppermute(above[half:], BOTH, Z_DOWN)
    far_top, other_up = lax.optimization_barrier((far_top, other))
    far_bottom, other_down = lax.optimization_barrier((far_bottom, other))
    other_far_top = lax.ppermute(far_top, BOTH, X_OTHER)
    other_below = lax.ppermute(other_up, BOTH, Z_UP)
    other_far_bottom = lax.ppermute(far_bottom, BOTH, X_OTHER)
    other_above = lax.ppermute(other_down, BOTH, Z_DOWN)
    return [far_top, far_bottom], [other_below, other_above, other_far_top, other_far_bottom]


def project_kernel(h_own_ref, h_partner_ref, *refs, parts, offsets, aliased):
    count = sum(parts)
    me = lax.axis_index("img")
    my_x, my_z, core = me // 8, me // 2 % 4, me % 2
    weights_refs = refs[:count]
    out_hbm, w_ref, h_ref, done_ref, sem, in_sem = refs[count + aliased :]
    rows = h_own_ref.shape[0]
    wide = 3 * HEAD_DIM
    loads = []
    at = 0
    for n, weights_ref in enumerate(weights_refs):
        end = at + weights_ref.shape[0]
        load = pltpu.make_async_copy(weights_ref, w_ref.at[at:end], in_sem.at[n])
        load.start()
        loads.append(load)
        at = end
    for n, (side, ref) in enumerate(((core, h_own_ref), (1 - core, h_partner_ref))):
        load = pltpu.make_async_copy(
            ref, h_ref.at[pl.ds(pl.multiple_of(side * rows, 16), rows)], in_sem.at[count + n]
        )
        load.start()
        loads.append(load)
    part = lax.broadcasted_iota(jnp.int32, (len(parts) * wide, 1), 0) % wide
    scale = jnp.where(part < HEAD_DIM, Q_SCALE, 1.0).astype(F32)
    for load in loads:
        load.wait()
    product = lax.dot_general(w_ref[...], h_ref[...], NT, preferred_element_type=F32)
    product = (product * scale).astype(BF16)
    copies = []
    for n in range(len(parts)):
        done_ref[n] = product[n * wide : (n + 1) * wide]
        target = (my_x + offsets[n][0]) % 2 * 4 + (my_z + offsets[n][1] + 4) % 4
        copy = pltpu.make_async_copy(done_ref.at[n], out_hbm.at[target], sem.at[n])
        copy.start()
        copies.append(copy)
    for copy in copies:
        copy.wait()


def project(offsets, h_own, h_partner, shards, parts, into=None):
    rows = h_own.shape[0]
    wide = 3 * HEAD_DIM
    aliased = 0 if into is None else 1
    return pl.pallas_call(
        functools.partial(
            project_kernel, parts=parts, offsets=offsets, aliased=aliased
        ),
        out_shape=jax.ShapeDtypeStruct((8, wide, 2 * rows), BF16),
        in_specs=[pl.BlockSpec(memory_space=pl.ANY)] * (2 + len(shards) + aliased),
        out_specs=pl.BlockSpec(memory_space=pl.ANY),
        scratch_shapes=[
            pltpu.VMEM((len(parts) * wide, D), BF16),
            pltpu.VMEM((2 * rows, D), BF16),
            pltpu.VMEM((len(parts), wide, 2 * rows), BF16),
            pltpu.SemaphoreType.DMA((len(parts),)),
            pltpu.SemaphoreType.DMA((len(shards) + 2,)),
        ],
        input_output_aliases={2 + len(shards): 0} if aliased else {},
        compiler_params=pltpu.CompilerParams(vmem_limit_bytes=VMEM_ALL),
        cost_estimate=pl.CostEstimate(
            flops=2 * 10**9, bytes_accessed=6 * 10**6, transcendentals=0
        ),
    )(h_own, h_partner, *shards, *([into] if aliased else []))


def attention_kernel(
    count_ref, all_hbm, out_ref, all_ref, k_ref, v_ref, bound_ref, sem, *, block, taken
):
    chips, features, rows = all_ref.shape
    total = chips * rows
    depth = HEAD_DIM

    @pl.when(pl.program_id(0) == 0)
    def _():
        copies = [
            pltpu.make_async_copy(all_hbm.at[chip], all_ref.at[chip], sem.at[chip])
            for chip in range(chips)
        ]
        for copy in copies:
            copy.start()
        count = count_ref[0]
        copies[0].wait()
        key_zero = all_ref[0, depth : 2 * depth, 0:1].astype(F32)
        q_most = jnp.zeros((1, rows), F32)
        k_most = jnp.zeros((1, rows), F32)
        v_most = jnp.zeros((HEAD_DIM, rows), F32)
        for chip in range(chips):
            if chip:
                copies[chip].wait()
            position = chip * rows + lax.broadcasted_iota(jnp.int32, (1, rows), 1)
            valid = position < count
            keys = jnp.where(valid, all_ref[chip, depth : 2 * depth, :].astype(F32), key_zero)
            values = jnp.where(valid, all_ref[chip, 2 * depth :, :].astype(F32), 0.0)
            queries = all_ref[chip, 0:depth, :].astype(F32)
            q_most = jnp.maximum(q_most, jnp.sum(queries * queries, axis=0, keepdims=True))
            k_most = jnp.maximum(k_most, jnp.sum(keys * keys, axis=0, keepdims=True))
            v_most = jnp.maximum(v_most, jnp.abs(values))
            keys = jnp.concatenate([keys, jnp.zeros((128 - depth, rows), F32)], axis=0)
            k_ref[chip * rows : (chip + 1) * rows, :] = keys.astype(BF16).T
            v_ref[0:depth, chip * rows : (chip + 1) * rows] = values.astype(BF16)
            v_ref[depth:, chip * rows : (chip + 1) * rows] = jnp.where(
                (lax.broadcasted_iota(jnp.int32, (16, rows), 0) == 0) & valid, 1.0, 0.0
            ).astype(BF16)
        bound_ref[0] = jnp.max(q_most) * jnp.max(k_most)
        bound_ref[1] = jnp.max(v_most)

    first = taken * pl.program_id(0)
    queries = jnp.concatenate([all_ref[first + n, 0:depth, :] for n in range(taken)], axis=1)
    queries = jnp.concatenate([queries, jnp.zeros((128 - depth, taken * rows), BF16)], axis=0)
    small = (bound_ref[0] < SAFE_BOUND * SAFE_BOUND) & (bound_ref[1] < SAFE_VALUE)

    def store(acc):
        result = acc[0:depth] / acc[depth : depth + 1]
        half = rows // 2
        for n in range(2 * taken):
            out_ref[n] = result[:, n * half : (n + 1) * half].astype(BF16)

    @pl.when(small)
    def _():
        acc = None
        for start in range(0, total, block):
            scores = jnp.dot(k_ref[start : start + block, :], queries, preferred_element_type=F32)
            weights = jnp.exp2(scores).astype(BF16)
            part = jnp.dot(v_ref[:, start : start + block], weights, preferred_element_type=F32)
            acc = part if acc is None else acc + part
        store(acc)

    @pl.when(jnp.logical_not(small))
    def _():
        def step(index, carried):
            most, acc = carried
            start = pl.multiple_of(index * block, block)
            scores = jnp.dot(
                k_ref[pl.ds(start, block), :], queries, preferred_element_type=F32
            )
            new_most = jnp.maximum(most, jnp.max(scores, axis=0, keepdims=True))
            weights = jnp.exp2(scores - new_most).astype(BF16)
            part = jnp.dot(
                v_ref[:, pl.ds(start, block)], weights, preferred_element_type=F32
            )
            return new_most, acc * jnp.exp2(most - new_most) + part

        start_state = (
            jnp.full((1, taken * rows), MASKED_SCORE, F32),
            jnp.zeros((depth + 16, taken * rows), F32),
        )
        store(lax.fori_loop(0, total // block, step, start_state)[1])


def attend_full(count, received):
    chips, features, rows = received.shape
    total = chips * rows
    taken = 2
    return pl.pallas_call(
        functools.partial(attention_kernel, block=512, taken=taken),
        out_shape=jax.ShapeDtypeStruct((2 * chips, HEAD_DIM, rows // 2), BF16),
        grid=(chips // taken,),
        in_specs=[
            pl.BlockSpec(memory_space=pltpu.SMEM),
            pl.BlockSpec(memory_space=pl.ANY),
        ],
        out_specs=pl.BlockSpec((2 * taken, HEAD_DIM, rows // 2), lambda i: (i, 0, 0)),
        scratch_shapes=[
            pltpu.VMEM(received.shape, BF16),
            pltpu.VMEM((total, 128), BF16),
            pltpu.VMEM((HEAD_DIM + 16, total), BF16),
            pltpu.SMEM((2,), F32),
            pltpu.SemaphoreType.DMA((chips,)),
        ],
        compiler_params=pltpu.CompilerParams(vmem_limit_bytes=VMEM_ALL),
    )(count, received)


def merge_kernel(bucket_ref, tag_ref, a_ref, x_ref, w_ref, gain_ref, out_ref):
    attended = a_ref[...]
    third = x_ref[...].astype(F32) + lax.dot_general(
        attended, w_ref[...], TN, preferred_element_type=F32
    )
    merged = normed(third, gain_ref[...]).astype(BF16)
    merged = jnp.concatenate([merged, tag_ref[...]], axis=1)
    places, patches = out_ref.shape[0], merged.shape[0]
    chosen = lax.broadcasted_iota(jnp.int32, (places, patches), 0) == bucket_ref[...]
    out_ref[...] = jnp.dot(
        chosen.astype(BF16), merged, preferred_element_type=F32
    ).astype(BF16)


def merge(bucket, tag, attended, second, w_out, gain, places):
    return pl.pallas_call(
        merge_kernel,
        out_shape=jax.ShapeDtypeStruct((places, D + TAG), BF16),
        in_specs=whole(6),
        out_specs=pl.BlockSpec(memory_space=pltpu.VMEM),
        compiler_params=pltpu.CompilerParams(vmem_limit_bytes=VMEM_LIMIT),
    )(bucket, tag, attended, second, w_out, gain)


def place_kernel(got_ref, out_ref):
    rows = out_ref.shape[0]
    places = got_ref.shape[0]
    tag = got_ref[:, D:].astype(F32).T[0:1].astype(jnp.int32)
    target = 4 * tag + lax.broadcasted_iota(jnp.int32, (1, places), 1) % 4
    index = lax.broadcasted_iota(jnp.int32, (4 * rows, 1), 0)
    wanted = 4 * (index % rows + 1) + index // rows
    chosen = (wanted == target).astype(BF16)
    found = jnp.dot(chosen, got_ref[:, :D], preferred_element_type=F32).astype(BF16)
    for n in range(4):
        out_ref[:, n * D : (n + 1) * D] = found[n * rows : (n + 1) * rows]


def place(got, rows):
    return pl.pallas_call(
        place_kernel,
        out_shape=jax.ShapeDtypeStruct((rows, 4 * D), BF16),
        in_specs=whole(1),
        out_specs=pl.BlockSpec(memory_space=pltpu.VMEM),
        compiler_params=pltpu.CompilerParams(vmem_limit_bytes=VMEM_LIMIT),
    )(got)


def routes_kernel(slots_ref, bucket_ref, tag_ref):
    rows = slots_ref.shape[1]
    slots = jnp.broadcast_to(slots_ref[...], (8, rows))
    owner = slots // rows
    sender = owner.T[:, 0:1]
    earlier = lax.broadcasted_iota(jnp.int32, (rows, rows), 0) < lax.broadcasted_iota(
        jnp.int32, (rows, rows), 1
    )
    rank = jnp.sum(((sender == owner[0:1]) & earlier).astype(jnp.int32), axis=0, keepdims=True)
    bucket = jnp.broadcast_to(4 * (2 * owner[0:1] + rank), (8, rows)).T[:, 0:1]
    lane = lax.broadcasted_iota(jnp.int32, (rows, 4 * rows), 1)
    mine = lane // 4 == lax.broadcasted_iota(jnp.int32, (rows, 4 * rows), 0)
    bucket_ref[...] = jnp.sum(jnp.where(mine, bucket + lane % 4, 0), axis=0, keepdims=True)
    place = (slots - owner * rows + 1).T[:, 0:1].astype(F32)
    patch = lax.broadcasted_iota(jnp.int32, (4 * rows, rows), 0) // 4
    spread = (patch == lax.broadcasted_iota(jnp.int32, (4 * rows, rows), 1)).astype(BF16)
    tag_ref[...] = jnp.dot(
        spread,
        jnp.broadcast_to(place, (rows, TAG)).astype(BF16),
        preferred_element_type=F32,
    ).astype(BF16)


def routes(slots):
    rows = slots.shape[0]
    return pl.pallas_call(
        routes_kernel,
        out_shape=[
            jax.ShapeDtypeStruct((1, 4 * rows), jnp.int32),
            jax.ShapeDtypeStruct((4 * rows, TAG), BF16),
        ],
        in_specs=whole(1),
        out_specs=whole(2),
        compiler_params=pltpu.CompilerParams(vmem_limit_bytes=VMEM_LIMIT),
        cost_estimate=pl.CostEstimate(flops=10**6, bytes_accessed=10**6, transcendentals=0),
    )(slots.reshape(1, rows))


def on_device(
    patches, window_ids, counts, gain_one, w_qkv1, w_out1, gain_two, w_qkv2, w_out2, gain_out, slots
):
    shard = jnp.swapaxes(w_qkv2, 1, 2).reshape(3 * HEAD_DIM, D)
    near = near_shards(shard)
    far, last = far_shards(near)

    second, hidden = layer_one(window_ids, patches, gain_one, gain_two, w_qkv1, w_out1)

    partner = lax.ppermute(hidden, BOTH, CORE_SWAP)
    projected = project(NEAR_OFFSETS, hidden, partner, near + far, (1, 1, 1, 1, 2))
    projected = project(FAR_OFFSETS, hidden, partner, last, (1, 1, 2), into=projected)
    groups = [[2 * chip + core for chip in range(8)] for core in range(2)]
    received = lax.all_to_all(
        projected, "img", split_axis=0, concat_axis=0, tiled=True, axis_index_groups=groups
    )
    slots, projected = lax.optimization_barrier((slots, projected))
    bucket_rows, tag = routes(slots)
    attended = attend_full(counts, received)
    attended = lax.all_to_all(attended, "img", split_axis=0, concat_axis=0, tiled=True)
    places = 128 * 2 * 4
    send = merge(bucket_rows, tag, attended.reshape(D, -1), second, w_out2, gain_out, places)
    got = lax.all_to_all(
        send.reshape(128, 8, D + TAG), BOTH, split_axis=0, concat_axis=0, tiled=True
    )
    return place(got.reshape(places, D + TAG), slots.shape[0])


def solution(mesh):
    return jax.shard_map(
        on_device,
        mesh=mesh,
        in_specs=(
            P("ctx", "img", None),
            P("ctx", "img"),
            P("ctx"),
            P(),
            P(),
            P(),
            P(),
            P(None, None, "img"),
            P(),
            P(),
            P(("ctx", "img")),
        ),
        out_specs=P(("ctx", "img"), None),
        check_vma=False,
    )
```
